32 devices in a mesh: rep: 4 (over x, core), fsdp: 8 (over z, y).
Axes of the slice: x: 2, y: 2, z: 4, core: 2. Of those that a mesh axis runs over, the one named last changes fastest.
Arguments:
- image_tokens: bfloat16 [32, 256, 2048], P(('rep', 'fsdp')), may hold values from -6 to 6
- text_tokens: bfloat16 [32, 128, 2048], P(('rep', 'fsdp')), may hold values from -6 to 6
- text_lengths: int32 [32], P(('rep', 'fsdp')), may hold values from 1 to 128, as said below
- timesteps: int32 [32], P(('rep', 'fsdp')), may hold values from 0 to 999
- cotangent: bfloat16 [32, 256, 2048], P(('rep', 'fsdp')), may hold values from -6 to 6
- mod_weight: bfloat16 [2048, 12288], P('fsdp'), may hold values from -0.125 to 0.125
- qkv_weight: bfloat16 [2048, 6144], P('fsdp'), may hold values from -0.125 to 0.125
- out_weight: bfloat16 [2048, 2048], P('fsdp'), may hold values from -1 to 1
- query_weight: bfloat16 [2048, 2048], P('fsdp'), may hold values from -0.125 to 0.125
- keyval_weight: bfloat16 [2048, 4096], P('fsdp'), may hold values from -0.125 to 0.125
- merge_weight: bfloat16 [2048, 2048], P('fsdp'), may hold values from -0.75 to 0.75
- cross_gain: bfloat16 [2048], P('fsdp'), may hold values from 0.25 to 1.75
- up_weight: bfloat16 [2048, 8192], P('fsdp'), may hold values from -0.125 to 0.125
- down_weight: bfloat16 [8192, 2048], P('fsdp'), may hold values from -0.0625 to 0.0625
Outputs:
- block_out: bfloat16 [32, 256, 2048], P(('rep', 'fsdp'))
- image_grad: bfloat16 [32, 256, 2048], P(('rep', 'fsdp'))
- text_grad: bfloat16 [32, 128, 2048], P(('rep', 'fsdp'))
- mod_grad: float32 [2048, 12288], P('fsdp')
- qkv_grad: float32 [2048, 6144], P('fsdp')
- out_grad: float32 [2048, 2048], P('fsdp')
- query_grad: float32 [2048, 2048], P('fsdp')
- keyval_grad: float32 [2048, 4096], P('fsdp')
- merge_grad: float32 [2048, 2048], P('fsdp')
- gain_grad: float32 [2048], P('fsdp')
- up_grad: float32 [2048, 8192], P('fsdp')
- down_grad: float32 [8192, 2048], P('fsdp')
The draws below stay inside these ranges and needn't reach their ends.
Inputs may be any that keep to these rules, and one draw needn't show every extreme that they name: `text_lengths`: valid text tokens of each image; slots from it on are padding. Some image uses all 128 slots.
All inputs are finite; a program needn't handle non-finite values.
Results may differ from the reference program's by a relative error of at most 0.025.
Values may be sent and summed in bfloat16 or wider, within the bound.
No kernel may reach another device: no remote copies, remote signals or barrier semaphores. Data moves between devices by JAX's collectives and lax.ppermute only.
A program may use at most 512 MiB of HBM per device.

```python
import math
import jax
import jax.numpy as jnp
from jax import lax

D = 2048
HEADS = 16
HD = 128
FF = 8192
DT = 2048
S = 256
TEXT = 128
IMAGES = 32


def draw_text_lengths(key, part):
    key = jax.random.fold_in(key, 7)
    length_key, spot_key = jax.random.split(key)
    lengths = jax.random.randint(length_key, (IMAGES,), 1, TEXT + 1)
    chosen = jax.random.randint(spot_key, (), 0, IMAGES)
    return jnp.where(jnp.arange(IMAGES) == chosen, TEXT, lengths).astype(jnp.int32)


def set_ends(result, own_key, smallest, largest):
    index_at = [jax.random.randint(jax.random.fold_in(own_key, axis), (), 0, length) for axis, length in enumerate(result.shape)]
    main_axis = result.shape.index(max(result.shape))
    neighbour = index_at[:main_axis] + [(index_at[main_axis] + 1) % result.shape[main_axis]] + index_at[main_axis + 1:]
    return result.at[tuple(index_at)].set(smallest).at[tuple(neighbour)].set(largest)


def block_scale(key, extent, shards, smallest, largest):
    def one(dim, shards_of):
        heights = jax.random.uniform(jax.random.fold_in(jax.random.fold_in(key, 6), dim), (shards_of,), jnp.float32, smallest / len(shards), largest / len(shards))
        return jnp.repeat(jnp.exp(heights), extent[dim] // shards_of).reshape((-1,) + (1,) * (len(extent) - dim - 1))

    factor_of = one(*shards[0])
    for cut in shards[1:]:
        factor_of = factor_of * one(*cut)
    return factor_of


def noise(key, shape, spread, most, cuts=(), kind=jnp.bfloat16):
    values = jax.random.normal(key, shape, jnp.float32) * spread
    if len(cuts) > 0:
        values = block_scale(key, shape, cuts, -0.22, 0.18) * values
    return jnp.clip(values, min=-most, max=most).astype(kind)


def setup_inputs(seed: int = 0) -> dict:
    splits = jax.random.split(jax.random.key(seed), 15)
    image_tokens = noise(splits[0], (IMAGES, S, D), 1.0, 6.0, ((0, 32),))
    text_tokens = noise(splits[1], (IMAGES, TEXT, DT), 1.0, 6.0, ((0, 32),))
    text_lengths = draw_text_lengths(jax.random.fold_in(splits[14], 71), 0)
    timesteps = set_ends(jax.random.randint(splits[3], (IMAGES,), 0, 1000), jax.random.fold_in(splits[3], 1), 0, 999).astype(jnp.int32)
    cotangent = noise(splits[4], (IMAGES, S, D), 1.0, 6.0, ((0, 32),))
    mod_weight = noise(splits[5], (D, 6 * D), D ** -0.5, 0.125, ((0, 8),))
    qkv_weight = noise(splits[6], (D, 3 * D), D ** -0.5, 0.125, ((0, 8),))
    out_weight = noise(splits[7], (D, D), (D // 64) ** -0.5, 1.0, ((0, 8),))
    query_weight = noise(splits[8], (D, D), D ** -0.5, 0.125, ((0, 8),))
    keyval_weight = noise(splits[9], (DT, 2 * D), DT ** -0.5, 0.125, ((0, 8),))
    merge_weight = noise(splits[10], (D, D), (D // 32) ** -0.5, 0.75, ((0, 8),))
    cross_gain = jnp.clip(1.0 + 0.15 * jax.random.normal(splits[11], (D,), jnp.float32), 0.25, 1.75).astype(jnp.bfloat16)
    up_weight = noise(splits[12], (D, FF), D ** -0.5, 0.125, ((0, 8),))
    down_weight = noise(splits[13], (FF, D), FF ** -0.5, 0.0625, ((0, 8),))
    return {"image_tokens": image_tokens, "text_tokens": text_tokens, "text_lengths": text_lengths, "timesteps": timesteps, "cotangent": cotangent, "mod_weight": mod_weight, "qkv_weight": qkv_weight, "out_weight": out_weight, "query_weight": query_weight, "keyval_weight": keyval_weight, "merge_weight": merge_weight, "cross_gain": cross_gain, "up_weight": up_weight, "down_weight": down_weight}


@jax.custom_vjp
def low(v):
    return lax.optimization_barrier(v.astype(jnp.bfloat16)).astype(jnp.float32)

@jax.custom_vjp
def low_back(v):
    return v

def low_keep(v):
    return (low(v), None)

def low_pass(kept, grad):
    return (grad,)

def back_keep(v):
    return (v, None)

def back_low(kept, grad):
    return (low(grad),)
low.defvjp(low_keep, low_pass)
low_back.defvjp(back_keep, back_low)
EPSILON = 1e-06
HIGHEST = lax.Precision.HIGHEST

def both_ways(value):
    return low(low_back(value))

def normed(value):
    return value * lax.rsqrt(lax.optimization_barrier(jnp.mean(value * value, axis=-1, keepdims=True)) + EPSILON)

def smooth_gate(value):
    return jax.nn.gelu(value, approximate=True)

def project(value, weight):
    return jnp.einsum('nsd,de->nse', value, weight, precision=HIGHEST)

def attention(queries, keys, values, key_valid, score_scale):
    scores = low_back(jnp.einsum('nqhd,nkhd->nhqk', queries, keys, precision=HIGHEST)) * score_scale
    if key_valid is not None:
        scores = jnp.where(key_valid, scores, -jnp.inf)
    raised = jnp.exp(scores - lax.optimization_barrier(jnp.max(scores, axis=-1, keepdims=True)))
    weights = low(raised / lax.optimization_barrier(jnp.sum(raised, axis=-1, keepdims=True)))
    mixed_heads = jnp.einsum('nhqk,nkhd->nqhd', weights, values, precision=HIGHEST)
    return both_ways(mixed_heads.reshape(mixed_heads.shape[0], mixed_heads.shape[1], -1))

def block_forward(weights, image_block, text_block, condition, key_valid):
    mod_weight, qkv_weight, out_weight, query_weight, keyval_weight, merge_weight, cross_gain, up_weight, down_weight = weights
    image_count = image_block.shape[0]
    score_scale = HD ** (-0.5)
    pieces = low_back(jnp.dot(condition, mod_weight, precision=HIGHEST)).reshape(image_count, 6, 1, D)
    shift_self, scale_self, gate_self = (pieces[:, 0], pieces[:, 1], pieces[:, 2])
    shift_mlp, scale_mlp, gate_mlp = (pieces[:, 3], pieces[:, 4], pieces[:, 5])
    act_one = low(normed(image_block) * (1.0 + scale_self) + shift_self)
    qkv_act = both_ways(project(act_one, qkv_weight))
    queries = qkv_act[..., :D].reshape(image_count, S, HEADS, HD)
    keys_self = qkv_act[..., D:2 * D].reshape(image_count, S, HEADS, HD)
    values_self = qkv_act[..., 2 * D:].reshape(image_count, S, HEADS, HD)
    mixed_self = attention(queries, keys_self, values_self, None, score_scale)
    hidden_one = image_block + gate_self * low_back(project(mixed_self, out_weight))
    act_two = low(normed(hidden_one) * cross_gain)
    cross_queries = both_ways(project(act_two, query_weight)).reshape(image_count, S, HEADS, HD)
    keyval = both_ways(project(text_block, keyval_weight))
    cross_keys = keyval[..., :D].reshape(image_count, TEXT, HEADS, HD)
    cross_values = keyval[..., D:].reshape(image_count, TEXT, HEADS, HD)
    mixed_cross = attention(cross_queries, cross_keys, cross_values, key_valid, score_scale)
    hidden_two = hidden_one + low_back(project(mixed_cross, merge_weight))
    act_three = low(normed(hidden_two) * (1.0 + scale_mlp) + shift_mlp)
    activated = low(smooth_gate(low_back(project(act_three, up_weight))))
    return hidden_two + gate_mlp * low_back(project(activated, down_weight))

def reference(image_tokens, text_tokens, text_lengths, timesteps, cotangent, mod_weight, qkv_weight, out_weight, query_weight, keyval_weight, merge_weight, cross_gain, up_weight, down_weight):
    weights = tuple((weight.astype(jnp.float32) for weight in (mod_weight, qkv_weight, out_weight, query_weight, keyval_weight, merge_weight, cross_gain, up_weight, down_weight)))
    half_width = D // 2
    frequency = jnp.exp(-math.log(10000.0) * jnp.arange(half_width, dtype=jnp.float32) / half_width)
    angles = timesteps.astype(jnp.float32)[:, None] * frequency[None, :]
    condition = low(jnp.concatenate([jnp.sin(angles), jnp.cos(angles)], axis=1))
    block_size = math.gcd(IMAGES, max(1, 4096 // S))
    block_count = IMAGES // block_size

    def one_block(totals, pieces):
        image_block, text_block, cond_block, length_block, grad_block = pieces
        key_valid = (jnp.arange(TEXT, dtype=jnp.int32)[None, :] < length_block[:, None])[:, None, None, :]

        def forward(weight_set, image_part, text_part):
            return block_forward(weight_set, image_part, text_part, cond_block, key_valid)
        outputs, backward = jax.vjp(forward, weights, image_block.astype(jnp.float32), text_block.astype(jnp.float32))
        weight_grads, image_part_grad, text_part_grad = backward(grad_block.astype(jnp.float32))
        totals = jax.tree.map(lambda first_term, second_term: first_term + second_term, totals, weight_grads)
        return (totals, (outputs.astype(jnp.bfloat16), image_part_grad.astype(jnp.bfloat16), text_part_grad.astype(jnp.bfloat16)))
    zeros = tuple((jnp.zeros_like(weight) for weight in weights))
    inputs = (image_tokens.reshape(block_count, block_size, S, D), text_tokens.reshape(block_count, block_size, TEXT, DT), condition.reshape(block_count, block_size, D), text_lengths.reshape(block_count, block_size), cotangent.reshape(block_count, block_size, S, D))
    totals, stacked = lax.scan(one_block, zeros, inputs)
    block_out = stacked[0].reshape(IMAGES, S, D)
    image_grad = stacked[1].reshape(IMAGES, S, D)
    text_grad = stacked[2].reshape(IMAGES, TEXT, DT)
    return (block_out, image_grad, text_grad, totals[0], totals[1], totals[2], totals[3], totals[4], totals[5], totals[6], totals[7], totals[8])
```

```python
import math

import jax
import jax.numpy as jnp
from jax import lax
from jax.sharding import PartitionSpec as P

HEADS = 16


EPSILON = 1e-06


def matmul(left, right):
    return jnp.dot(left, right, preferred_element_type=jnp.float32)


def outer_sum(left, right):
    return lax.dot_general(
        left, right, (((0,), (0,)), ((), ())), preferred_element_type=jnp.float32
    )


def back_product(left, right):
    return lax.dot_general(
        left, right, (((1,), (1,)), ((), ())), preferred_element_type=jnp.float32
    )


def normed(value):
    return value * lax.rsqrt(jnp.mean(value * value, axis=-1, keepdims=True) + EPSILON)


def normed_back(value, grad):
    return jax.vjp(normed, value)[1](grad)[0]


def smooth_gate(value):
    return jax.nn.gelu(value, approximate=True)


def attend(queries, keys, values, key_valid, score_scale):
    scores = (
        jnp.einsum("nqhd,nkhd->nhqk", queries, keys, preferred_element_type=jnp.float32)
        * score_scale
    )
    if key_valid is not None:
        scores = jnp.where(key_valid, scores, -jnp.inf)
    row_top = jnp.max(scores, axis=-1, keepdims=True)
    raised = jnp.exp(scores - row_top)
    totals = jnp.sum(raised, axis=-1, keepdims=True)
    weights = (raised / totals).astype(jnp.bfloat16)
    mixed_heads = jnp.einsum("nhqk,nkhd->nqhd", weights, values, preferred_element_type=jnp.float32)
    return (mixed_heads.astype(jnp.bfloat16), row_top + jnp.log(totals))


def attend_back(queries, keys, values, logsum, grad_mixed, key_valid, score_scale):
    scores = (
        jnp.einsum("nqhd,nkhd->nhqk", queries, keys, preferred_element_type=jnp.float32)
        * score_scale
    )
    if key_valid is not None:
        scores = jnp.where(key_valid, scores, -jnp.inf)
    weights = jnp.exp(scores - logsum)
    grad_weights = jnp.einsum(
        "nqhd,nkhd->nhqk", grad_mixed, values, preferred_element_type=jnp.float32
    )
    grad_values = jnp.einsum(
        "nhqk,nqhd->nkhd",
        weights.astype(jnp.bfloat16),
        grad_mixed,
        preferred_element_type=jnp.float32,
    )
    inner_sum = jnp.sum(weights * grad_weights, axis=-1, keepdims=True)
    grad_scores = (score_scale * (weights * (grad_weights - inner_sum))).astype(jnp.bfloat16)
    grad_queries = jnp.einsum(
        "nhqk,nkhd->nqhd", grad_scores, keys, preferred_element_type=jnp.float32
    )
    grad_keys = jnp.einsum(
        "nhqk,nqhd->nkhd", grad_scores, queries, preferred_element_type=jnp.float32
    )
    return (grad_queries, grad_keys, grad_values)


PEERS = 4


def swap(value, mask):
    return lax.ppermute(value, "rep", [(peer, peer ^ mask) for peer in range(PEERS)])


def group_rows(value):
    far = swap(value, 2)
    near = swap(value, 1)
    return jnp.concatenate([value, near, swap(far, 1), far], axis=0)


def group_sum(left, right, product):
    rows = left.shape[0] // PEERS
    sent = product(left[rows : 3 * rows], right).astype(jnp.bfloat16)
    got = swap(sent, 1)
    across = product(left[3 * rows :], right) + got[rows:].astype(jnp.float32)
    crossed = swap(across.astype(jnp.bfloat16), 2)
    own = product(left[:rows], right) + got[:rows].astype(jnp.float32)
    return own + crossed.astype(jnp.float32)


def body(
    image_tokens,
    text_tokens,
    text_lengths,
    timesteps,
    cotangent,
    mod_weight,
    qkv_weight,
    out_weight,
    query_weight,
    keyval_weight,
    merge_weight,
    cross_gain,
    up_weight,
    down_weight,
):
    images, length, width = image_tokens.shape
    text_count, text_width = text_tokens.shape[1:]
    group = lax.axis_size("fsdp")
    rank = lax.axis_index("rep")
    member = lax.axis_index("fsdp")
    heads = HEADS // PEERS
    head_width = width // HEADS
    part = width // PEERS
    score_scale = head_width ** (-0.5)
    shard_rows = mod_weight.shape[0]
    hidden = up_weight.shape[1]
    rows = images * length
    all_images = PEERS * images

    def gather(value):
        return lax.all_gather(value, "fsdp", axis=0, tiled=True)

    def scatter(value):
        return lax.psum_scatter(
            value.astype(jnp.bfloat16), "fsdp", scatter_dimension=0, tiled=True
        )

    def own_part(value, blocks):
        count = value.shape[1] // (blocks * PEERS)
        return lax.dynamic_index_in_dim(
            value.reshape(value.shape[0], blocks, PEERS, count), rank, 2, keepdims=False
        ).reshape(value.shape[0], blocks * count)

    def all_parts(value, blocks):
        count = value.shape[1] // blocks
        found = lax.all_gather(value.reshape(value.shape[0], blocks, count), "rep", axis=2)
        return found.reshape(value.shape[0], -1).astype(jnp.float32)

    def ordered(found):
        stacked = jnp.stack(found)
        return [
            lax.dynamic_index_in_dim(stacked, rank ^ place, 0, keepdims=False)
            for place in range(PEERS)
        ]

    def columns_to_rows(value):
        blocks = value.reshape(PEERS, part, -1)
        found = [
            lax.dynamic_index_in_dim(blocks, rank ^ mask, 0, keepdims=False)
            for mask in range(PEERS)
        ]
        found = [found[0]] + [swap(found[mask], mask) for mask in range(1, PEERS)]
        return jnp.concatenate(ordered(found), axis=1)

    def rows_to_columns(value):
        count = value.shape[1] // PEERS
        found = [
            lax.dynamic_slice_in_dim(value, (rank ^ mask) * count, count, 1)
            for mask in range(PEERS)
        ]
        found = [found[0]] + [swap(found[mask], mask) for mask in range(1, PEERS)]
        return jnp.concatenate(ordered(found), axis=0)

    half_width = width // 2
    all_steps = lax.all_gather(timesteps, ("rep", "fsdp"), axis=0, tiled=True)
    column = member * shard_rows + jnp.arange(shard_rows, dtype=jnp.int32)
    place = jnp.where(column < half_width, column, column - half_width)
    frequency = jnp.exp(-math.log(10000.0) * place.astype(jnp.float32) / half_width)
    angles = all_steps.astype(jnp.float32)[:, None] * frequency[None, :]
    cond_slice = jnp.where(column < half_width, jnp.sin(angles), jnp.cos(angles)).astype(
        jnp.bfloat16
    )
    cond_group = lax.dynamic_slice_in_dim(cond_slice, rank * group * images, group * images, 0)
    terms = matmul(cond_group, mod_weight)
    found = lax.all_to_all(
        terms.reshape(group, images, -1), "fsdp", split_axis=0, concat_axis=0, tiled=True
    )
    modulation = jnp.sum(found, axis=0)
    pieces = modulation.reshape(images, 6, 1, width)
    shift_self, scale_self, gate_self = (pieces[:, 0], pieces[:, 1], pieces[:, 2])
    shift_mlp, scale_mlp, gate_mlp = (pieces[:, 3], pieces[:, 4], pieces[:, 5])

    def flatten(value):
        return value.reshape(-1, value.shape[-1])

    def own_rows(value):
        return value.reshape(images, length, width)

    def split_heads(value):
        return value.reshape(all_images, -1, heads, head_width)

    qkv_part = gather(own_part(qkv_weight, 3))
    keyval_part = gather(own_part(keyval_weight, 2))
    out_part = columns_to_rows(gather(own_part(out_weight, 1)))
    gain_full = gather(cross_gain)
    query_part = gather(own_part(query_weight, 1))
    merge_part = columns_to_rows(gather(own_part(merge_weight, 1)))
    up_part = gather(own_part(up_weight, group))
    down_part = gather(
        lax.dynamic_index_in_dim(
            down_weight.reshape(PEERS, -1, width), rank, 0, keepdims=False
        )
    )

    residual = image_tokens.astype(jnp.float32)
    norm_one = normed(residual)
    act_one = group_rows(flatten(norm_one * (1.0 + scale_self) + shift_self).astype(jnp.bfloat16))
    text_all = group_rows(flatten(text_tokens))
    length_all = group_rows(text_lengths)
    qkv_act = matmul(act_one, qkv_part).astype(jnp.bfloat16)
    queries = split_heads(qkv_act[:, :part])
    keys_self = split_heads(qkv_act[:, part : 2 * part])
    values_self = split_heads(qkv_act[:, 2 * part :])
    mixed_self, logsum_self = attend(queries, keys_self, values_self, None, score_scale)
    mixed_flat = mixed_self.reshape(-1, part)
    branch_one = own_rows(group_sum(mixed_flat, out_part, matmul))
    hidden_one = residual + gate_self * branch_one

    norm_two = normed(hidden_one)
    act_two = group_rows(flatten(norm_two * gain_full).astype(jnp.bfloat16))
    cross_queries = split_heads(matmul(act_two, query_part).astype(jnp.bfloat16))
    keyval = matmul(text_all, keyval_part).astype(jnp.bfloat16)
    cross_keys = split_heads(keyval[:, :part])
    cross_values = split_heads(keyval[:, part:])
    key_valid = (jnp.arange(text_count, dtype=jnp.int32)[None, :] < length_all[:, None])[
        :, None, None, :
    ]
    mixed_cross, logsum_cross = attend(
        cross_queries, cross_keys, cross_values, key_valid, score_scale
    )
    cross_flat = mixed_cross.reshape(-1, part)
    hidden_two = hidden_one + own_rows(group_sum(cross_flat, merge_part, matmul))

    norm_three = normed(hidden_two)
    act_three = group_rows(
        flatten(norm_three * (1.0 + scale_mlp) + shift_mlp).astype(jnp.bfloat16)
    )
    pre_act = matmul(act_three, up_part)
    activated = smooth_gate(pre_act).astype(jnp.bfloat16)
    branch_three = own_rows(group_sum(activated, down_part, matmul))
    block_out = (hidden_two + gate_mlp * branch_three).astype(jnp.bfloat16)

    grad_block = cotangent.astype(jnp.float32)
    grad_gate_mlp = jnp.sum(grad_block * branch_three, axis=1)
    grad_three = group_rows(flatten(gate_mlp * grad_block).astype(jnp.bfloat16))
    grad_activated = back_product(grad_three, down_part)
    down_grad = scatter(outer_sum(activated, grad_three))
    grad_pre = jax.vjp(smooth_gate, pre_act)[1](grad_activated)[0].astype(jnp.bfloat16)
    up_grad = scatter(outer_sum(act_three, grad_pre))
    grad_act_three = own_rows(group_sum(grad_pre, up_part, back_product))
    grad_shift_mlp = jnp.sum(grad_act_three, axis=1)
    grad_scale_mlp = jnp.sum(grad_act_three * norm_three, axis=1)
    grad_two = grad_block + normed_back(hidden_two, grad_act_three * (1.0 + scale_mlp))

    grad_merge = group_rows(flatten(grad_two).astype(jnp.bfloat16))
    merge_grad = scatter(
        rows_to_columns(outer_sum(cross_flat, grad_merge).astype(jnp.bfloat16))
    )
    grad_mixed_cross = back_product(grad_merge, merge_part).astype(jnp.bfloat16)
    grad_cross_queries, grad_cross_keys, grad_cross_values = attend_back(
        cross_queries,
        cross_keys,
        cross_values,
        logsum_cross,
        split_heads(grad_mixed_cross),
        key_valid,
        score_scale,
    )
    grad_query = grad_cross_queries.reshape(-1, part).astype(jnp.bfloat16)
    grad_keyval = jnp.concatenate(
        [grad_cross_keys.reshape(-1, part), grad_cross_values.reshape(-1, part)], axis=1
    ).astype(jnp.bfloat16)
    query_grad = scatter(outer_sum(act_two, grad_query))
    keyval_grad = scatter(outer_sum(text_all, grad_keyval))
    text_grad = (
        group_sum(grad_keyval, keyval_part, back_product)
        .astype(jnp.bfloat16)
        .reshape(text_tokens.shape)
    )
    grad_act_two = own_rows(group_sum(grad_query, query_part, back_product))
    gain_term = jnp.sum(grad_act_two * norm_two, axis=1)
    grad_one = grad_two + normed_back(hidden_one, grad_act_two * gain_full)

    grad_gate_self = jnp.sum(grad_one * branch_one, axis=1)
    grad_out = group_rows(flatten(gate_self * grad_one).astype(jnp.bfloat16))
    out_grad = scatter(rows_to_columns(outer_sum(mixed_flat, grad_out).astype(jnp.bfloat16)))
    grad_mixed_self = back_product(grad_out, out_part).astype(jnp.bfloat16)
    grad_queries, grad_keys, grad_values = attend_back(
        queries,
        keys_self,
        values_self,
        logsum_self,
        split_heads(grad_mixed_self),
        None,
        score_scale,
    )
    grad_qkv = jnp.concatenate(
        [
            grad_queries.reshape(-1, part),
            grad_keys.reshape(-1, part),
            grad_values.reshape(-1, part),
        ],
        axis=1,
    ).astype(jnp.bfloat16)
    qkv_grad = scatter(outer_sum(act_one, grad_qkv))
    grad_act_one = own_rows(group_sum(grad_qkv, qkv_part, back_product))
    grad_shift_self = jnp.sum(grad_act_one, axis=1)
    grad_scale_self = jnp.sum(grad_act_one * norm_one, axis=1)
    image_grad = (grad_one + normed_back(residual, grad_act_one * (1.0 + scale_self))).astype(
        jnp.bfloat16
    )

    vectors = jnp.concatenate(
        [
            grad_shift_self,
            grad_scale_self,
            grad_gate_self,
            grad_shift_mlp,
            grad_scale_mlp,
            grad_gate_mlp,
            gain_term,
        ],
        axis=1,
    ).astype(jnp.bfloat16)
    all_vectors = lax.all_gather(vectors, ("rep", "fsdp"), axis=0, tiled=True)
    mod_grad = outer_sum(cond_slice, all_vectors[:, : 6 * width])
    gain_grad = jnp.sum(
        lax.dynamic_slice_in_dim(
            all_vectors, 6 * width + member * shard_rows, shard_rows, 1
        ).astype(jnp.float32),
        axis=0,
    )
    return (
        block_out,
        image_grad,
        text_grad,
        mod_grad,
        all_parts(qkv_grad, 3),
        all_parts(out_grad, 1),
        all_parts(query_grad, 1),
        all_parts(keyval_grad, 2),
        all_parts(merge_grad, 1),
        gain_grad,
        all_parts(up_grad, group),
        lax.all_gather(down_grad, "rep", axis=0, tiled=True).astype(jnp.float32),
    )


def solution(mesh):
    placed = (
        P(("rep", "fsdp"), None, None),
        P(("rep", "fsdp"), None, None),
        P(("rep", "fsdp")),
        P(("rep", "fsdp")),
        P(("rep", "fsdp"), None, None),
        P("fsdp", None),
        P("fsdp", None),
        P("fsdp", None),
        P("fsdp", None),
        P("fsdp", None),
        P("fsdp", None),
        P("fsdp"),
        P("fsdp", None),
        P("fsdp", None),
    )
    return jax.shard_map(
        body,
        mesh=mesh,
        in_specs=placed,
        out_specs=(
            P(("rep", "fsdp"), None, None),
            P(("rep", "fsdp"), None, None),
            P(("rep", "fsdp"), None, None),
            P("fsdp", None),
            P("fsdp", None),
            P("fsdp", None),
            P("fsdp", None),
            P("fsdp", None),
            P("fsdp", None),
            P("fsdp"),
            P("fsdp", None),
            P("fsdp", None),
        ),
        check_vma=False,
    )
```

```python
import math

import jax
import jax.numpy as jnp
from jax import lax
from jax.experimental import pallas as pl
from jax.experimental.pallas import tpu as pltpu
from jax.sharding import PartitionSpec as P

HEADS = 16


EPSILON = 1e-06


def matmul(left, right):
    return jnp.dot(left, right, preferred_element_type=jnp.float32)


def outer_sum(left, right):
    return lax.dot_general(
        left, right, (((0,), (0,)), ((), ())), preferred_element_type=jnp.float32
    )


def back_product(left, right):
    return lax.dot_general(
        left, right, (((1,), (1,)), ((), ())), preferred_element_type=jnp.float32
    )


def normed(value):
    return value * lax.rsqrt(jnp.mean(value * value, axis=-1, keepdims=True) + EPSILON)


def normed_back(value, grad):
    return jax.vjp(normed, value)[1](grad)[0]


def smooth_gate(value):
    return jax.nn.gelu(value, approximate=True)


def row_block(rows, columns, column=0):
    return pl.BlockSpec((rows, columns), lambda image, *_: (image, column))


def parts_of(value, count):
    width = value.shape[1] // count
    return [value[:, i * width : (i + 1) * width] for i in range(count)]


def scores_of(queries, keys, limit, scale):
    scores = back_product(queries, keys) * scale
    if limit is not None:
        slot = lax.broadcasted_iota(jnp.int32, scores.shape, 1)
        scores = jnp.where(slot < limit, scores, -jnp.inf)
    return scores


def attend_heads(queries, keys, values, limit, scale, mixed_ref, logsum_ref):
    head_width = keys[0].shape[1]
    for head, (query, key, value) in enumerate(zip(queries, keys, values)):
        scores = scores_of(query, key, limit, scale)
        row_top = jnp.max(scores, axis=1, keepdims=True)
        raised = jnp.exp(scores - row_top)
        totals = jnp.sum(raised, axis=1, keepdims=True)
        weights = (raised / totals).astype(jnp.bfloat16)
        mixed_ref[:, head * head_width : (head + 1) * head_width] = matmul(weights, value).astype(
            jnp.bfloat16
        )
        logsum_ref[:, head : head + 1] = row_top + jnp.log(totals)


def attend_heads_back(queries, keys, values, limit, scale, logsum_ref, grads, outs):
    grad_query_ref, grad_key_ref, grad_value_ref = outs
    for head, (query, key, value, grad) in enumerate(zip(queries, keys, values, grads)):
        scores = scores_of(query, key, limit, scale)
        weights = jnp.exp(scores - logsum_ref[:, head : head + 1])
        grad_weights = back_product(grad, value)
        grad_value_ref(head, outer_sum(weights.astype(jnp.bfloat16), grad))
        inner_sum = jnp.sum(weights * grad_weights, axis=1, keepdims=True)
        grad_scores = (scale * (weights * (grad_weights - inner_sum))).astype(jnp.bfloat16)
        grad_query_ref(head, matmul(grad_scores, key))
        grad_key_ref(head, outer_sum(grad_scores, query))


def head_writer(ref, first, width):
    def write(head, value):
        start = first + head * width
        ref[:, start : start + width] = value.astype(jnp.bfloat16)

    return write


VMEM_LIMIT = 48 * 1024 * 1024


def attention_cost(images, length, slots, heads, width, products):
    pairs = images * heads * length * slots
    return pl.CostEstimate(
        flops=2 * products * pairs * width, bytes_accessed=8 * pairs, transcendentals=pairs
    )


def attend_self(qkv, images, heads, scale):
    rows, columns = qkv.shape
    length, part = rows // images, columns // 3

    def kernel(qkv_ref, mixed_ref, logsum_ref):
        blocks = parts_of(qkv_ref, 3 * heads)
        attend_heads(
            blocks[:heads],
            blocks[heads : 2 * heads],
            blocks[2 * heads :],
            None,
            scale,
            mixed_ref,
            logsum_ref,
        )

    return pl.pallas_call(
        kernel,
        grid=(images,),
        in_specs=[row_block(length, columns)],
        out_specs=[row_block(length, part), row_block(length, heads)],
        out_shape=[
            jax.ShapeDtypeStruct((rows, part), jnp.bfloat16),
            jax.ShapeDtypeStruct((rows, heads), jnp.float32),
        ],
        compiler_params=pltpu.CompilerParams(vmem_limit_bytes=VMEM_LIMIT),
        cost_estimate=attention_cost(images, length, length, heads, part // heads, 2),
        name="attend_self",
    )(qkv)


def attend_self_back(qkv, logsum, grad_mixed, images, heads, scale):
    rows, columns = qkv.shape
    length, part = rows // images, columns // 3

    def kernel(qkv_ref, logsum_ref, grad_ref, out_ref):
        blocks = parts_of(qkv_ref, 3 * heads)
        writers = [head_writer(out_ref, i * part, part // heads) for i in range(3)]
        attend_heads_back(
            blocks[:heads],
            blocks[heads : 2 * heads],
            blocks[2 * heads :],
            None,
            scale,
            logsum_ref,
            parts_of(grad_ref, heads),
            writers,
        )

    return pl.pallas_call(
        kernel,
        grid=(images,),
        in_specs=[row_block(length, columns), row_block(length, heads), row_block(length, part)],
        out_specs=row_block(length, columns),
        out_shape=jax.ShapeDtypeStruct((rows, columns), jnp.bfloat16),
        compiler_params=pltpu.CompilerParams(vmem_limit_bytes=VMEM_LIMIT),
        cost_estimate=attention_cost(images, length, length, heads, part // heads, 5),
        name="attend_self_back",
    )(qkv, logsum, grad_mixed)


def attend_cross(queries, keyval, limits, images, heads, scale):
    rows, part = queries.shape
    length, slots = rows // images, keyval.shape[0] // images

    def kernel(limits_ref, query_ref, keyval_ref, mixed_ref, logsum_ref):
        blocks = parts_of(keyval_ref, 2 * heads)
        attend_heads(
            parts_of(query_ref, heads),
            blocks[:heads],
            blocks[heads:],
            limits_ref[pl.program_id(0)],
            scale,
            mixed_ref,
            logsum_ref,
        )

    return pl.pallas_call(
        kernel,
        grid_spec=pltpu.PrefetchScalarGridSpec(
            num_scalar_prefetch=1,
            grid=(images,),
            in_specs=[row_block(length, part), row_block(slots, 2 * part)],
            out_specs=[row_block(length, part), row_block(length, heads)],
        ),
        out_shape=[
            jax.ShapeDtypeStruct((rows, part), jnp.bfloat16),
            jax.ShapeDtypeStruct((rows, heads), jnp.float32),
        ],
        compiler_params=pltpu.CompilerParams(vmem_limit_bytes=VMEM_LIMIT),
        cost_estimate=attention_cost(images, length, slots, heads, part // heads, 2),
        name="attend_cross",
    )(limits, queries, keyval)


def attend_cross_back(queries, keyval, limits, logsum, grad_mixed, images, heads, scale):
    rows, part = queries.shape
    length, slots = rows // images, keyval.shape[0] // images

    def kernel(limits_ref, query_ref, keyval_ref, logsum_ref, grad_ref, out_ref, text_ref):
        blocks = parts_of(keyval_ref, 2 * heads)
        width = part // heads
        attend_heads_back(
            parts_of(query_ref, heads),
            blocks[:heads],
            blocks[heads:],
            limits_ref[pl.program_id(0)],
            scale,
            logsum_ref,
            parts_of(grad_ref, heads),
            [
                head_writer(out_ref, 0, width),
                head_writer(text_ref, 0, width),
                head_writer(text_ref, part, width),
            ],
        )

    return pl.pallas_call(
        kernel,
        grid_spec=pltpu.PrefetchScalarGridSpec(
            num_scalar_prefetch=1,
            grid=(images,),
            in_specs=[
                row_block(length, part),
                row_block(slots, 2 * part),
                row_block(length, heads),
                row_block(length, part),
            ],
            out_specs=[row_block(length, part), row_block(slots, 2 * part)],
        ),
        out_shape=[
            jax.ShapeDtypeStruct((rows, part), jnp.bfloat16),
            jax.ShapeDtypeStruct((images * slots, 2 * part), jnp.bfloat16),
        ],
        compiler_params=pltpu.CompilerParams(vmem_limit_bytes=VMEM_LIMIT),
        cost_estimate=attention_cost(images, length, slots, heads, part // heads, 5),
        name="attend_cross_back",
    )(limits, queries, keyval, logsum, grad_mixed)


def pick_blocks(weights, counts, rank):
    rows = weights[0].shape[0]
    width = weights[0].shape[1] // (counts[0] * PEERS)
    firsts = [sum(counts[:i]) for i in range(len(counts))]

    def kernel(rank_ref, *refs):
        step = pl.program_id(0)
        out_ref = refs[-1]
        for ref, first, count in zip(refs, firsts, counts):

            @pl.when((step >= first) & (step < first + count))
            def _():
                out_ref[...] = ref[...]

    def spec(first, count):
        return pl.BlockSpec(
            (rows, width),
            lambda step, rank_ref: (
                0,
                jnp.clip(step - first, 0, count - 1) * PEERS + rank_ref[0],
            ),
        )

    return pl.pallas_call(
        kernel,
        grid_spec=pltpu.PrefetchScalarGridSpec(
            num_scalar_prefetch=1,
            grid=(sum(counts),),
            in_specs=[spec(first, count) for first, count in zip(firsts, counts)],
            out_specs=pl.BlockSpec((rows, width), lambda step, rank_ref: (0, step)),
        ),
        out_shape=jax.ShapeDtypeStruct((rows, width * sum(counts)), weights[0].dtype),
        name="pick_blocks",
    )(rank.reshape(1), *weights)


def spread_blocks(found, first, count, width):
    rows = found.shape[1]

    def kernel(found_ref, out_ref):
        out_ref[...] = found_ref[...].astype(jnp.float32)

    return pl.pallas_call(
        kernel,
        grid=(count, PEERS),
        in_specs=[
            pl.BlockSpec((None, rows, width), lambda block, peer: (peer, 0, first + block))
        ],
        out_specs=pl.BlockSpec((rows, width), lambda block, peer: (0, block * PEERS + peer)),
        out_shape=jax.ShapeDtypeStruct((rows, count * PEERS * width), jnp.float32),
        name="spread_blocks",
    )(found)


PEERS = 4


def swap(value, mask):
    return lax.ppermute(value, "rep", [(peer, peer ^ mask) for peer in range(PEERS)])


def group_rows(value):
    far = swap(value, 2)
    near = swap(value, 1)
    return jnp.concatenate([value, near, swap(far, 1), far], axis=0)


def group_sum(left, right, product):
    rows = left.shape[0] // PEERS
    sent = product(left[rows : 3 * rows], right).astype(jnp.bfloat16)
    got = swap(sent, 1)
    across = product(left[3 * rows :], right) + got[rows:].astype(jnp.float32)
    crossed = swap(across.astype(jnp.bfloat16), 2)
    own = product(left[:rows], right) + got[:rows].astype(jnp.float32)
    return own + crossed.astype(jnp.float32)


def ring_member(place, size):
    place = place % size
    return jnp.where(place < size // 2, 2 * place, 2 * (size - 1 - place) + 1)


def ring_pairs(size, step):
    order = [2 * i for i in range(size // 2)] + [2 * i + 1 for i in reversed(range(size // 2))]
    return [(order[i], order[(i + step) % size]) for i in range(size)]


def after(value, earlier):
    return lax.optimization_barrier((value, earlier))[0]


def ring_gather(value, size):
    rows = value.shape[0] // 2
    onward, back = [value[:rows]], [value[rows:]]
    for _ in range(size - 1):
        onward.append(lax.ppermute(onward[-1], "fsdp", ring_pairs(size, 1)))
        back.append(lax.ppermute(back[-1], "fsdp", ring_pairs(size, -1)))
    return onward, back


def lay_out(onward, back, starts, widths):
    size = len(onward)
    rows = onward[0].shape[0]
    total = 2 * size * rows
    count = len(widths)
    edges = [sum(widths[:i]) for i in range(count)]

    def kernel(*refs):
        starts_ref, halves, outs = refs[0], refs[1 : 1 + 2 * size], refs[1 + 2 * size : -1]
        done = refs[-1]
        copies = []
        for i, half in enumerate(halves):
            start = pl.multiple_of(starts_ref[i], rows)
            for j, out in enumerate(outs):
                copies.append(
                    pltpu.make_async_copy(
                        half.at[:, edges[j] : edges[j] + widths[j]],
                        out.at[pl.ds(start, rows), :],
                        done.at[i, j],
                    )
                )
        for copy in copies:
            copy.start()
        for copy in copies:
            copy.wait()

    return pl.pallas_call(
        kernel,
        out_shape=[jax.ShapeDtypeStruct((total, w), onward[0].dtype) for w in widths],
        in_specs=[pl.BlockSpec(memory_space=pltpu.SMEM)]
        + [pl.BlockSpec(memory_space=pltpu.VMEM)] * (2 * size),
        out_specs=[pl.BlockSpec(memory_space=pl.ANY)] * count,
        scratch_shapes=[pltpu.SemaphoreType.DMA((2 * size, count))],
        compiler_params=pltpu.CompilerParams(vmem_limit_bytes=VMEM_LIMIT),
        cost_estimate=pl.CostEstimate(
            flops=0, bytes_accessed=4 * total * sum(widths), transcendentals=0
        ),
        name="lay_out",
    )(starts, *onward, *back)


def ring_scatter(values, size, place, shard_rows):
    half = shard_rows // 2

    def piece(offset, lower):
        start = ring_member(place + offset, size) * shard_rows + (half if lower else 0)
        return jnp.concatenate(
            [lax.dynamic_slice_in_dim(v, start, half, 0) for v in values], axis=1
        )

    onward, back = piece(-1, False), piece(1, True)
    for step in range(1, size):
        onward = lax.ppermute(onward, "fsdp", ring_pairs(size, 1))
        back = lax.ppermute(back, "fsdp", ring_pairs(size, -1))
        mine_onward, mine_back = piece(-step - 1, False), piece(step + 1, True)
        onward = (onward.astype(jnp.float32) + mine_onward.astype(jnp.float32)).astype(jnp.bfloat16)
        back = (back.astype(jnp.float32) + mine_back.astype(jnp.float32)).astype(jnp.bfloat16)
    return jnp.concatenate([onward, back], axis=0)


def exchange(value, size):
    value = value[None]
    member = lax.axis_index("fsdp")
    mask = 1
    while mask < size:
        other = lax.ppermute(value, "fsdp", [(i, i ^ mask) for i in range(size)])
        low = (member & mask) == 0
        value = jnp.concatenate(
            [jnp.where(low, value, other), jnp.where(low, other, value)], axis=0
        )
        mask *= 2
    return value


def everyone(value, size):
    mask = size // 2
    while mask:
        pairs = [(i, i ^ mask) for i in range(size)]
        value = jnp.concatenate([value, lax.ppermute(value, "fsdp", pairs)], axis=0)
        mask //= 2
    value = jnp.concatenate([value, swap(value, 2)], axis=0)
    return jnp.concatenate([value, swap(value, 1)], axis=0)


def body(
    image_tokens,
    text_tokens,
    text_lengths,
    timesteps,
    cotangent,
    mod_weight,
    qkv_weight,
    out_weight,
    query_weight,
    keyval_weight,
    merge_weight,
    cross_gain,
    up_weight,
    down_weight,
):
    images, length, width = image_tokens.shape
    text_count, text_width = text_tokens.shape[1:]
    group = lax.axis_size("fsdp")
    rank = lax.axis_index("rep")
    member = lax.axis_index("fsdp")
    heads = HEADS // PEERS
    head_width = width // HEADS
    part = width // PEERS
    score_scale = head_width ** (-0.5)
    shard_rows = mod_weight.shape[0]
    hidden = up_weight.shape[1]
    rows = images * length
    all_images = PEERS * images

    def scatter(*values):
        return ring_scatter(
            [value.astype(jnp.bfloat16) for value in values],
            group,
            spot,
            values[0].shape[0] // group,
        )

    def own_part(value, blocks):
        count = value.shape[1] // (blocks * PEERS)
        return lax.dynamic_index_in_dim(
            value.reshape(value.shape[0], blocks, PEERS, count), rank, 2, keepdims=False
        ).reshape(value.shape[0], blocks * count)

    def ordered(found):
        stacked = jnp.stack(found)
        return [
            lax.dynamic_index_in_dim(stacked, rank ^ place, 0, keepdims=False)
            for place in range(PEERS)
        ]

    def columns_to_rows(value):
        blocks = value.reshape(PEERS, part, -1)
        found = [
            lax.dynamic_index_in_dim(blocks, rank ^ mask, 0, keepdims=False)
            for mask in range(PEERS)
        ]
        found = [found[0]] + [swap(found[mask], mask) for mask in range(1, PEERS)]
        return jnp.concatenate(ordered(found), axis=1)

    def rows_to_columns(value):
        count = value.shape[1] // PEERS
        found = [
            lax.dynamic_slice_in_dim(value, (rank ^ mask) * count, count, 1)
            for mask in range(PEERS)
        ]
        found = [found[0]] + [swap(found[mask], mask) for mask in range(1, PEERS)]
        return jnp.concatenate(ordered(found), axis=0)

    half_width = width // 2
    group_steps = exchange(timesteps, group).reshape(-1)
    all_steps = everyone(timesteps.reshape(images, 1), group).reshape(-1)
    gain_full = exchange(cross_gain.reshape(1, -1), group).reshape(-1)
    column = member * shard_rows + jnp.arange(shard_rows, dtype=jnp.int32)
    place = jnp.where(column < half_width, column, column - half_width)
    frequency = jnp.exp(-math.log(10000.0) * place.astype(jnp.float32) / half_width)

    def conditions(steps):
        angles = steps.astype(jnp.float32)[:, None] * frequency[None, :]
        return jnp.where(column < half_width, jnp.sin(angles), jnp.cos(angles)).astype(
            jnp.bfloat16
        )

    cond_group = conditions(group_steps)
    terms = matmul(cond_group, mod_weight)
    found = lax.all_to_all(
        terms.reshape(group, images, -1), "fsdp", split_axis=0, concat_axis=0, tiled=True
    )
    modulation = jnp.sum(found, axis=0)
    pieces = modulation.reshape(images, 6, 1, width)
    shift_self, scale_self, gate_self = (pieces[:, 0], pieces[:, 1], pieces[:, 2])
    shift_mlp, scale_mlp, gate_mlp = (pieces[:, 3], pieces[:, 4], pieces[:, 5])

    def flatten(value):
        return value.reshape(-1, value.shape[-1])

    def own_rows(value):
        return value.reshape(images, length, width)

    aligned = hidden // (group * PEERS) % 128 == 0
    spot = jnp.where(member % 2 == 0, member // 2, group - 1 - member // 2)
    starts = jnp.stack(
        [ring_member(spot - k, group) * shard_rows for k in range(group)]
        + [ring_member(spot + k, group) * shard_rows + shard_rows // 2 for k in range(group)]
    ).astype(jnp.int32)
    down_rows = down_weight.shape[0] // PEERS
    down_starts = starts // shard_rows * down_rows + starts % shard_rows // (shard_rows // 2) * (
        down_rows // 2
    )

    def gather(value, widths, begin, earlier):
        if earlier is not None:
            value = after(value, (earlier[0][-3], earlier[1][-3]))
        pieces_found = ring_gather(value, group)
        return lay_out(*pieces_found, begin, widths), pieces_found

    (qkv_part, out_part), ring = gather(
        pick_blocks([qkv_weight, out_weight], [3, 1], rank),
        [3 * part, part],
        starts,
        None,
    )
    (query_part, keyval_part, merge_part), ring = gather(
        pick_blocks([query_weight, keyval_weight, merge_weight], [1, 2, 1], rank),
        [part, 2 * part, part],
        starts,
        ring,
    )
    (up_part,), ring = gather(
        pick_blocks([up_weight], [group], rank) if aligned else own_part(up_weight, group),
        [hidden // PEERS],
        starts,
        ring,
    )
    (down_part,), ring = gather(
        lax.dynamic_index_in_dim(
            down_weight.reshape(PEERS, -1, width), rank, 0, keepdims=False
        ),
        [width],
        down_starts,
        ring,
    )
    out_part = columns_to_rows(out_part)
    merge_part = columns_to_rows(merge_part)

    residual = image_tokens.astype(jnp.float32)
    norm_one = normed(residual)
    act_one = group_rows(flatten(norm_one * (1.0 + scale_self) + shift_self).astype(jnp.bfloat16))
    text_all = group_rows(flatten(text_tokens))
    length_all = group_rows(text_lengths)
    qkv_act = matmul(act_one, qkv_part).astype(jnp.bfloat16)
    mixed_flat, logsum_self = attend_self(qkv_act, all_images, heads, score_scale)
    branch_one = own_rows(group_sum(mixed_flat, out_part, matmul))
    hidden_one = residual + gate_self * branch_one

    norm_two = normed(hidden_one)
    act_two = group_rows(flatten(norm_two * gain_full).astype(jnp.bfloat16))
    cross_queries = matmul(act_two, query_part).astype(jnp.bfloat16)
    keyval = matmul(text_all, keyval_part).astype(jnp.bfloat16)
    cross_flat, logsum_cross = attend_cross(
        cross_queries, keyval, length_all, all_images, heads, score_scale
    )
    hidden_two = hidden_one + own_rows(group_sum(cross_flat, merge_part, matmul))

    norm_three = normed(hidden_two)
    act_three = group_rows(
        flatten(norm_three * (1.0 + scale_mlp) + shift_mlp).astype(jnp.bfloat16)
    )
    pre_act = matmul(act_three, up_part)
    activated, slope_back = jax.vjp(smooth_gate, pre_act)
    activated, slope = lax.optimization_barrier(
        (
            activated.astype(jnp.bfloat16),
            slope_back(jnp.ones_like(pre_act))[0].astype(jnp.bfloat16),
        )
    )
    branch_three = own_rows(group_sum(activated, down_part, matmul))
    block_out = (hidden_two + gate_mlp * branch_three).astype(jnp.bfloat16)

    grad_block = cotangent.astype(jnp.float32)
    grad_gate_mlp = jnp.sum(grad_block * branch_three, axis=1)
    grad_three = group_rows(flatten(gate_mlp * grad_block).astype(jnp.bfloat16))
    grad_activated = back_product(grad_three, down_part)
    grad_pre = (grad_activated * slope.astype(jnp.float32)).astype(jnp.bfloat16)
    mlp_grads = scatter(outer_sum(activated, grad_three), outer_sum(act_three, grad_pre))
    grad_act_three = own_rows(group_sum(grad_pre, up_part, back_product))
    grad_shift_mlp = jnp.sum(grad_act_three, axis=1)
    grad_scale_mlp = jnp.sum(grad_act_three * norm_three, axis=1)
    grad_two = grad_block + normed_back(hidden_two, grad_act_three * (1.0 + scale_mlp))

    grad_merge = group_rows(flatten(grad_two).astype(jnp.bfloat16))
    merge_term = rows_to_columns(outer_sum(cross_flat, grad_merge).astype(jnp.bfloat16))
    grad_mixed_cross = back_product(grad_merge, merge_part).astype(jnp.bfloat16)
    grad_query, grad_keyval = attend_cross_back(
        cross_queries,
        keyval,
        length_all,
        logsum_cross,
        grad_mixed_cross,
        all_images,
        heads,
        score_scale,
    )
    cross_grads = scatter(
        outer_sum(act_two, grad_query), outer_sum(text_all, grad_keyval), merge_term
    )
    text_grad = (
        group_sum(grad_keyval, keyval_part, back_product)
        .astype(jnp.bfloat16)
        .reshape(text_tokens.shape)
    )
    grad_act_two = own_rows(group_sum(grad_query, query_part, back_product))
    gain_term = jnp.sum(grad_act_two * norm_two, axis=1)
    grad_one = grad_two + normed_back(hidden_one, grad_act_two * gain_full)

    grad_gate_self = jnp.sum(grad_one * branch_one, axis=1)
    grad_out = group_rows(flatten(gate_self * grad_one).astype(jnp.bfloat16))
    out_term = rows_to_columns(outer_sum(mixed_flat, grad_out).astype(jnp.bfloat16))
    grad_mixed_self = back_product(grad_out, out_part).astype(jnp.bfloat16)
    grad_qkv = attend_self_back(
        qkv_act, logsum_self, grad_mixed_self, all_images, heads, score_scale
    )
    self_grads = scatter(outer_sum(act_one, grad_qkv), out_term)
    grad_act_one = own_rows(group_sum(grad_qkv, qkv_part, back_product))
    grad_shift_self = jnp.sum(grad_act_one, axis=1)
    grad_scale_self = jnp.sum(grad_act_one * norm_one, axis=1)
    image_grad = (grad_one + normed_back(residual, grad_act_one * (1.0 + scale_self))).astype(
        jnp.bfloat16
    )

    early = everyone(
        jnp.concatenate(
            [grad_gate_self, grad_shift_mlp, grad_scale_mlp, grad_gate_mlp, gain_term], axis=1
        ).astype(jnp.bfloat16),
        group,
    )
    late = everyone(
        jnp.concatenate([grad_shift_self, grad_scale_self], axis=1).astype(jnp.bfloat16), group
    )
    all_vectors = jnp.concatenate([late, early[:, : 4 * width]], axis=1)
    mod_grad = outer_sum(conditions(all_steps), all_vectors)
    gain_grad = jnp.sum(
        lax.dynamic_slice_in_dim(
            early, 4 * width + member * shard_rows, shard_rows, 1
        ).astype(jnp.float32),
        axis=0,
    )
    self_all, cross_all, mlp_all = [
        lax.all_gather(found, "rep", axis=0) for found in (self_grads, cross_grads, mlp_grads)
    ]
    down_grad = mlp_all[:, :, :width].reshape(-1, width).astype(jnp.float32)
    if aligned:
        up_width = hidden // (group * PEERS)
        up_grad = spread_blocks(mlp_all, width // up_width, group, up_width)
    else:
        up_grad = (
            mlp_all[:, :, width:]
            .reshape(PEERS, shard_rows, group, -1)
            .transpose(1, 2, 0, 3)
            .reshape(shard_rows, hidden)
            .astype(jnp.float32)
        )
    return (
        block_out,
        image_grad,
        text_grad,
        mod_grad,
        spread_blocks(self_all, 0, 3, part),
        spread_blocks(self_all, 3, 1, part),
        spread_blocks(cross_all, 0, 1, part),
        spread_blocks(cross_all, 1, 2, part),
        spread_blocks(cross_all, 3, 1, part),
        gain_grad,
        up_grad,
        down_grad,
    )


def solution(mesh):
    placed = (
        P(("rep", "fsdp"), None, None),
        P(("rep", "fsdp"), None, None),
        P(("rep", "fsdp")),
        P(("rep", "fsdp")),
        P(("rep", "fsdp"), None, None),
        P("fsdp", None),
        P("fsdp", None),
        P("fsdp", None),
        P("fsdp", None),
        P("fsdp", None),
        P("fsdp", None),
        P("fsdp"),
        P("fsdp", None),
        P("fsdp", None),
    )
    return jax.shard_map(
        body,
        mesh=mesh,
        in_specs=placed,
        out_specs=(
            P(("rep", "fsdp"), None, None),
            P(("rep", "fsdp"), None, None),
            P(("rep", "fsdp"), None, None),
            P("fsdp", None),
            P("fsdp", None),
            P("fsdp", None),
            P("fsdp", None),
            P("fsdp", None),
            P("fsdp", None),
            P("fsdp"),
            P("fsdp", None),
            P("fsdp", None),
        ),
        check_vma=False,
    )
```

```python
import math

import jax
import jax.numpy as jnp
from jax import lax
from jax.experimental import pallas as pl
from jax.experimental.pallas import tpu as pltpu
from jax.sharding import PartitionSpec as P

HEADS = 16


EPSILON = 1e-06


def matmul(left, right):
    return jnp.dot(left, right, preferred_element_type=jnp.float32)


def outer_sum(left, right):
    return lax.dot_general(
        left, right, (((0,), (0,)), ((), ())), preferred_element_type=jnp.float32
    )


def back_product(left, right):
    return lax.dot_general(
        left, right, (((1,), (1,)), ((), ())), preferred_element_type=jnp.float32
    )


def normed(value):
    return value * lax.rsqrt(jnp.mean(value * value, axis=-1, keepdims=True) + EPSILON)


def normed_back(value, grad):
    return jax.vjp(normed, value)[1](grad)[0]


def smooth_gate(value):
    return jax.nn.gelu(value, approximate=True)


def row_block(rows, columns, column=0):
    return pl.BlockSpec((rows, columns), lambda image, *_: (image, column))


def parts_of(value, count):
    width = value.shape[1] // count
    return [value[:, i * width : (i + 1) * width] for i in range(count)]


def scores_of(queries, keys, limit, scale):
    scores = back_product(queries, keys) * scale
    if limit is not None:
        slot = lax.broadcasted_iota(jnp.int32, scores.shape, 1)
        scores = jnp.where(slot < limit, scores, -jnp.inf)
    return scores


def attend_heads(queries, keys, values, limit, scale, mixed_ref, logsum_ref):
    head_width = keys[0].shape[1]
    for head, (query, key, value) in enumerate(zip(queries, keys, values)):
        scores = scores_of(query, key, limit, scale)
        row_top = jnp.max(scores, axis=1, keepdims=True)
        raised = jnp.exp(scores - row_top)
        totals = jnp.sum(raised, axis=1, keepdims=True)
        weights = (raised / totals).astype(jnp.bfloat16)
        mixed_ref[:, head * head_width : (head + 1) * head_width] = matmul(weights, value).astype(
            jnp.bfloat16
        )
        logsum_ref[:, head : head + 1] = row_top + jnp.log(totals)


def attend_heads_back(queries, keys, values, limit, scale, logsum_ref, grads, outs):
    grad_query_ref, grad_key_ref, grad_value_ref = outs
    for head, (query, key, value, grad) in enumerate(zip(queries, keys, values, grads)):
        scores = scores_of(query, key, limit, scale)
        weights = jnp.exp(scores - logsum_ref[:, head : head + 1])
        grad_weights = back_product(grad, value)
        grad_value_ref(head, outer_sum(weights.astype(jnp.bfloat16), grad))
        inner_sum = jnp.sum(weights * grad_weights, axis=1, keepdims=True)
        grad_scores = (scale * (weights * (grad_weights - inner_sum))).astype(jnp.bfloat16)
        grad_query_ref(head, matmul(grad_scores, key))
        grad_key_ref(head, outer_sum(grad_scores, query))


def head_writer(ref, first, width):
    def write(head, value):
        start = first + head * width
        ref[:, start : start + width] = value.astype(jnp.bfloat16)

    return write


VMEM_LIMIT = 48 * 1024 * 1024


def cost(flops, moved, transcendentals=0):
    return pl.CostEstimate(
        flops=int(flops), bytes_accessed=int(moved), transcendentals=int(transcendentals)
    )


def attention_cost(images, length, slots, heads, width, products):
    pairs = images * heads * length * slots
    return cost(2 * products * pairs * width, 8 * pairs, pairs)


def attend_self(qkv, images, heads, scale):
    rows, columns = qkv.shape
    length, part = rows // images, columns // 3

    def kernel(qkv_ref, mixed_ref, logsum_ref):
        blocks = parts_of(qkv_ref, 3 * heads)
        attend_heads(
            blocks[:heads],
            blocks[heads : 2 * heads],
            blocks[2 * heads :],
            None,
            scale,
            mixed_ref,
            logsum_ref,
        )

    return pl.pallas_call(
        kernel,
        grid=(images,),
        in_specs=[row_block(length, columns)],
        out_specs=[row_block(length, part), row_block(length, heads)],
        out_shape=[
            jax.ShapeDtypeStruct((rows, part), jnp.bfloat16),
            jax.ShapeDtypeStruct((rows, heads), jnp.float32),
        ],
        compiler_params=pltpu.CompilerParams(vmem_limit_bytes=VMEM_LIMIT),
        cost_estimate=attention_cost(images, length, length, heads, part // heads, 2),
        name="attend_self",
    )(qkv)


def attend_self_back(qkv, logsum, grad_mixed, images, heads, scale):
    rows, columns = qkv.shape
    length, part = rows // images, columns // 3

    def kernel(qkv_ref, logsum_ref, grad_ref, out_ref):
        blocks = parts_of(qkv_ref, 3 * heads)
        writers = [head_writer(out_ref, i * part, part // heads) for i in range(3)]
        attend_heads_back(
            blocks[:heads],
            blocks[heads : 2 * heads],
            blocks[2 * heads :],
            None,
            scale,
            logsum_ref,
            parts_of(grad_ref, heads),
            writers,
        )

    return pl.pallas_call(
        kernel,
        grid=(images,),
        in_specs=[row_block(length, columns), row_block(length, heads), row_block(length, part)],
        out_specs=row_block(length, columns),
        out_shape=jax.ShapeDtypeStruct((rows, columns), jnp.bfloat16),
        compiler_params=pltpu.CompilerParams(vmem_limit_bytes=VMEM_LIMIT),
        cost_estimate=attention_cost(images, length, length, heads, part // heads, 5),
        name="attend_self_back",
    )(qkv, logsum, grad_mixed)


def attend_cross(queries, keyval, limits, images, heads, scale):
    rows, part = queries.shape
    length, slots = rows // images, keyval.shape[0] // images

    def kernel(limits_ref, query_ref, keyval_ref, mixed_ref, logsum_ref):
        blocks = parts_of(keyval_ref, 2 * heads)
        attend_heads(
            parts_of(query_ref, heads),
            blocks[:heads],
            blocks[heads:],
            limits_ref[pl.program_id(0)],
            scale,
            mixed_ref,
            logsum_ref,
        )

    return pl.pallas_call(
        kernel,
        grid_spec=pltpu.PrefetchScalarGridSpec(
            num_scalar_prefetch=1,
            grid=(images,),
            in_specs=[row_block(length, part), row_block(slots, 2 * part)],
            out_specs=[row_block(length, part), row_block(length, heads)],
        ),
        out_shape=[
            jax.ShapeDtypeStruct((rows, part), jnp.bfloat16),
            jax.ShapeDtypeStruct((rows, heads), jnp.float32),
        ],
        compiler_params=pltpu.CompilerParams(vmem_limit_bytes=VMEM_LIMIT),
        cost_estimate=attention_cost(images, length, slots, heads, part // heads, 2),
        name="attend_cross",
    )(limits, queries, keyval)


def attend_cross_back(queries, keyval, limits, logsum, grad_mixed, images, heads, scale):
    rows, part = queries.shape
    length, slots = rows // images, keyval.shape[0] // images

    def kernel(limits_ref, query_ref, keyval_ref, logsum_ref, grad_ref, out_ref, text_ref):
        blocks = parts_of(keyval_ref, 2 * heads)
        width = part // heads
        attend_heads_back(
            parts_of(query_ref, heads),
            blocks[:heads],
            blocks[heads:],
            limits_ref[pl.program_id(0)],
            scale,
            logsum_ref,
            parts_of(grad_ref, heads),
            [
                head_writer(out_ref, 0, width),
                head_writer(text_ref, 0, width),
                head_writer(text_ref, part, width),
            ],
        )

    return pl.pallas_call(
        kernel,
        grid_spec=pltpu.PrefetchScalarGridSpec(
            num_scalar_prefetch=1,
            grid=(images,),
            in_specs=[
                row_block(length, part),
                row_block(slots, 2 * part),
                row_block(length, heads),
                row_block(length, part),
            ],
            out_specs=[row_block(length, part), row_block(slots, 2 * part)],
        ),
        out_shape=[
            jax.ShapeDtypeStruct((rows, part), jnp.bfloat16),
            jax.ShapeDtypeStruct((images * slots, 2 * part), jnp.bfloat16),
        ],
        compiler_params=pltpu.CompilerParams(vmem_limit_bytes=VMEM_LIMIT),
        cost_estimate=attention_cost(images, length, slots, heads, part // heads, 5),
        name="attend_cross_back",
    )(limits, queries, keyval, logsum, grad_mixed)


def pick_blocks(weights, counts, rank):
    rows = weights[0].shape[0]
    width = weights[0].shape[1] // (counts[0] * PEERS)
    firsts = [sum(counts[:i]) for i in range(len(counts))]

    def kernel(rank_ref, *refs):
        step = pl.program_id(0)
        out_ref = refs[-1]
        for ref, first, count in zip(refs, firsts, counts):

            @pl.when((step >= first) & (step < first + count))
            def _():
                out_ref[...] = ref[...]

    def spec(first, count):
        return pl.BlockSpec(
            (rows, width),
            lambda step, rank_ref: (
                0,
                jnp.clip(step - first, 0, count - 1) * PEERS + rank_ref[0],
            ),
        )

    return pl.pallas_call(
        kernel,
        grid_spec=pltpu.PrefetchScalarGridSpec(
            num_scalar_prefetch=1,
            grid=(sum(counts),),
            in_specs=[spec(first, count) for first, count in zip(firsts, counts)],
            out_specs=pl.BlockSpec((rows, width), lambda step, rank_ref: (0, step)),
        ),
        out_shape=jax.ShapeDtypeStruct((rows, width * sum(counts)), weights[0].dtype),
        cost_estimate=cost(0, 4 * rows * width * sum(counts)),
        name="pick_blocks",
    )(rank.reshape(1), *weights)


def spread_blocks(found, first, count, width):
    rows = found.shape[0] // PEERS

    def kernel(found_ref, out_ref):
        for peer in range(PEERS):
            out_ref[:, peer * width : (peer + 1) * width] = found_ref[
                peer * rows : (peer + 1) * rows, :
            ].astype(jnp.float32)

    return pl.pallas_call(
        kernel,
        grid=(count,),
        in_specs=[pl.BlockSpec((PEERS * rows, width), lambda block: (0, first + block))],
        out_specs=pl.BlockSpec((rows, PEERS * width), lambda block: (0, block)),
        out_shape=jax.ShapeDtypeStruct((rows, count * PEERS * width), jnp.float32),
        cost_estimate=cost(0, 6 * rows * count * PEERS * width),
        compiler_params=pltpu.CompilerParams(vmem_limit_bytes=VMEM_LIMIT),
        name="spread_blocks",
    )(found)


def spread_rows(found, width):
    rows = found.shape[0] // PEERS

    def kernel(found_ref, out_ref):
        out_ref[...] = found_ref[...].astype(jnp.float32)

    return pl.pallas_call(
        kernel,
        grid=(PEERS,),
        in_specs=[pl.BlockSpec((rows, width), lambda peer: (peer, 0))],
        out_specs=pl.BlockSpec((rows, width), lambda peer: (peer, 0)),
        out_shape=jax.ShapeDtypeStruct((PEERS * rows, width), jnp.float32),
        cost_estimate=cost(0, 6 * PEERS * rows * width),
        compiler_params=pltpu.CompilerParams(vmem_limit_bytes=VMEM_LIMIT),
        name="spread_rows",
    )(found)


PEERS = 4


def swap(value, mask):
    return lax.ppermute(value, "rep", [(peer, peer ^ mask) for peer in range(PEERS)])


def stack_rows(parts):
    rows, columns = parts[0].shape
    count = len(parts)

    def kernel(*refs):
        for i in range(count):

            @pl.when(pl.program_id(0) == i)
            def _():
                refs[-1][...] = refs[i][...]

    return pl.pallas_call(
        kernel,
        grid=(count,),
        in_specs=[pl.BlockSpec((rows, columns), lambda step: (0, 0))] * count,
        out_specs=pl.BlockSpec((rows, columns), lambda step: (step, 0)),
        out_shape=jax.ShapeDtypeStruct((count * rows, columns), parts[0].dtype),
        cost_estimate=cost(0, 4 * count * rows * columns),
        compiler_params=pltpu.CompilerParams(vmem_limit_bytes=VMEM_LIMIT),
        name="stack_rows",
    )(*parts)


def stack_columns(parts):
    orders = ((0, 1, 2, 3), (2, 3, 0, 1), (1, 0, 3, 2), (3, 2, 1, 0))
    rows, columns = parts[0].shape
    block = rows // PEERS

    def kernel(*refs):
        for i, order in enumerate(orders):

            @pl.when(pl.program_id(0) == i)
            def _():
                for j, source in enumerate(order):
                    refs[-1][j * block : (j + 1) * block, :] = refs[i][
                        source * block : (source + 1) * block, :
                    ]

    return pl.pallas_call(
        kernel,
        grid=(PEERS,),
        in_specs=[pl.BlockSpec((rows, columns), lambda step: (0, 0))] * PEERS,
        out_specs=pl.BlockSpec((rows, columns), lambda step: (0, step)),
        out_shape=jax.ShapeDtypeStruct((rows, PEERS * columns), parts[0].dtype),
        cost_estimate=cost(0, 4 * PEERS * rows * columns),
        compiler_params=pltpu.CompilerParams(vmem_limit_bytes=VMEM_LIMIT),
        name="stack_columns",
    )(*parts)


def narrow(total):
    return (total.astype(jnp.bfloat16),)


def plus(total, extra):
    return (total + extra.astype(jnp.float32),)


def narrow_plus(total, extra):
    return ((total + extra.astype(jnp.float32)).astype(jnp.bfloat16),)


def halves(total):
    rows = total.shape[0] // 2
    return (total[:rows].astype(jnp.bfloat16), total[rows:].astype(jnp.bfloat16))


def scaled(total, factor):
    return ((total * factor.astype(jnp.float32)).astype(jnp.bfloat16),)


def gate_and_slope(total):
    value, back = jax.vjp(smooth_gate, total)
    return (value.astype(jnp.bfloat16), back(jnp.ones_like(total))[0].astype(jnp.bfloat16))


def multiply(
    left, right, turned, finish=narrow, types=(jnp.bfloat16,), first=0, rows=None, extra=None, half=None
):
    rows = left.shape[0] if rows is None else rows
    depth = left.shape[1]
    breadth = right.shape[1] // (1 if half is None else 2)
    columns = right.shape[0] if turned else breadth
    width = min(512, columns)
    skip = 0 if half is None else half * breadth // (depth if turned else width)
    product = back_product if turned else matmul
    tall = rows // 2 if finish is halves else rows

    def kernel(*refs):
        left_ref, right_ref = refs[:2]
        outs = refs[-len(types) :]
        blocks = [ref[...] for ref in refs[2 : -len(types)]]
        for out, value in zip(outs, finish(product(left_ref[...], right_ref[...]), *blocks)):
            out[...] = value

    specs = [
        pl.BlockSpec((rows, depth), lambda step: (first // rows, 0)),
        pl.BlockSpec((width, depth), lambda step: (step, skip))
        if turned
        else pl.BlockSpec((depth, width), lambda step: (0, skip + step)),
    ]
    values = [left, right]
    if extra is not None:
        extra, start = extra
        specs.append(pl.BlockSpec((rows, width), lambda step: (start // rows, step)))
        values.append(extra)
    found = pl.pallas_call(
        kernel,
        grid=(columns // width,),
        in_specs=specs,
        out_specs=[pl.BlockSpec((tall, width), lambda step: (0, step))] * len(types),
        out_shape=[jax.ShapeDtypeStruct((tall, columns), kind) for kind in types],
        cost_estimate=cost(2 * rows * depth * columns, 2 * (rows * depth + depth * columns + rows * columns)),
        compiler_params=pltpu.CompilerParams(vmem_limit_bytes=VMEM_LIMIT),
        name="multiply",
    )(*values)
    return found[0] if len(types) == 1 else found


def weight_term(left, right, column_block=None):
    depth, rows = left.shape
    columns = right.shape[1] if column_block is None else right.shape[1] // PEERS
    height, width = min(1024, rows), min(512, columns)
    shift = columns // width
    chosen = jnp.zeros((1,), jnp.int32) if column_block is None else column_block.reshape(1)

    def kernel(chosen_ref, left_ref, right_ref, out_ref):
        out_ref[...] = outer_sum(left_ref[...], right_ref[...]).astype(jnp.bfloat16)

    return pl.pallas_call(
        kernel,
        grid_spec=pltpu.PrefetchScalarGridSpec(
            num_scalar_prefetch=1,
            grid=(columns // width, rows // height),
            in_specs=[
                pl.BlockSpec((depth, height), lambda j, i, chosen_ref: (0, i)),
                pl.BlockSpec(
                    (depth, width), lambda j, i, chosen_ref: (0, chosen_ref[0] * shift + j)
                ),
            ],
            out_specs=pl.BlockSpec((height, width), lambda j, i, chosen_ref: (i, j)),
        ),
        out_shape=jax.ShapeDtypeStruct((rows, columns), jnp.bfloat16),
        cost_estimate=cost(2 * rows * depth * columns, 2 * (rows * depth + depth * columns + rows * columns)),
        compiler_params=pltpu.CompilerParams(vmem_limit_bytes=VMEM_LIMIT),
        name="weight_term",
    )(chosen, left, right)


def multiply_rest(left, right, turned, got):
    (rows, columns), depth = got[0].shape, left.shape[1]
    width = min(512, columns)
    product = back_product if turned else matmul

    def kernel(left_ref, right_ref, got_ref, got_far_ref, own_ref, far_ref):
        total = product(left_ref[...], right_ref[...])
        own_ref[...] = total[:rows] + got_ref[...].astype(jnp.float32)
        far_ref[...] = (total[rows:] + got_far_ref[...].astype(jnp.float32)).astype(jnp.bfloat16)

    return pl.pallas_call(
        kernel,
        grid=(columns // width,),
        in_specs=[
            pl.BlockSpec((2 * rows, depth), lambda step: (0, 0)),
            pl.BlockSpec((width, depth), lambda step: (step, 0))
            if turned
            else pl.BlockSpec((depth, width), lambda step: (0, step)),
        ]
        + [pl.BlockSpec((rows, width), lambda step: (0, step))] * 2,
        out_specs=[pl.BlockSpec((rows, width), lambda step: (0, step))] * 2,
        out_shape=[
            jax.ShapeDtypeStruct((rows, columns), jnp.float32),
            jax.ShapeDtypeStruct((rows, columns), jnp.bfloat16),
        ],
        cost_estimate=cost(
            4 * rows * depth * columns, 2 * (2 * rows * depth + depth * columns + 5 * rows * columns)
        ),
        compiler_params=pltpu.CompilerParams(vmem_limit_bytes=VMEM_LIMIT),
        name="multiply_rest",
    )(left, right, *got)


class Order:
    def __init__(self):
        self.token = ()

    def run(self, work, first, *others):
        if self.token:
            first, self.token = lax.optimization_barrier((first, self.token))
        found = work(first, *others)
        self.token = tuple(jax.tree.leaves(found))
        return found

    def hold(self, value):
        value, self.token = lax.optimization_barrier((value, self.token))
        return value

    def tick(self, *rings):
        heads = [ring.pieces[-1] for ring in rings]
        heads, self.token = lax.optimization_barrier((heads, self.token))
        for ring, head in zip(rings, heads):
            ring.pieces[-1] = head
            if ring.sevenths < 7:
                ring.send()

    def wait(self, *values):
        self.token = self.token + tuple(jax.tree.leaves(values))


class GroupSum:
    def __init__(self, order, left, right, turned, half=None):
        self.order, self.left, self.right, self.turned = order, left, right, turned
        self.half = half
        self.rows = left.shape[0] // PEERS

    def near(self):
        rows = self.rows
        sent = self.order.run(
            lambda left: multiply(
                left,
                self.right,
                self.turned,
                halves,
                (jnp.bfloat16, jnp.bfloat16),
                first=2 * rows,
                rows=2 * rows,
            ),
            self.left,
        )
        self.got = [swap(part, 1) for part in sent]

    def rest(self):
        self.mine, self.sent = self.order.run(
            lambda left: multiply_rest(left, self.right, self.turned, self.got), self.left
        )
        self.crossed = swap(self.sent, 2)

    def send(self):
        self.near()
        self.rest()
        return self

def ring_member(place, size):
    place = place % size
    return jnp.where(place < size // 2, 2 * place, 2 * (size - 1 - place) + 1)


def ring_pairs(size, step):
    order = [2 * i for i in range(size // 2)] + [2 * i + 1 for i in reversed(range(size // 2))]
    return [(order[i], order[(i + step) % size]) for i in range(size)]


def after(value, earlier):
    return lax.optimization_barrier((value, earlier))[0]


class Gather:
    def __init__(self, value, size, step):
        self.size, self.step, self.pieces = size, step, [value]
        self.sevenths = 0

    def send(self):
        self.sevenths += 1
        while len(self.pieces) - 1 < self.sevenths * (self.size - 1) // 7:
            self.pieces.append(
                lax.ppermute(self.pieces[-1], "fsdp", ring_pairs(self.size, self.step))
            )

    def starts(self, place, rows):
        return jnp.stack(
            [ring_member(place - self.step * k, self.size) * rows for k in range(self.size)]
        ).astype(jnp.int32)


def lay_out(pieces, starts, widths):
    size = len(pieces)
    rows = pieces[0].shape[0]
    count = len(widths)
    edges = [sum(widths[:i]) for i in range(count)]

    def kernel(starts_ref, *refs):
        shards, outs, done = refs[:size], refs[size:-1], refs[-1]
        copies = []
        for i, shard in enumerate(shards):
            start = pl.multiple_of(starts_ref[i], rows)
            for j, out in enumerate(outs):
                copies.append(
                    pltpu.make_async_copy(
                        shard.at[:, edges[j] : edges[j] + widths[j]],
                        out.at[pl.ds(start, rows), :],
                        done.at[i, j],
                    )
                )
        for copy in copies:
            copy.start()
        for copy in copies:
            copy.wait()

    return pl.pallas_call(
        kernel,
        out_shape=[jax.ShapeDtypeStruct((size * rows, w), pieces[0].dtype) for w in widths],
        in_specs=[pl.BlockSpec(memory_space=pltpu.SMEM)]
        + [pl.BlockSpec(memory_space=pltpu.VMEM)] * size,
        out_specs=[pl.BlockSpec(memory_space=pl.ANY)] * count,
        scratch_shapes=[pltpu.SemaphoreType.DMA((size, count))],
        compiler_params=pltpu.CompilerParams(vmem_limit_bytes=VMEM_LIMIT),
        cost_estimate=cost(0, 4 * size * rows * sum(widths)),
        name="lay_out",
    )(starts, *pieces)


def ring_add(entries, spots, rows, got):
    flat = [value for values in entries for value in values]
    lengths = [sum(value.shape[1] for value in values) for values in entries]
    count = len(flat)

    def kernel(spots_ref, *refs):
        outs = refs[-len(entries) :]
        i = 0
        for entry, values in enumerate(entries):
            first = 0
            for value in values:
                place = slice(first, first + value.shape[1])
                block = refs[i][...]
                if got is not None:
                    here = refs[count + entry][:, place].astype(jnp.float32)
                    block = (here + block.astype(jnp.float32)).astype(jnp.bfloat16)
                outs[entry][:, place] = block
                first += value.shape[1]
                i += 1

    def spec(i):
        return pl.BlockSpec(
            (rows, flat[i].shape[1]), lambda step, spots_ref: (spots_ref[i], 0)
        )

    plain = [pl.BlockSpec((rows, length), lambda step, spots_ref: (0, 0)) for length in lengths]
    arrived = [] if got is None else list(got)
    return pl.pallas_call(
        kernel,
        grid_spec=pltpu.PrefetchScalarGridSpec(
            num_scalar_prefetch=1,
            grid=(1,),
            in_specs=[spec(i) for i in range(count)] + plain[: len(arrived)],
            out_specs=plain,
        ),
        out_shape=[jax.ShapeDtypeStruct((rows, length), jnp.bfloat16) for length in lengths],
        cost_estimate=cost(rows * sum(lengths), 6 * rows * sum(lengths)),
        compiler_params=pltpu.CompilerParams(vmem_limit_bytes=VMEM_LIMIT),
        name="ring_add",
    )(spots, *flat, *arrived)


class Scatter:
    def __init__(self, order, entries, size, place, rows):
        self.order, self.entries = order, entries
        self.size, self.place, self.rows, self.step = size, place, rows, 0
        self.values = [[value for value, _ in values] for values, _, _ in entries]
        self.sums = order.run(
            lambda first: ring_add(
                [[first] + self.values[0][1:]] + self.values[1:], self.spots(), self.rows, None
            ),
            self.values[0][0],
        )

    def spots(self):
        found = []
        for values, direction, block in self.entries:
            shard = ring_member(self.place - direction * (self.step + 1), self.size)
            found += [rows_of(shard) // self.rows + block for _, rows_of in values]
        return jnp.stack(found).astype(jnp.int32)

    def reach(self, seventh):
        while self.step < seventh * (self.size - 1) // 7:
            self.step += 1
            arrived = [
                lax.ppermute(value, "fsdp", ring_pairs(self.size, direction))
                for value, (_, direction, _) in zip(self.sums, self.entries)
            ]
            spots = self.spots()
            self.sums = self.order.run(
                lambda got: ring_add(self.values, spots, self.rows, got), arrived
            )


def exchange(value, size, between):
    value = value[None]
    member = lax.axis_index("fsdp")
    mask = 1
    while mask < size:
        other = between(lax.ppermute(value, "fsdp", [(i, i ^ mask) for i in range(size)]))
        low = (member & mask) == 0
        value = jnp.concatenate(
            [jnp.where(low, value, other), jnp.where(low, other, value)], axis=0
        )
        mask *= 2
    return value


class Everyone:
    def __init__(self, order, value, size):
        self.order, self.value = order, value
        self.hops = [("fsdp", size // 2 >> i, size) for i in range(size.bit_length() - 1)]
        self.hops += [("rep", 2, PEERS), ("rep", 1, PEERS)]
        self.send()

    def send(self):
        axis, mask, size = self.hops.pop(0)
        self.got = lax.ppermute(self.value, axis, [(i, i ^ mask) for i in range(size)])

    def hop(self, count=1):
        for _ in range(count):
            self.value = self.order.run(
                lambda got: jnp.concatenate([self.value, got], axis=0), self.got
            )
            if self.hops:
                self.send()


def body(
    image_tokens,
    text_tokens,
    text_lengths,
    timesteps,
    cotangent,
    mod_weight,
    qkv_weight,
    out_weight,
    query_weight,
    keyval_weight,
    merge_weight,
    cross_gain,
    up_weight,
    down_weight,
):
    images, length, width = image_tokens.shape
    text_count, text_width = text_tokens.shape[1:]
    group = lax.axis_size("fsdp")
    rank = lax.axis_index("rep")
    member = lax.axis_index("fsdp")
    heads = HEADS // PEERS
    head_width = width // HEADS
    part = width // PEERS
    score_scale = head_width ** (-0.5)
    shard_rows = mod_weight.shape[0]
    hidden = up_weight.shape[1]
    rows = images * length
    all_images = PEERS * images

    def own_part(value, blocks):
        count = value.shape[1] // (blocks * PEERS)
        return lax.dynamic_index_in_dim(
            value.reshape(value.shape[0], blocks, PEERS, count), rank, 2, keepdims=False
        ).reshape(value.shape[0], blocks * count)

    def ordered(found):
        stacked = jnp.stack(found)
        return [
            lax.dynamic_index_in_dim(stacked, rank ^ place, 0, keepdims=False)
            for place in range(PEERS)
        ]

    def columns_to_rows(value):
        blocks = value.reshape(PEERS, part, -1)
        found = [
            lax.dynamic_index_in_dim(blocks, rank ^ mask, 0, keepdims=False)
            for mask in range(PEERS)
        ]
        found = [found[0]] + [swap(found[mask], mask) for mask in range(1, PEERS)]
        return jnp.concatenate(ordered(found), axis=1)

    order = Order()
    aligned = hidden // (group * PEERS) % 128 == 0
    spot = jnp.where(member % 2 == 0, member // 2, group - 1 - member // 2)
    def flatten(value):
        return value.reshape(-1, value.shape[-1])

    def own_rows(value):
        return value.reshape(images, length, width)

    first_pick = order.run(lambda w: pick_blocks([w, out_weight], [3, 1], rank), qkv_weight)
    second_pick = order.run(
        lambda w: pick_blocks([w, keyval_weight, merge_weight], [1, 2, 1], rank), query_weight
    )
    first, second = Gather(first_pick, group, 1), Gather(second_pick, group, -1)
    order.tick(first, second)
    picks = [
        lambda w: pick_blocks([w], [group], rank) if aligned else own_part(w, group),
        lambda w: lax.dynamic_index_in_dim(
            w.reshape(PEERS, -1, width), rank, 0, keepdims=False
        ),
    ]
    sources = [up_weight, down_weight]
    picked = []

    def pick_between(value):
        if len(picked) < len(picks):
            i = len(picked)
            picked.append(order.run(picks[i], sources[i]))
        return after(value, order.token)

    small = exchange(
        jnp.concatenate([timesteps.astype(jnp.float32), cross_gain.astype(jnp.float32)]),
        group,
        pick_between,
    )
    while len(picked) < len(picks):
        pick_between(small)
    third_pick, fourth_pick = picked
    small = order.hold(small)
    order.tick(first, second)
    group_steps = small[:, :images].reshape(-1)
    gain_full = small[:, images:].reshape(-1)
    sequence = [0]
    while len(sequence) < group:
        sequence += [index + group // (2 * len(sequence)) for index in sequence]
    all_steps = small[:, :images][member ^ jnp.array(sequence, dtype=jnp.int32)].reshape(-1)
    all_steps = jnp.concatenate([all_steps, swap(all_steps, 2)])
    all_steps = jnp.concatenate([all_steps, swap(all_steps, 1)])
    length_far = swap(text_lengths, 2)
    length_all = jnp.concatenate(
        [text_lengths, length_far, swap(text_lengths, 1), swap(length_far, 1)]
    )

    half_width = width // 2
    column = member * shard_rows + jnp.arange(shard_rows, dtype=jnp.int32)
    place = jnp.where(column < half_width, column, column - half_width)
    frequency = jnp.exp(-math.log(10000.0) * place.astype(jnp.float32) / half_width)

    def conditions(steps):
        angles = steps.astype(jnp.float32)[:, None] * frequency[None, :]
        return jnp.where(column < half_width, jnp.sin(angles), jnp.cos(angles)).astype(
            jnp.bfloat16
        )

    terms = order.run(lambda steps: matmul(conditions(steps), mod_weight), group_steps)
    found = lax.all_to_all(
        terms.reshape(group, images, -1), "fsdp", split_axis=0, concat_axis=0, tiled=True
    )
    order.wait(all_steps, length_all)
    residual = image_tokens.astype(jnp.float32)
    grad_block = cotangent.astype(jnp.float32)

    def start(found):
        pieces = jnp.sum(found, axis=0).reshape(images, 6, 1, width)
        act = flatten(normed(residual) * (1.0 + pieces[:, 1]) + pieces[:, 0])
        return pieces, act.astype(jnp.bfloat16)

    pieces, act_one = order.run(start, found)
    shift_self, scale_self, gate_self = (pieces[:, 0], pieces[:, 1], pieces[:, 2])
    shift_mlp, scale_mlp, gate_mlp = (pieces[:, 3], pieces[:, 4], pieces[:, 5])
    norm_one = normed(residual)

    def send_rows(value):
        return [value, swap(value, 2), swap(value, 1)]

    def join_rows(parts):
        far = order.hold(parts[1])
        return order.run(
            lambda last: stack_rows([parts[0], far, parts[2], last]), swap(far, 1)
        )

    def send_columns(value):
        return [value, swap(value, 1), swap(value, 2)]

    def join_columns(parts):
        far = order.hold(parts[2])
        return order.run(
            lambda last: stack_columns([parts[0], parts[1], far, last]), swap(far, 1)
        )

    act_one = send_rows(act_one)
    text_all = send_rows(after(flatten(text_tokens), act_one[1]))
    order.tick(first, second)
    grad_three = order.run(lambda gate: flatten(gate * grad_block).astype(jnp.bfloat16), gate_mlp)
    order.tick(first, second)
    act_one = join_rows(act_one)
    order.tick(first, second)
    text_all = join_rows(text_all)
    order.tick(first, second)
    order.tick(first, second)
    third, fourth = Gather(third_pick, group, 1), Gather(fourth_pick, group, -1)
    order.tick(first, second, third, fourth)

    qkv_part, out_part = order.run(
        lambda last: lay_out(
            first.pieces[:-1] + [last], first.starts(spot, shard_rows), [3 * part, part]
        ),
        first.pieces[-1],
    )
    out_part = columns_to_rows(out_part)
    query_part, keyval_part, merge_part = order.run(
        lambda last: lay_out(
            second.pieces[:-1] + [last], second.starts(spot, shard_rows), [part, 2 * part, part]
        ),
        second.pieces[-1],
    )
    merge_part = columns_to_rows(merge_part)
    qkv_act = order.run(lambda a: multiply(a, qkv_part, False), act_one)
    order.tick(third, fourth)
    keyval = order.run(lambda a: multiply(a, keyval_part, False), text_all)
    mixed_flat, logsum_self = order.run(
        lambda a: attend_self(a, all_images, heads, score_scale), qkv_act
    )
    order.wait(out_part)
    branch_sum = GroupSum(order, mixed_flat, out_part, False)
    branch_sum.near()
    order.tick(third, fourth)
    branch_sum.rest()
    order.wait(merge_part)
    order.tick(third, fourth)

    def finish_self(crossed):
        branch_one = own_rows(branch_sum.mine + crossed.astype(jnp.float32))
        hidden_one = residual + gate_self * branch_one
        return (
            branch_one,
            hidden_one,
            flatten(normed(hidden_one) * gain_full).astype(jnp.bfloat16),
        )

    branch_one, hidden_one, act_two = order.run(finish_self, branch_sum.crossed)
    norm_two = normed(hidden_one)
    act_two = send_rows(act_two)
    grad_three = send_rows(after(grad_three, act_two[1]))
    order.tick(third, fourth)
    act_two = join_rows(act_two)
    cross_queries = order.run(lambda a: multiply(a, query_part, False), act_two)
    cross_flat, logsum_cross = order.run(
        lambda a: attend_cross(a, keyval, length_all, all_images, heads, score_scale),
        cross_queries,
    )
    branch_sum = GroupSum(order, cross_flat, merge_part, False)
    branch_sum.near()
    order.tick(third, fourth)
    branch_sum.rest()
    order.tick(third, fourth)

    def finish_cross(crossed):
        hidden_two = hidden_one + own_rows(branch_sum.mine + crossed.astype(jnp.float32))
        act = flatten(normed(hidden_two) * (1.0 + scale_mlp) + shift_mlp)
        return hidden_two, act.astype(jnp.bfloat16)

    hidden_two, act_three = order.run(finish_cross, branch_sum.crossed)
    norm_three = normed(hidden_two)
    act_three = send_rows(act_three)
    mixed_parts = send_columns(after(mixed_flat, act_three[1]))
    order.tick(third, fourth)
    act_three = join_rows(act_three)
    grad_three = join_rows(grad_three)
    cross_parts = send_columns(after(cross_flat, mixed_parts[2]))

    (up_part,) = order.run(
        lambda last: lay_out(
            third.pieces[:-1] + [last], third.starts(spot, shard_rows), [hidden // PEERS]
        ),
        third.pieces[-1],
    )
    activated, slope = order.run(
        lambda a: multiply(a, up_part, False, gate_and_slope, (jnp.bfloat16, jnp.bfloat16)),
        act_three,
    )
    (down_part,) = order.run(
        lambda last: lay_out(
            fourth.pieces[:-1] + [last], fourth.starts(spot, shard_rows), [width]
        ),
        fourth.pieces[-1],
    )
    mixed_all = join_columns(mixed_parts)

    def shard_start(shard):
        return shard * shard_rows

    def swapped_start(shard):
        begin = shard * shard_rows
        return ((begin // part) ^ rank) * part + begin % part

    def ring(values):
        return Scatter(order, [(values, 1, 0), (values, -1, 1)], group, spot, shard_rows // 2)

    grad_pre = order.run(
        lambda a: multiply(a, down_part, True, scaled, extra=(slope, 0)), grad_three
    )
    branch_sum = GroupSum(order, grad_pre, up_part, True).send()
    down_term = order.run(lambda a: weight_term(a, grad_three), activated)
    up_term = order.run(lambda a: weight_term(a, grad_pre), act_three)
    mlp_ring = Scatter(
        order,
        [([(down_term, shard_start)], 1, 0), ([(up_term, shard_start)], -1, 0)],
        group,
        spot,
        shard_rows,
    )

    def finish_mlp_back(crossed):
        grad_act = own_rows(branch_sum.mine + crossed.astype(jnp.float32))
        grad_two = grad_block + normed_back(hidden_two, grad_act * (1.0 + scale_mlp))
        return (
            jnp.sum(grad_act, axis=1),
            jnp.sum(grad_act * norm_three, axis=1),
            grad_two,
            flatten(grad_two).astype(jnp.bfloat16),
        )

    grad_shift_mlp, grad_scale_mlp, grad_two, grad_merge = order.run(
        finish_mlp_back, branch_sum.crossed
    )
    grad_merge = send_rows(grad_merge)
    cross_all_heads = join_columns(cross_parts)
    mlp_ring.reach(1)
    grad_merge = join_rows(grad_merge)

    grad_mixed = order.run(lambda a: multiply(a, merge_part, True), grad_merge)
    grad_query, grad_keyval = order.run(
        lambda a: attend_cross_back(
            cross_queries, keyval, length_all, logsum_cross, a, all_images, heads, score_scale
        ),
        grad_mixed,
    )
    branch_sum = GroupSum(order, grad_query, query_part, True)
    branch_sum.near()
    mlp_ring.reach(2)
    branch_sum.rest()
    query_term = order.run(lambda a: weight_term(a, grad_query), act_two)
    keyval_term = order.run(lambda a: weight_term(a, grad_keyval), text_all)
    merge_term = order.run(lambda a: weight_term(a, grad_merge, rank), cross_all_heads)
    cross_ring = ring(
        [(query_term, shard_start), (keyval_term, shard_start), (merge_term, swapped_start)]
    )
    mlp_ring.reach(3)

    def finish_cross_back(crossed):
        grad_act = own_rows(branch_sum.mine + crossed.astype(jnp.float32))
        grad_one = grad_two + normed_back(hidden_one, grad_act * gain_full)
        return (
            jnp.sum(grad_act * norm_two, axis=1),
            jnp.sum(grad_one * branch_one, axis=1),
            grad_one,
            flatten(gate_self * grad_one).astype(jnp.bfloat16),
        )

    gain_term, grad_gate_self, grad_one, grad_out = order.run(
        finish_cross_back, branch_sum.crossed
    )
    grad_out = send_rows(grad_out)
    mlp_ring.reach(4)
    cross_ring.reach(1)
    grad_out = join_rows(grad_out)

    grad_mixed = order.run(lambda a: multiply(a, out_part, True), grad_out)
    grad_qkv = order.run(
        lambda a: attend_self_back(qkv_act, logsum_self, a, all_images, heads, score_scale),
        grad_mixed,
    )
    branch_sum = GroupSum(order, grad_qkv, qkv_part, True)
    branch_sum.near()
    mlp_ring.reach(5)
    cross_ring.reach(2)
    branch_sum.rest()
    qkv_term = order.run(lambda a: weight_term(a, grad_qkv), act_one)
    out_term = order.run(lambda a: weight_term(a, grad_out, rank), mixed_all)
    self_ring = ring([(qkv_term, shard_start), (out_term, swapped_start)])
    mlp_ring.reach(6)
    cross_ring.reach(3)

    def finish_self_back(crossed):
        grad_act = own_rows(branch_sum.mine + crossed.astype(jnp.float32))
        image_grad = grad_one + normed_back(residual, grad_act * (1.0 + scale_self))
        return (
            jnp.sum(grad_act, axis=1),
            jnp.sum(grad_act * norm_one, axis=1),
            image_grad.astype(jnp.bfloat16),
        )

    grad_shift_self, grad_scale_self, image_grad = order.run(finish_self_back, branch_sum.crossed)

    cross_ring.reach(4)
    self_ring.reach(1)
    mlp_sum = GroupSum(order, activated, down_part, False)
    mlp_sum.near()
    mlp_ring.reach(7)
    down_all, up_all = [
        lax.all_gather(found, "rep", axis=0, tiled=True) for found in mlp_ring.sums
    ]
    mlp_sum.rest()
    cross_ring.reach(5)
    self_ring.reach(2)

    def finish_mlp(crossed):
        branch_three = own_rows(mlp_sum.mine + crossed.astype(jnp.float32))
        block_out = (hidden_two + gate_mlp * branch_three).astype(jnp.bfloat16)
        vectors = jnp.concatenate(
            [
                grad_shift_self,
                grad_scale_self,
                grad_gate_self,
                grad_shift_mlp,
                grad_scale_mlp,
                jnp.sum(grad_block * branch_three, axis=1),
                gain_term,
            ],
            axis=1,
        )
        return block_out, vectors.astype(jnp.bfloat16)

    block_out, vectors = order.run(finish_mlp, mlp_sum.crossed)
    everyone = Everyone(order, vectors, group)
    cross_ring.reach(6)
    self_ring.reach(3)
    everyone.hop()
    text_sum = GroupSum(order, grad_keyval, keyval_part, True)
    text_sum.near()
    cross_ring.reach(7)
    cross_all = lax.all_gather(jnp.concatenate(cross_ring.sums, axis=0), "rep", axis=0, tiled=True)
    self_ring.reach(4)
    text_sum.rest()
    everyone.hop()
    self_ring.reach(5)
    everyone.hop()
    down_grad = order.run(lambda a: spread_rows(a, width), down_all)
    text_grad = order.run(
        lambda crossed: (text_sum.mine + crossed.astype(jnp.float32))
        .astype(jnp.bfloat16)
        .reshape(text_tokens.shape),
        text_sum.crossed,
    )
    self_ring.reach(6)
    everyone.hop(len(everyone.hops))
    if aligned:
        up_grad = order.run(
            lambda a: spread_blocks(a, 0, group, hidden // (group * PEERS)), up_all
        )
    else:
        up_grad = (
            up_all.reshape(PEERS, shard_rows, group, -1)
            .transpose(1, 2, 0, 3)
            .reshape(shard_rows, hidden)
            .astype(jnp.float32)
        )
    self_ring.reach(7)
    self_all = lax.all_gather(
        jnp.concatenate(self_ring.sums, axis=0), "rep", axis=0, tiled=True
    )
    everyone.hop(1 + len(everyone.hops))

    def finish_modulation(found):
        return (
            outer_sum(conditions(all_steps), found[:, : 6 * width]),
            jnp.sum(
                lax.dynamic_slice_in_dim(
                    found, 6 * width + member * shard_rows, shard_rows, 1
                ).astype(jnp.float32),
                axis=0,
            ),
        )

    mod_grad, gain_grad = order.run(finish_modulation, everyone.value)
    query_grad = order.run(lambda a: spread_blocks(a, 0, 1, part), cross_all)
    keyval_grad = order.run(lambda a: spread_blocks(a, 1, 2, part), cross_all)
    merge_grad = order.run(lambda a: spread_blocks(a, 3, 1, part), cross_all)
    return (
        block_out,
        image_grad,
        text_grad,
        mod_grad,
        order.run(lambda a: spread_blocks(a, 0, 3, part), self_all),
        order.run(lambda a: spread_blocks(a, 3, 1, part), self_all),
        query_grad,
        keyval_grad,
        merge_grad,
        gain_grad,
        up_grad,
        down_grad,
    )


def solution(mesh):
    placed = (
        P(("rep", "fsdp"), None, None),
        P(("rep", "fsdp"), None, None),
        P(("rep", "fsdp")),
        P(("rep", "fsdp")),
        P(("rep", "fsdp"), None, None),
        P("fsdp", None),
        P("fsdp", None),
        P("fsdp", None),
        P("fsdp", None),
        P("fsdp", None),
        P("fsdp", None),
        P("fsdp"),
        P("fsdp", None),
        P("fsdp", None),
    )
    return jax.shard_map(
        body,
        mesh=mesh,
        in_specs=placed,
        out_specs=(
            P(("rep", "fsdp"), None, None),
            P(("rep", "fsdp"), None, None),
            P(("rep", "fsdp"), None, None),
            P("fsdp", None),
            P("fsdp", None),
            P("fsdp", None),
            P("fsdp", None),
            P("fsdp", None),
            P("fsdp", None),
            P("fsdp"),
            P("fsdp", None),
            P("fsdp", None),
        ),
        check_vma=False,
    )
```

```python
import math

import jax
import jax.numpy as jnp
from jax import lax
from jax.experimental import pallas as pl
from jax.experimental.pallas import tpu as pltpu
from jax.sharding import PartitionSpec as P

HEADS = 16


EPSILON = 1e-06


def matmul(left, right):
    return jnp.dot(left, right, preferred_element_type=jnp.float32)


def outer_sum(left, right):
    return lax.dot_general(
        left, right, (((0,), (0,)), ((), ())), preferred_element_type=jnp.float32
    )


def back_product(left, right):
    return lax.dot_general(
        left, right, (((1,), (1,)), ((), ())), preferred_element_type=jnp.float32
    )


def normed(value):
    return value * lax.rsqrt(jnp.mean(value * value, axis=-1, keepdims=True) + EPSILON)


def normed_back(value, grad):
    return jax.vjp(normed, value)[1](grad)[0]


def smooth_gate(value):
    return jax.nn.gelu(value, approximate=True)


def row_block(rows, columns, column=0):
    return pl.BlockSpec((rows, columns), lambda image, *_: (image, column))


def parts_of(value, count):
    width = value.shape[1] // count
    return [value[:, i * width : (i + 1) * width] for i in range(count)]


def scores_of(queries, keys, limit, scale):
    scores = back_product(queries, keys) * scale
    if limit is not None:
        slot = lax.broadcasted_iota(jnp.int32, scores.shape, 1)
        scores = jnp.where(slot < limit, scores, -jnp.inf)
    return scores


def attend_heads(queries, keys, values, limit, scale, mixed_ref, logsum_ref):
    head_width = keys[0].shape[1]
    for head, (query, key, value) in enumerate(zip(queries, keys, values)):
        scores = scores_of(query, key, limit, scale)
        row_top = jnp.max(scores, axis=1, keepdims=True)
        raised = jnp.exp(scores - row_top)
        totals = jnp.sum(raised, axis=1, keepdims=True)
        weights = (raised / totals).astype(jnp.bfloat16)
        mixed_ref[:, head * head_width : (head + 1) * head_width] = matmul(weights, value).astype(
            jnp.bfloat16
        )
        logsum_ref[:, head : head + 1] = row_top + jnp.log(totals)


def attend_heads_back(queries, keys, values, limit, scale, logsum_ref, grads, outs):
    grad_query_ref, grad_key_ref, grad_value_ref = outs
    for head, (query, key, value, grad) in enumerate(zip(queries, keys, values, grads)):
        scores = scores_of(query, key, limit, scale)
        weights = jnp.exp(scores - logsum_ref[:, head : head + 1])
        grad_weights = back_product(grad, value)
        grad_value_ref(head, outer_sum(weights.astype(jnp.bfloat16), grad))
        inner_sum = jnp.sum(weights * grad_weights, axis=1, keepdims=True)
        grad_scores = (scale * (weights * (grad_weights - inner_sum))).astype(jnp.bfloat16)
        grad_query_ref(head, matmul(grad_scores, key))
        grad_key_ref(head, outer_sum(grad_scores, query))


def head_writer(ref, first, width):
    def write(head, value):
        start = first + head * width
        ref[:, start : start + width] = value.astype(jnp.bfloat16)

    return write


VMEM_LIMIT = 48 * 1024 * 1024


def cost(flops, moved, transcendentals=0):
    return pl.CostEstimate(
        flops=int(flops), bytes_accessed=int(moved), transcendentals=int(transcendentals)
    )


def attention_cost(images, length, slots, heads, width, products):
    pairs = images * heads * length * slots
    return cost(2 * products * pairs * width, 8 * pairs, pairs)


def attend_self(qkv, images, heads, scale):
    rows, columns = qkv.shape
    length, part = rows // images, columns // 3

    def kernel(qkv_ref, mixed_ref, logsum_ref):
        blocks = parts_of(qkv_ref, 3 * heads)
        attend_heads(
            blocks[:heads],
            blocks[heads : 2 * heads],
            blocks[2 * heads :],
            None,
            scale,
            mixed_ref,
            logsum_ref,
        )

    return pl.pallas_call(
        kernel,
        grid=(images,),
        in_specs=[row_block(length, columns)],
        out_specs=[row_block(length, part), row_block(length, heads)],
        out_shape=[
            jax.ShapeDtypeStruct((rows, part), jnp.bfloat16),
            jax.ShapeDtypeStruct((rows, heads), jnp.float32),
        ],
        compiler_params=pltpu.CompilerParams(vmem_limit_bytes=VMEM_LIMIT),
        cost_estimate=attention_cost(images, length, length, heads, part // heads, 2),
        name="attend_self",
    )(qkv)


def attend_self_back(qkv, logsum, grad_mixed, images, heads, scale):
    rows, columns = qkv.shape
    length, part = rows // images, columns // 3

    def kernel(qkv_ref, logsum_ref, grad_ref, out_ref):
        blocks = parts_of(qkv_ref, 3 * heads)
        writers = [head_writer(out_ref, i * part, part // heads) for i in range(3)]
        attend_heads_back(
            blocks[:heads],
            blocks[heads : 2 * heads],
            blocks[2 * heads :],
            None,
            scale,
            logsum_ref,
            parts_of(grad_ref, heads),
            writers,
        )

    return pl.pallas_call(
        kernel,
        grid=(images,),
        in_specs=[row_block(length, columns), row_block(length, heads), row_block(length, part)],
        out_specs=row_block(length, columns),
        out_shape=jax.ShapeDtypeStruct((rows, columns), jnp.bfloat16),
        compiler_params=pltpu.CompilerParams(vmem_limit_bytes=VMEM_LIMIT),
        cost_estimate=attention_cost(images, length, length, heads, part // heads, 5),
        name="attend_self_back",
    )(qkv, logsum, grad_mixed)


def attend_cross(queries, keyval, limits, images, heads, scale):
    rows, part = queries.shape
    length, slots = rows // images, keyval.shape[0] // images

    def kernel(limits_ref, query_ref, keyval_ref, mixed_ref, logsum_ref):
        blocks = parts_of(keyval_ref, 2 * heads)
        attend_heads(
            parts_of(query_ref, heads),
            blocks[:heads],
            blocks[heads:],
            limits_ref[pl.program_id(0)],
            scale,
            mixed_ref,
            logsum_ref,
        )

    return pl.pallas_call(
        kernel,
        grid_spec=pltpu.PrefetchScalarGridSpec(
            num_scalar_prefetch=1,
            grid=(images,),
            in_specs=[row_block(length, part), row_block(slots, 2 * part)],
            out_specs=[row_block(length, part), row_block(length, heads)],
        ),
        out_shape=[
            jax.ShapeDtypeStruct((rows, part), jnp.bfloat16),
            jax.ShapeDtypeStruct((rows, heads), jnp.float32),
        ],
        compiler_params=pltpu.CompilerParams(vmem_limit_bytes=VMEM_LIMIT),
        cost_estimate=attention_cost(images, length, slots, heads, part // heads, 2),
        name="attend_cross",
    )(limits, queries, keyval)


def attend_cross_back(queries, keyval, limits, logsum, grad_mixed, images, heads, scale):
    rows, part = queries.shape
    length, slots = rows // images, keyval.shape[0] // images

    def kernel(limits_ref, query_ref, keyval_ref, logsum_ref, grad_ref, out_ref, text_ref):
        blocks = parts_of(keyval_ref, 2 * heads)
        width = part // heads
        attend_heads_back(
            parts_of(query_ref, heads),
            blocks[:heads],
            blocks[heads:],
            limits_ref[pl.program_id(0)],
            scale,
            logsum_ref,
            parts_of(grad_ref, heads),
            [
                head_writer(out_ref, 0, width),
                head_writer(text_ref, 0, width),
                head_writer(text_ref, part, width),
            ],
        )

    return pl.pallas_call(
        kernel,
        grid_spec=pltpu.PrefetchScalarGridSpec(
            num_scalar_prefetch=1,
            grid=(images,),
            in_specs=[
                row_block(length, part),
                row_block(slots, 2 * part),
                row_block(length, heads),
                row_block(length, part),
            ],
            out_specs=[row_block(length, part), row_block(slots, 2 * part)],
        ),
        out_shape=[
            jax.ShapeDtypeStruct((rows, part), jnp.bfloat16),
            jax.ShapeDtypeStruct((images * slots, 2 * part), jnp.bfloat16),
        ],
        compiler_params=pltpu.CompilerParams(vmem_limit_bytes=VMEM_LIMIT),
        cost_estimate=attention_cost(images, length, slots, heads, part // heads, 5),
        name="attend_cross_back",
    )(limits, queries, keyval, logsum, grad_mixed)


def pick_blocks(weights, counts, rank):
    rows = weights[0].shape[0]
    width = weights[0].shape[1] // (counts[0] * PEERS)
    firsts = [sum(counts[:i]) for i in range(len(counts))]

    def kernel(rank_ref, *refs):
        step = pl.program_id(0)
        out_ref = refs[-1]
        for ref, first, count in zip(refs, firsts, counts):

            @pl.when((step >= first) & (step < first + count))
            def _():
                out_ref[...] = ref[...]

    def spec(first, count):
        return pl.BlockSpec(
            (rows, width),
            lambda step, rank_ref: (
                0,
                jnp.clip(step - first, 0, count - 1) * PEERS + rank_ref[0],
            ),
        )

    return pl.pallas_call(
        kernel,
        grid_spec=pltpu.PrefetchScalarGridSpec(
            num_scalar_prefetch=1,
            grid=(sum(counts),),
            in_specs=[spec(first, count) for first, count in zip(firsts, counts)],
            out_specs=pl.BlockSpec((rows, width), lambda step, rank_ref: (0, step)),
        ),
        out_shape=jax.ShapeDtypeStruct((rows, width * sum(counts)), weights[0].dtype),
        cost_estimate=cost(0, 4 * rows * width * sum(counts)),
        name="pick_blocks",
    )(rank.reshape(1), *weights)


def spread_blocks(found, first, count, width):
    rows = found.shape[0] // PEERS

    def kernel(found_ref, out_ref):
        for peer in range(PEERS):
            out_ref[:, peer * width : (peer + 1) * width] = found_ref[
                peer * rows : (peer + 1) * rows, :
            ].astype(jnp.float32)

    return pl.pallas_call(
        kernel,
        grid=(count,),
        in_specs=[pl.BlockSpec((PEERS * rows, width), lambda block: (0, first + block))],
        out_specs=pl.BlockSpec((rows, PEERS * width), lambda block: (0, block)),
        out_shape=jax.ShapeDtypeStruct((rows, count * PEERS * width), jnp.float32),
        cost_estimate=cost(0, 6 * rows * count * PEERS * width),
        compiler_params=pltpu.CompilerParams(vmem_limit_bytes=VMEM_LIMIT),
        name="spread_blocks",
    )(found)


def spread_peers(found, rank, first, count, width):
    rows = found[0].shape[0]

    def kernel(rank_ref, *refs):
        for peer in range(PEERS):
            for mask in range(PEERS):

                @pl.when((rank_ref[0] ^ mask) == peer)
                def _():
                    refs[-1][:, peer * width : (peer + 1) * width] = refs[mask][...].astype(
                        jnp.float32
                    )

    return pl.pallas_call(
        kernel,
        grid_spec=pltpu.PrefetchScalarGridSpec(
            num_scalar_prefetch=1,
            grid=(count,),
            in_specs=[pl.BlockSpec((rows, width), lambda block, rank_ref: (0, first + block))]
            * PEERS,
            out_specs=pl.BlockSpec((rows, PEERS * width), lambda block, rank_ref: (0, block)),
        ),
        out_shape=jax.ShapeDtypeStruct((rows, count * PEERS * width), jnp.float32),
        cost_estimate=cost(0, 6 * rows * count * PEERS * width),
        compiler_params=pltpu.CompilerParams(vmem_limit_bytes=VMEM_LIMIT),
        name="spread_peers",
    )(rank.reshape(1), *found)


def spread_rows(found, width):
    rows = found.shape[0] // PEERS

    def kernel(found_ref, out_ref):
        out_ref[...] = found_ref[...].astype(jnp.float32)

    return pl.pallas_call(
        kernel,
        grid=(PEERS,),
        in_specs=[pl.BlockSpec((rows, width), lambda peer: (peer, 0))],
        out_specs=pl.BlockSpec((rows, width), lambda peer: (peer, 0)),
        out_shape=jax.ShapeDtypeStruct((PEERS * rows, width), jnp.float32),
        cost_estimate=cost(0, 6 * PEERS * rows * width),
        compiler_params=pltpu.CompilerParams(vmem_limit_bytes=VMEM_LIMIT),
        name="spread_rows",
    )(found)


PEERS = 4


def swap(value, mask):
    return lax.ppermute(value, "rep", [(peer, peer ^ mask) for peer in range(PEERS)])


def stack_rows(parts):
    rows, columns = parts[0].shape
    count = len(parts)

    def kernel(*refs):
        ins, out, held, arrived, left = refs[:count], refs[count], refs[-3], refs[-2], refs[-1]
        fetches = [
            pltpu.make_async_copy(ins[i], held.at[i], arrived.at[i]) for i in range(count)
        ]
        stores = [
            pltpu.make_async_copy(held.at[i], out.at[i * rows : (i + 1) * rows, :], left.at[i])
            for i in range(count)
        ]
        for fetch in fetches:
            fetch.start()
        for fetch, store in zip(fetches, stores):
            fetch.wait()
            store.start()
        for store in stores:
            store.wait()

    return pl.pallas_call(
        kernel,
        in_specs=[pl.BlockSpec(memory_space=pl.ANY)] * count,
        out_specs=pl.BlockSpec(memory_space=pl.ANY),
        out_shape=jax.ShapeDtypeStruct((count * rows, columns), parts[0].dtype),
        scratch_shapes=[
            pltpu.VMEM((count, rows, columns), parts[0].dtype),
            pltpu.SemaphoreType.DMA((count,)),
            pltpu.SemaphoreType.DMA((count,)),
        ],
        cost_estimate=cost(0, 4 * count * rows * columns),
        compiler_params=pltpu.CompilerParams(vmem_limit_bytes=VMEM_LIMIT),
        name="stack_rows",
    )(*parts)


def stack_columns(parts):
    orders = ((0, 1, 2, 3), (2, 3, 0, 1), (1, 0, 3, 2), (3, 2, 1, 0))
    rows, columns = parts[0].shape
    block = rows // PEERS

    def kernel(*refs):
        for i, order in enumerate(orders):

            @pl.when(pl.program_id(0) == i)
            def _():
                for j, source in enumerate(order):
                    refs[-1][j * block : (j + 1) * block, :] = refs[i][
                        source * block : (source + 1) * block, :
                    ]

    return pl.pallas_call(
        kernel,
        grid=(PEERS,),
        in_specs=[pl.BlockSpec((rows, columns), lambda step: (0, 0))] * PEERS,
        out_specs=pl.BlockSpec((rows, columns), lambda step: (0, step)),
        out_shape=jax.ShapeDtypeStruct((rows, PEERS * columns), parts[0].dtype),
        cost_estimate=cost(0, 4 * PEERS * rows * columns),
        compiler_params=pltpu.CompilerParams(vmem_limit_bytes=VMEM_LIMIT),
        name="stack_columns",
    )(*parts)


def narrow(total):
    return (total.astype(jnp.bfloat16),)


def plus(total, extra):
    return (total + extra.astype(jnp.float32),)


def narrow_plus(total, extra):
    return ((total + extra.astype(jnp.float32)).astype(jnp.bfloat16),)


def halves(total):
    rows = total.shape[0] // 2
    return (total[:rows].astype(jnp.bfloat16), total[rows:].astype(jnp.bfloat16))


def scaled(total, factor):
    return ((total * factor.astype(jnp.float32)).astype(jnp.bfloat16),)


def gate_and_slope(total):
    value, back = jax.vjp(smooth_gate, total)
    return (value.astype(jnp.bfloat16), back(jnp.ones_like(total))[0].astype(jnp.bfloat16))


def multiply(
    left, right, turned, finish=narrow, types=(jnp.bfloat16,), first=0, rows=None, extra=None, half=None
):
    rows = left.shape[0] if rows is None else rows
    depth = left.shape[1]
    breadth = right.shape[1] // (1 if half is None else 2)
    columns = right.shape[0] if turned else breadth
    width = min(512, columns)
    skip = 0 if half is None else half * breadth // (depth if turned else width)
    product = back_product if turned else matmul
    tall = rows // 2 if finish is halves else rows

    def kernel(*refs):
        left_ref, right_ref = refs[:2]
        outs = refs[-len(types) :]
        blocks = [ref[...] for ref in refs[2 : -len(types)]]
        for out, value in zip(outs, finish(product(left_ref[...], right_ref[...]), *blocks)):
            out[...] = value

    specs = [
        pl.BlockSpec((rows, depth), lambda step: (first // rows, 0)),
        pl.BlockSpec((width, depth), lambda step: (step, skip))
        if turned
        else pl.BlockSpec((depth, width), lambda step: (0, skip + step)),
    ]
    values = [left, right]
    if extra is not None:
        extra, start = extra
        specs.append(pl.BlockSpec((rows, width), lambda step: (start // rows, step)))
        values.append(extra)
    found = pl.pallas_call(
        kernel,
        grid=(columns // width,),
        in_specs=specs,
        out_specs=[pl.BlockSpec((tall, width), lambda step: (0, step))] * len(types),
        out_shape=[jax.ShapeDtypeStruct((tall, columns), kind) for kind in types],
        cost_estimate=cost(2 * rows * depth * columns, 2 * (rows * depth + depth * columns + rows * columns)),
        compiler_params=pltpu.CompilerParams(vmem_limit_bytes=VMEM_LIMIT),
        name="multiply",
    )(*values)
    return found[0] if len(types) == 1 else found


def weight_term(left, right, rank=None, into=None, first=0, total=None):
    depth, rows = left.shape
    columns = right.shape[1] if rank is None else right.shape[1] // PEERS
    height = min(1024, rows) if rank is None else rows // PEERS
    width = min(512, columns)
    shift = columns // width
    chosen = jnp.zeros((1,), jnp.int32) if rank is None else rank.reshape(1)
    total = columns if total is None else total

    def kernel(chosen_ref, left_ref, right_ref, *refs):
        refs[-1][...] = outer_sum(left_ref[...], right_ref[...]).astype(jnp.bfloat16)

    return pl.pallas_call(
        kernel,
        grid_spec=pltpu.PrefetchScalarGridSpec(
            num_scalar_prefetch=1,
            grid=(columns // width, rows // height),
            in_specs=[
                pl.BlockSpec(
                    (depth, height),
                    lambda j, i, chosen_ref: (0, i if rank is None else i ^ chosen_ref[0]),
                ),
                pl.BlockSpec(
                    (depth, width), lambda j, i, chosen_ref: (0, chosen_ref[0] * shift + j)
                ),
            ]
            + [pl.BlockSpec(memory_space=pl.ANY)] * (into is not None),
            out_specs=pl.BlockSpec(
                (height, width), lambda j, i, chosen_ref: (i, first // width + j)
            ),
        ),
        out_shape=jax.ShapeDtypeStruct((rows, total), jnp.bfloat16),
        input_output_aliases={} if into is None else {3: 0},
        cost_estimate=cost(
            2 * rows * depth * columns, 2 * (rows * depth + depth * columns + rows * columns)
        ),
        compiler_params=pltpu.CompilerParams(vmem_limit_bytes=VMEM_LIMIT),
        name="weight_term",
    )(chosen, left, right, *([] if into is None else [into]))


def multiply_rest(left, right, turned, got):
    (rows, columns), depth = got[0].shape, left.shape[1]
    width = min(512, columns)
    product = back_product if turned else matmul

    def kernel(left_ref, right_ref, got_ref, got_far_ref, own_ref, far_ref):
        total = product(left_ref[...], right_ref[...])
        own_ref[...] = total[:rows] + got_ref[...].astype(jnp.float32)
        far_ref[...] = (total[rows:] + got_far_ref[...].astype(jnp.float32)).astype(jnp.bfloat16)

    return pl.pallas_call(
        kernel,
        grid=(columns // width,),
        in_specs=[
            pl.BlockSpec((2 * rows, depth), lambda step: (0, 0)),
            pl.BlockSpec((width, depth), lambda step: (step, 0))
            if turned
            else pl.BlockSpec((depth, width), lambda step: (0, step)),
        ]
        + [pl.BlockSpec((rows, width), lambda step: (0, step))] * 2,
        out_specs=[pl.BlockSpec((rows, width), lambda step: (0, step))] * 2,
        out_shape=[
            jax.ShapeDtypeStruct((rows, columns), jnp.float32),
            jax.ShapeDtypeStruct((rows, columns), jnp.bfloat16),
        ],
        cost_estimate=cost(
            4 * rows * depth * columns, 2 * (2 * rows * depth + depth * columns + 5 * rows * columns)
        ),
        compiler_params=pltpu.CompilerParams(vmem_limit_bytes=VMEM_LIMIT),
        name="multiply_rest",
    )(left, right, *got)


class Order:
    def __init__(self):
        self.token = ()

    def run(self, work, first, *others):
        if self.token:
            first, self.token = lax.optimization_barrier((first, self.token))
        found = work(first, *others)
        self.token = tuple(jax.tree.leaves(found))
        return found

    def hold(self, value):
        value, self.token = lax.optimization_barrier((value, self.token))
        return value

    def tick(self, *rings):
        heads = [ring.pieces[-1] for ring in rings]
        heads, self.token = lax.optimization_barrier((heads, self.token))
        for ring, head in zip(rings, heads):
            ring.pieces[-1] = head
            if ring.sevenths < 7:
                ring.send()

    def wait(self, *values):
        self.token = self.token + tuple(jax.tree.leaves(values))


class State:
    pass


class GroupSum:
    def __init__(self, order, left, right, turned, half=None):
        self.order, self.left, self.right, self.turned = order, left, right, turned
        self.half = half
        self.rows = left.shape[0] // PEERS

    def near(self):
        rows = self.rows
        sent = self.order.run(
            lambda left: multiply(
                left,
                self.right,
                self.turned,
                halves,
                (jnp.bfloat16, jnp.bfloat16),
                first=2 * rows,
                rows=2 * rows,
            ),
            self.left,
        )
        self.got = [swap(part, 1) for part in sent]

    def rest(self):
        self.mine, self.sent = self.order.run(
            lambda left: multiply_rest(left, self.right, self.turned, self.got), self.left
        )
        self.crossed = swap(self.sent, 2)

    def send(self):
        self.near()
        self.rest()
        return self

def ring_member(place, size):
    place = place % size
    return jnp.where(place < size // 2, 2 * place, 2 * (size - 1 - place) + 1)


def ring_pairs(size, step):
    order = [2 * i for i in range(size // 2)] + [2 * i + 1 for i in reversed(range(size // 2))]
    return [(order[i], order[(i + step) % size]) for i in range(size)]


def after(value, earlier):
    return lax.optimization_barrier((value, earlier))[0]


class Gather:
    def __init__(self, value, size, step):
        self.size, self.step, self.pieces = size, step, [value]
        self.sevenths = 0

    def send(self):
        self.sevenths += 1
        while len(self.pieces) - 1 < self.sevenths * (self.size - 1) // 7:
            self.pieces.append(
                lax.ppermute(self.pieces[-1], "fsdp", ring_pairs(self.size, self.step))
            )

    def starts(self, place, rows):
        return jnp.stack(
            [ring_member(place - self.step * k, self.size) * rows for k in range(self.size)]
        ).astype(jnp.int32)


def lay_out(pieces, starts, widths):
    size = len(pieces)
    rows = pieces[0].shape[0]
    count = len(widths)
    edges = [sum(widths[:i]) for i in range(count)]

    def kernel(starts_ref, *refs):
        shards, outs, done = refs[:size], refs[size:-1], refs[-1]
        copies = []
        for i, shard in enumerate(shards):
            start = pl.multiple_of(starts_ref[i], rows)
            for j, out in enumerate(outs):
                copies.append(
                    pltpu.make_async_copy(
                        shard.at[:, edges[j] : edges[j] + widths[j]],
                        out.at[pl.ds(start, rows), :],
                        done.at[i, j],
                    )
                )
        for copy in copies:
            copy.start()
        for copy in copies:
            copy.wait()

    return pl.pallas_call(
        kernel,
        out_shape=[jax.ShapeDtypeStruct((size * rows, w), pieces[0].dtype) for w in widths],
        in_specs=[pl.BlockSpec(memory_space=pltpu.SMEM)]
        + [pl.BlockSpec(memory_space=pltpu.VMEM)] * size,
        out_specs=[pl.BlockSpec(memory_space=pl.ANY)] * count,
        scratch_shapes=[pltpu.SemaphoreType.DMA((size, count))],
        compiler_params=pltpu.CompilerParams(vmem_limit_bytes=VMEM_LIMIT),
        cost_estimate=cost(0, 4 * size * rows * sum(widths)),
        name="lay_out",
    )(starts, *pieces)


def ring_add(values, spots, rows, got):
    count = len(values)
    columns = values[0].shape[1]
    width = min(1024, columns)

    def kernel(spots_ref, *refs):
        for i in range(count):
            block = refs[i][...]
            refs[-count + i][...] = block if got is None else refs[count + i][...] + block

    def spec(i):
        return pl.BlockSpec((rows, width), lambda step, spots_ref: (spots_ref[i], step))

    plain = [pl.BlockSpec((rows, width), lambda step, spots_ref: (0, step))] * count
    arrived = [] if got is None else list(got)
    return pl.pallas_call(
        kernel,
        grid_spec=pltpu.PrefetchScalarGridSpec(
            num_scalar_prefetch=1,
            grid=(columns // width,),
            in_specs=[spec(i) for i in range(count)] + plain[: len(arrived)],
            out_specs=plain,
        ),
        out_shape=[jax.ShapeDtypeStruct((rows, columns), jnp.bfloat16)] * count,
        cost_estimate=cost(rows * columns * count, 6 * rows * columns * count),
        compiler_params=pltpu.CompilerParams(vmem_limit_bytes=VMEM_LIMIT),
        name="ring_add",
    )(spots, *values, *arrived)


class Scatter:
    def __init__(self, order, entries, size, place, rows, shard_rows):
        self.order, self.entries = order, entries
        self.size, self.place, self.rows, self.step = size, place, rows, 0
        self.sevenths, self.blocks = 0, shard_rows // rows
        self.values = [value for value, _, _ in entries]
        self.sums = order.run(
            lambda first: ring_add([first] + self.values[1:], self.spots(), self.rows, None),
            self.values[0],
        )

    def spots(self):
        return jnp.stack(
            [
                ring_member(self.place - direction * (self.step + 1), self.size) * self.blocks
                + block
                for _, direction, block in self.entries
            ]
        ).astype(jnp.int32)

    def reach(self):
        self.sevenths += 1
        while self.step < self.sevenths * (self.size - 1) // 7:
            self.step += 1
            arrived = [
                lax.ppermute(value, "fsdp", ring_pairs(self.size, direction))
                for value, (_, direction, _) in zip(self.sums, self.entries)
            ]
            spots = self.spots()
            self.sums = self.order.run(
                lambda got: ring_add(self.values, spots, self.rows, got), arrived
            )
        return self.sevenths == 7


class Exchange:
    def __init__(self, order, value, size):
        self.order, self.value, self.size, self.mask = order, value[None], size, 1
        self.send()

    def send(self):
        pairs = [(i, i ^ self.mask) for i in range(self.size)]
        self.got = lax.ppermute(self.value, "fsdp", pairs)

    def hop(self):
        low = (lax.axis_index("fsdp") & self.mask) == 0

        def join(got):
            return jnp.concatenate(
                [jnp.where(low, self.value, got), jnp.where(low, got, self.value)], axis=0
            )

        self.value = self.order.run(join, self.got)
        self.mask *= 2
        if self.mask < self.size:
            self.send()


class Everyone:
    def __init__(self, order, value, size):
        self.order, self.value = order, value
        self.hops = [("fsdp", size // 2 >> i, size) for i in range(size.bit_length() - 1)]
        self.hops += [("rep", 2, PEERS), ("rep", 1, PEERS)]
        self.left = len(self.hops)
        self.send()

    def send(self):
        axis, mask, size = self.hops.pop(0)
        self.got = lax.ppermute(self.value, axis, [(i, i ^ mask) for i in range(size)])

    def hop(self):
        if self.left:
            self.value = self.order.run(
                lambda got: jnp.concatenate([self.value, got], axis=0), self.got
            )
            self.left -= 1
            if self.hops:
                self.send()


PLAN = (
    "p1", "p2", "a0", "r", "p3", "p4", "A", "e", "A", "e", "A", "e", "terms", "A", "start", "xa",
    "A", "ja", "st", "xt", "A", "jt", "sg", "A", "ab", "lay1", "lay2", "qkv", "B", "kv", "B",
    "self", "wo", "near1", "rest1", "wm", "B", "x1", "fin1", "y2", "B", "join2", "sm", "cq",
    "cross", "near2", "B", "rest2", "x2", "B", "fin2", "y3", "B", "join3", "sc", "jm", "jg",
    "lay3", "up", "lay4", "pre", "near3", "rest3", "dterm", "uterm", "F0", "x3", "fin3", "jc",
    "near6", "y4", "F", "join4", "mm4", "cback", "near4", "F", "rest4", "qterm", "kterm", "mterm",
    "C0", "x4", "F", "fin4", "rest6", "y5", "F", "C", "join5", "mm5", "sback", "near5", "F", "C",
    "rest5", "qkvterm", "oterm", "S0", "x5", "F", "C", "fin5", "C", "S", "F", "C", "S", "x6",
    "fin6", "C", "S", "h", "near7", "C", "S", "rest7", "h", "S", "h", "dout", "fin7", "S", "h",
    "uout", "S", "h", "mod", "cout", "sout",
)


def body(
    image_tokens,
    text_tokens,
    text_lengths,
    timesteps,
    cotangent,
    mod_weight,
    qkv_weight,
    out_weight,
    query_weight,
    keyval_weight,
    merge_weight,
    cross_gain,
    up_weight,
    down_weight,
):
    images, length, width = image_tokens.shape
    text_count, text_width = text_tokens.shape[1:]
    group = lax.axis_size("fsdp")
    rank = lax.axis_index("rep")
    member = lax.axis_index("fsdp")
    heads = HEADS // PEERS
    head_width = width // HEADS
    part = width // PEERS
    score_scale = head_width ** (-0.5)
    shard_rows = mod_weight.shape[0]
    hidden = up_weight.shape[1]
    rows = images * length
    all_images = PEERS * images

    def own_part(value, blocks):
        count = value.shape[1] // (blocks * PEERS)
        return lax.dynamic_index_in_dim(
            value.reshape(value.shape[0], blocks, PEERS, count), rank, 2, keepdims=False
        ).reshape(value.shape[0], blocks * count)

    def ordered(found):
        stacked = jnp.stack(found)
        return [
            lax.dynamic_index_in_dim(stacked, rank ^ place, 0, keepdims=False)
            for place in range(PEERS)
        ]

    def columns_to_rows(value):
        blocks = value.reshape(PEERS, part, -1)
        found = [
            lax.dynamic_index_in_dim(blocks, rank ^ mask, 0, keepdims=False)
            for mask in range(PEERS)
        ]
        found = [found[0]] + [swap(found[mask], mask) for mask in range(1, PEERS)]
        return jnp.concatenate(ordered(found), axis=1)

    order = Order()
    aligned = hidden // (group * PEERS) % 128 == 0
    spot = jnp.where(member % 2 == 0, member // 2, group - 1 - member // 2)
    def flatten(value):
        return value.reshape(-1, value.shape[-1])

    def own_rows(value):
        return value.reshape(images, length, width)

    half_width = width // 2
    column = member * shard_rows + jnp.arange(shard_rows, dtype=jnp.int32)
    place = jnp.where(column < half_width, column, column - half_width)
    frequency = jnp.exp(-math.log(10000.0) * place.astype(jnp.float32) / half_width)

    def conditions(steps):
        angles = steps.astype(jnp.float32)[:, None] * frequency[None, :]
        return jnp.where(column < half_width, jnp.sin(angles), jnp.cos(angles)).astype(
            jnp.bfloat16
        )

    residual = image_tokens.astype(jnp.float32)
    grad_block = cotangent.astype(jnp.float32)
    norm_one = normed(residual)

    def send_rows(value):
        return [value, swap(value, 2), swap(value, 1)]

    def join_rows(parts):
        far = order.hold(parts[1])
        return order.run(
            lambda last: stack_rows([parts[0], far, parts[2], last]), swap(far, 1)
        )

    def send_columns(value):
        return [value, swap(value, 1), swap(value, 2)]

    def join_columns(parts):
        far = order.hold(parts[2])
        return order.run(
            lambda last: stack_columns([parts[0], parts[1], far, last]), swap(far, 1)
        )

    v = State()
    mine = jnp.concatenate([timesteps, text_lengths]).astype(jnp.float32)
    mine = [mine, swap(mine, 2), swap(mine, 1)]

    def p1():
        v.pick1 = order.run(lambda w: pick_blocks([w, out_weight], [3, 1], rank), qkv_weight)

    def p2():
        v.pick2 = order.run(
            lambda w: pick_blocks([w, keyval_weight, merge_weight], [1, 2, 1], rank),
            query_weight,
        )

    def p3():
        v.pick3 = order.run(
            lambda w: pick_blocks([w], [group], rank) if aligned else own_part(w, group),
            up_weight,
        )

    def p4():
        v.pick4 = order.run(
            lambda w: lax.dynamic_index_in_dim(
                w.reshape(PEERS, -1, width), rank, 0, keepdims=False
            ),
            down_weight,
        )

    def a0():
        v.first, v.second = Gather(v.pick1, group, 1), Gather(v.pick2, group, -1)
        order.tick(v.first, v.second)

    def ab():
        v.third, v.fourth = Gather(v.pick3, group, 1), Gather(v.pick4, group, -1)
        order.tick(v.first, v.second, v.third, v.fourth)

    def r():
        far = order.hold(mine[1])
        found = order.run(
            lambda last: jnp.stack([mine[0], far, mine[2], last]), swap(far, 1)
        )
        v.length_all = found[:, images:].reshape(-1).astype(jnp.int32)
        v.exchange = Exchange(
            order,
            jnp.concatenate([found[:, :images].reshape(-1), cross_gain.astype(jnp.float32)]),
            group,
        )

    def e():
        v.exchange.hop()

    def terms():
        while v.exchange.mask < group:
            e()
        small = v.exchange.value
        v.gain_full = small[:, all_images:].reshape(-1)
        sequence = [0]
        while len(sequence) < group:
            sequence += [index + group // (2 * len(sequence)) for index in sequence]
        steps = small[:, :all_images][member ^ jnp.array(sequence, dtype=jnp.int32)]
        v.all_steps = steps.reshape(group, PEERS, images).transpose(1, 0, 2).reshape(-1)
        found = order.run(
            lambda steps: matmul(conditions(steps), mod_weight), small[:, :images].reshape(-1)
        )
        v.terms = lax.all_to_all(
            found.reshape(group, images, -1), "fsdp", split_axis=0, concat_axis=0, tiled=True
        )

    def start():
        def work(found):
            pieces = jnp.sum(found, axis=0).reshape(images, 6, 1, width)
            act = flatten(normed(residual) * (1.0 + pieces[:, 1]) + pieces[:, 0])
            grad_three = flatten(pieces[:, 5] * grad_block)
            return pieces, act.astype(jnp.bfloat16), grad_three.astype(jnp.bfloat16)

        pieces, act_one, v.grad_three = order.run(work, v.terms)
        v.shift_self, v.scale_self, v.gate_self = (pieces[:, 0], pieces[:, 1], pieces[:, 2])
        v.shift_mlp, v.scale_mlp, v.gate_mlp = (pieces[:, 3], pieces[:, 4], pieces[:, 5])
        v.act_one = send_rows(act_one)

    def ja():
        v.act_one = join_rows(v.act_one)

    def st():
        v.text_all = send_rows(order.hold(flatten(text_tokens)))

    def jt():
        v.text_all = join_rows(v.text_all)

    def sg():
        v.grad_three = send_rows(order.hold(v.grad_three))

    def jg():
        v.grad_three = join_rows(v.grad_three)

    def lay1():
        v.qkv_part, out_part = order.run(
            lambda last: lay_out(
                v.first.pieces[:-1] + [last], v.first.starts(spot, shard_rows), [3 * part, part]
            ),
            v.first.pieces[-1],
        )
        v.out_part = columns_to_rows(out_part)

    def lay2():
        v.query_part, v.keyval_part, merge_part = order.run(
            lambda last: lay_out(
                v.second.pieces[:-1] + [last],
                v.second.starts(spot, shard_rows),
                [part, 2 * part, part],
            ),
            v.second.pieces[-1],
        )
        v.merge_part = columns_to_rows(merge_part)

    def qkv():
        v.qkv_act = order.run(lambda a: multiply(a, v.qkv_part, False), v.act_one)

    def kv():
        v.keyval = order.run(lambda a: multiply(a, v.keyval_part, False), v.text_all)

    def self_attend():
        v.mixed_flat, v.logsum_self = order.run(
            lambda a: attend_self(a, all_images, heads, score_scale), v.qkv_act
        )

    def near1():
        v.sum1 = GroupSum(order, v.mixed_flat, v.out_part, False)
        v.sum1.near()

    def fin1():
        def finish(crossed):
            branch_one = own_rows(v.sum1.mine + crossed.astype(jnp.float32))
            hidden_one = residual + v.gate_self * branch_one
            return (
                branch_one,
                hidden_one,
                flatten(normed(hidden_one) * v.gain_full).astype(jnp.bfloat16),
            )

        v.branch_one, v.hidden_one, act_two = order.run(finish, v.sum1.crossed)
        v.norm_two = normed(v.hidden_one)
        v.act_two = send_rows(act_two)

    def join2():
        v.act_two = join_rows(v.act_two)

    def cq():
        v.cross_queries = order.run(lambda a: multiply(a, v.query_part, False), v.act_two)

    def cross():
        v.cross_flat, v.logsum_cross = order.run(
            lambda a: attend_cross(a, v.keyval, v.length_all, all_images, heads, score_scale),
            v.cross_queries,
        )

    def near2():
        v.sum2 = GroupSum(order, v.cross_flat, v.merge_part, False)
        v.sum2.near()

    def fin2():
        def finish(crossed):
            hidden_two = v.hidden_one + own_rows(v.sum2.mine + crossed.astype(jnp.float32))
            act = flatten(normed(hidden_two) * (1.0 + v.scale_mlp) + v.shift_mlp)
            return hidden_two, act.astype(jnp.bfloat16)

        v.hidden_two, act_three = order.run(finish, v.sum2.crossed)
        v.norm_three = normed(v.hidden_two)
        v.act_three = send_rows(act_three)

    def join3():
        v.act_three = join_rows(v.act_three)

    def sm():
        v.mixed_parts = send_columns(order.hold(v.mixed_flat))

    def jm():
        v.mixed_all = join_columns(v.mixed_parts)

    def sc():
        v.cross_parts = send_columns(order.hold(v.cross_flat))

    def jc():
        v.cross_all = join_columns(v.cross_parts)

    def lay3():
        (v.up_part,) = order.run(
            lambda last: lay_out(
                v.third.pieces[:-1] + [last], v.third.starts(spot, shard_rows), [hidden // PEERS]
            ),
            v.third.pieces[-1],
        )

    def up():
        v.activated, v.slope = order.run(
            lambda a: multiply(a, v.up_part, False, gate_and_slope, (jnp.bfloat16, jnp.bfloat16)),
            v.act_three,
        )

    def lay4():
        (v.down_part,) = order.run(
            lambda last: lay_out(
                v.fourth.pieces[:-1] + [last], v.fourth.starts(spot, shard_rows), [width]
            ),
            v.fourth.pieces[-1],
        )

    def pre():
        v.grad_pre = order.run(
            lambda a: multiply(a, v.down_part, True, scaled, extra=(v.slope, 0)), v.grad_three
        )

    def ring(value):
        halves = [(value, 1, 0), (value, -1, 1)]
        return Scatter(order, halves, group, spot, shard_rows // 2, shard_rows)

    def near3():
        v.sum3 = GroupSum(order, v.grad_pre, v.up_part, True)
        v.sum3.near()

    def dterm():
        v.down_term = order.run(lambda a: weight_term(a, v.grad_three), v.activated)

    def uterm():
        v.up_term = order.run(lambda a: weight_term(a, v.grad_pre), v.act_three)

    def mlp_start():
        v.mlp_ring = Scatter(
            order,
            [(v.down_term, 1, 0), (v.up_term, -1, 0)],
            group,
            spot,
            shard_rows,
            shard_rows,
        )

    def mlp_step():
        if v.mlp_ring.reach():
            v.down_all, v.up_all = [over_ranks(found) for found in v.mlp_ring.sums]

    def over_ranks(found):
        return lax.all_gather(found, "rep", axis=0, tiled=True)

    def fin3():
        def finish(crossed):
            grad_act = own_rows(v.sum3.mine + crossed.astype(jnp.float32))
            grad_two = grad_block + normed_back(v.hidden_two, grad_act * (1.0 + v.scale_mlp))
            return (
                jnp.sum(grad_act, axis=1),
                jnp.sum(grad_act * v.norm_three, axis=1),
                grad_two,
                flatten(grad_two).astype(jnp.bfloat16),
            )

        v.grad_shift_mlp, v.grad_scale_mlp, v.grad_two, grad_merge = order.run(
            finish, v.sum3.crossed
        )
        v.grad_merge = send_rows(grad_merge)

    def join4():
        v.grad_merge = join_rows(v.grad_merge)

    def mm4():
        v.grad_mixed = order.run(lambda a: multiply(a, v.merge_part, True), v.grad_merge)

    def cback():
        v.grad_query, v.grad_keyval = order.run(
            lambda a: attend_cross_back(
                v.cross_queries,
                v.keyval,
                v.length_all,
                v.logsum_cross,
                a,
                all_images,
                heads,
                score_scale,
            ),
            v.grad_mixed,
        )

    def near4():
        v.sum4 = GroupSum(order, v.grad_query, v.query_part, True)
        v.sum4.near()

    def qterm():
        v.cross_term = order.run(
            lambda a: weight_term(a, v.grad_query, first=0, total=4 * part), v.act_two
        )

    def kterm():
        v.cross_term = order.run(
            lambda a, into: weight_term(a, v.grad_keyval, None, into, part, 4 * part),
            v.text_all,
            v.cross_term,
        )

    def mterm():
        v.cross_term = order.run(
            lambda a, into: weight_term(a, v.grad_merge, rank, into, 3 * part, 4 * part),
            v.cross_all,
            v.cross_term,
        )

    def cross_start():
        v.cross_ring = ring(v.cross_term)

    def cross_step():
        if v.cross_ring.reach():
            v.cross_found = over_ranks(jnp.concatenate(v.cross_ring.sums, axis=0))

    def fin4():
        def finish(crossed):
            grad_act = own_rows(v.sum4.mine + crossed.astype(jnp.float32))
            grad_one = v.grad_two + normed_back(v.hidden_one, grad_act * v.gain_full)
            return (
                jnp.sum(grad_act * v.norm_two, axis=1),
                jnp.sum(grad_one * v.branch_one, axis=1),
                grad_one,
                flatten(v.gate_self * grad_one).astype(jnp.bfloat16),
            )

        v.gain_term, v.grad_gate_self, v.grad_one, grad_out = order.run(finish, v.sum4.crossed)
        v.grad_out = send_rows(grad_out)

    def join5():
        v.grad_out = join_rows(v.grad_out)

    def mm5():
        v.grad_mixed = order.run(lambda a: multiply(a, v.out_part, True), v.grad_out)

    def sback():
        v.grad_qkv = order.run(
            lambda a: attend_self_back(
                v.qkv_act, v.logsum_self, a, all_images, heads, score_scale
            ),
            v.grad_mixed,
        )

    def near5():
        v.sum5 = GroupSum(order, v.grad_qkv, v.qkv_part, True)
        v.sum5.near()

    def qkvterm():
        v.self_term = order.run(
            lambda a: weight_term(a, v.grad_qkv, first=0, total=4 * part), v.act_one
        )

    def oterm():
        v.self_term = order.run(
            lambda a, into: weight_term(a, v.grad_out, rank, into, 3 * part, 4 * part),
            v.mixed_all,
            v.self_term,
        )

    def self_start():
        v.self_ring = ring(v.self_term)

    def self_step():
        if v.self_ring.reach():
            own = jnp.concatenate(v.self_ring.sums, axis=0)
            far = swap(own, 2)
            v.self_found = [own, swap(own, 1), far, swap(far, 1)]

    def fin5():
        def finish(crossed):
            grad_act = own_rows(v.sum5.mine + crossed.astype(jnp.float32))
            image_grad = v.grad_one + normed_back(residual, grad_act * (1.0 + v.scale_self))
            return (
                jnp.sum(grad_act, axis=1),
                jnp.sum(grad_act * norm_one, axis=1),
                image_grad.astype(jnp.bfloat16),
            )

        v.grad_shift_self, v.grad_scale_self, v.image_grad = order.run(finish, v.sum5.crossed)

    def near6():
        v.sum6 = GroupSum(order, v.activated, v.down_part, False)
        v.sum6.near()

    def fin6():
        def finish(crossed):
            branch_three = own_rows(v.sum6.mine + crossed.astype(jnp.float32))
            block_out = (v.hidden_two + v.gate_mlp * branch_three).astype(jnp.bfloat16)
            vectors = jnp.concatenate(
                [
                    v.grad_shift_self,
                    v.grad_scale_self,
                    v.grad_gate_self,
                    v.grad_shift_mlp,
                    v.grad_scale_mlp,
                    jnp.sum(grad_block * branch_three, axis=1),
                    v.gain_term,
                ],
                axis=1,
            )
            return block_out, vectors.astype(jnp.bfloat16)

        v.block_out, vectors = order.run(finish, v.sum6.crossed)
        v.everyone = Everyone(order, vectors, group)

    def hop():
        v.everyone.hop()

    def near7():
        v.sum7 = GroupSum(order, v.grad_keyval, v.keyval_part, True)
        v.sum7.near()

    def fin7():
        v.text_grad = order.run(
            lambda crossed: (v.sum7.mine + crossed.astype(jnp.float32))
            .astype(jnp.bfloat16)
            .reshape(text_tokens.shape),
            v.sum7.crossed,
        )

    def down_out():
        v.down_grad = order.run(lambda a: spread_rows(a, width), v.down_all)

    def up_out():
        if aligned:
            v.up_grad = order.run(
                lambda a: spread_blocks(a, 0, group, hidden // (group * PEERS)), v.up_all
            )
        else:
            v.up_grad = (
                v.up_all.reshape(PEERS, shard_rows, group, -1)
                .transpose(1, 2, 0, 3)
                .reshape(shard_rows, hidden)
                .astype(jnp.float32)
            )

    def mod_out():
        while v.everyone.left:
            hop()

        def finish(found):
            return (
                outer_sum(conditions(v.all_steps), found[:, : 6 * width]),
                jnp.sum(
                    lax.dynamic_slice_in_dim(
                        found, 6 * width + member * shard_rows, shard_rows, 1
                    ).astype(jnp.float32),
                    axis=0,
                ),
            )

        v.mod_grad, v.gain_grad = order.run(finish, v.everyone.value)

    def cross_out():
        v.query_grad, v.keyval_grad, v.merge_grad = [
            order.run(lambda a: spread_blocks(a, start, count, part), v.cross_found)
            for start, count in ((0, 1), (1, 2), (3, 1))
        ]

    def self_out():
        v.qkv_grad, v.out_grad = [
            order.run(
                lambda last: spread_peers(
                    v.self_found[:-1] + [last], rank, start, count, part
                ),
                v.self_found[-1],
            )
            for start, count in ((0, 3), (3, 1))
        ]

    work = {
        "A": lambda: order.tick(v.first, v.second),
        "B": lambda: order.tick(v.third, v.fourth),
        "xa": lambda: order.wait(v.act_one[1]),
        "xt": lambda: order.wait(v.text_all[1]),
        "F0": mlp_start,
        "F": mlp_step,
        "C0": cross_start,
        "C": cross_step,
        "S0": self_start,
        "S": self_step,
        "h": hop,
        "self": self_attend,
        "wo": lambda: order.wait(v.out_part),
        "wm": lambda: order.wait(v.merge_part),
        "dout": down_out,
        "uout": up_out,
        "mod": mod_out,
        "cout": cross_out,
        "sout": self_out,
        "x1": lambda: order.wait(v.sum1.crossed),
        "x2": lambda: order.wait(v.sum2.crossed),
        "x3": lambda: order.wait(v.sum3.crossed),
        "x4": lambda: order.wait(v.sum4.crossed),
        "x5": lambda: order.wait(v.sum5.crossed),
        "x6": lambda: order.wait(v.sum6.crossed),
        "y2": lambda: order.wait(v.act_two[1]),
        "y3": lambda: order.wait(v.act_three[1]),
        "y4": lambda: order.wait(v.grad_merge[1]),
        "y5": lambda: order.wait(v.grad_out[1]),
        "rest1": lambda: v.sum1.rest(),
        "rest2": lambda: v.sum2.rest(),
        "rest3": lambda: v.sum3.rest(),
        "rest4": lambda: v.sum4.rest(),
        "rest5": lambda: v.sum5.rest(),
        "rest6": lambda: v.sum6.rest(),
        "rest7": lambda: v.sum7.rest(),
    }
    for step in (
        (p1, p2, p3, p4, a0, ab, r, e, terms, start, ja, st, jt, sg, jg)
        + (lay1, lay2, qkv, kv, near1, fin1, join2, cq, cross, near2, fin2, join3, sm, jm, sc, jc)
        + (lay3, up, lay4, pre, near3, dterm, uterm, fin3, join4, mm4, cback, near4, qterm, kterm)
        + (mterm, fin4, join5, mm5, sback, near5, qkvterm, oterm, fin5, near6, fin6, near7, fin7)
    ):
        work[step.__name__] = step
    for name in PLAN:
        work[name]()
    return (
        v.block_out,
        v.image_grad,
        v.text_grad,
        v.mod_grad,
        v.qkv_grad,
        v.out_grad,
        v.query_grad,
        v.keyval_grad,
        v.merge_grad,
        v.gain_grad,
        v.up_grad,
        v.down_grad,
    )


def solution(mesh):
    placed = (
        P(("rep", "fsdp"), None, None),
        P(("rep", "fsdp"), None, None),
        P(("rep", "fsdp")),
        P(("rep", "fsdp")),
        P(("rep", "fsdp"), None, None),
        P("fsdp", None),
        P("fsdp", None),
        P("fsdp", None),
        P("fsdp", None),
        P("fsdp", None),
        P("fsdp", None),
        P("fsdp"),
        P("fsdp", None),
        P("fsdp", None),
    )
    return jax.shard_map(
        body,
        mesh=mesh,
        in_specs=placed,
        out_specs=(
            P(("rep", "fsdp"), None, None),
            P(("rep", "fsdp"), None, None),
            P(("rep", "fsdp"), None, None),
            P("fsdp", None),
            P("fsdp", None),
            P("fsdp", None),
            P("fsdp", None),
            P("fsdp", None),
            P("fsdp", None),
            P("fsdp"),
            P("fsdp", None),
            P("fsdp", None),
        ),
        check_vma=False,
    )
```

```python
import math

import jax
import jax.numpy as jnp
from jax import lax
from jax.experimental import pallas as pl
from jax.experimental.pallas import tpu as pltpu
from jax.sharding import PartitionSpec as P

HEADS = 16


EPSILON = 1e-06


def matmul(left, right):
    return jnp.dot(left, right, preferred_element_type=jnp.float32)


def outer_sum(left, right):
    return lax.dot_general(
        left, right, (((0,), (0,)), ((), ())), preferred_element_type=jnp.float32
    )


def back_product(left, right):
    return lax.dot_general(
        left, right, (((1,), (1,)), ((), ())), preferred_element_type=jnp.float32
    )


def normed(value):
    return value * lax.rsqrt(jnp.mean(value * value, axis=-1, keepdims=True) + EPSILON)


def normed_back(value, grad):
    return jax.vjp(normed, value)[1](grad)[0]


def smooth_gate(value):
    return jax.nn.gelu(value, approximate=True)


def row_block(rows, columns, column=0):
    return pl.BlockSpec((rows, columns), lambda image, *_: (image, column))


def parts_of(value, count):
    width = value.shape[1] // count
    return [value[:, i * width : (i + 1) * width] for i in range(count)]


def scores_of(queries, keys, limit, scale):
    scores = back_product(queries, keys) * scale
    if limit is not None:
        slot = lax.broadcasted_iota(jnp.int32, scores.shape, 1)
        scores = jnp.where(slot < limit, scores, -jnp.inf)
    return scores


def attend_heads(queries, keys, values, limit, scale, mixed_ref, logsum_ref):
    head_width = keys[0].shape[1]
    for head, (query, key, value) in enumerate(zip(queries, keys, values)):
        scores = scores_of(query, key, limit, scale)
        row_top = jnp.max(scores, axis=1, keepdims=True)
        raised = jnp.exp(scores - row_top)
        totals = jnp.sum(raised, axis=1, keepdims=True)
        weights = (raised / totals).astype(jnp.bfloat16)
        mixed_ref[:, head * head_width : (head + 1) * head_width] = matmul(weights, value).astype(
            jnp.bfloat16
        )
        logsum_ref[:, head : head + 1] = row_top + jnp.log(totals)


def attend_heads_back(queries, keys, values, limit, scale, logsum_ref, grads, outs):
    grad_query_ref, grad_key_ref, grad_value_ref = outs
    for head, (query, key, value, grad) in enumerate(zip(queries, keys, values, grads)):
        scores = scores_of(query, key, limit, scale)
        weights = jnp.exp(scores - logsum_ref[:, head : head + 1])
        grad_weights = back_product(grad, value)
        grad_value_ref(head, outer_sum(weights.astype(jnp.bfloat16), grad))
        inner_sum = jnp.sum(weights * grad_weights, axis=1, keepdims=True)
        grad_scores = (scale * (weights * (grad_weights - inner_sum))).astype(jnp.bfloat16)
        grad_query_ref(head, matmul(grad_scores, key))
        grad_key_ref(head, outer_sum(grad_scores, query))


def head_writer(ref, first, width):
    def write(head, value):
        start = first + head * width
        ref[:, start : start + width] = value.astype(jnp.bfloat16)

    return write


VMEM_LIMIT = 48 * 1024 * 1024


def cost(flops, moved, transcendentals=0):
    return pl.CostEstimate(
        flops=int(flops), bytes_accessed=int(moved), transcendentals=int(transcendentals)
    )


def attention_cost(images, length, slots, heads, width, products):
    pairs = images * heads * length * slots
    return cost(2 * products * pairs * width, 8 * pairs, pairs)


def attend_self(qkv, images, heads, scale):
    rows, columns = qkv.shape
    length, part = rows // images, columns // 3

    def kernel(qkv_ref, mixed_ref, logsum_ref):
        blocks = parts_of(qkv_ref, 3 * heads)
        attend_heads(
            blocks[:heads],
            blocks[heads : 2 * heads],
            blocks[2 * heads :],
            None,
            scale,
            mixed_ref,
            logsum_ref,
        )

    return pl.pallas_call(
        kernel,
        grid=(images,),
        in_specs=[row_block(length, columns)],
        out_specs=[row_block(length, part), row_block(length, heads)],
        out_shape=[
            jax.ShapeDtypeStruct((rows, part), jnp.bfloat16),
            jax.ShapeDtypeStruct((rows, heads), jnp.float32),
        ],
        compiler_params=pltpu.CompilerParams(vmem_limit_bytes=VMEM_LIMIT),
        cost_estimate=attention_cost(images, length, length, heads, part // heads, 2),
        name="attend_self",
    )(qkv)


def attend_self_back(qkv, logsum, grad_mixed, images, heads, scale):
    rows, columns = qkv.shape
    length, part = rows // images, columns // 3

    def kernel(qkv_ref, logsum_ref, grad_ref, out_ref):
        blocks = parts_of(qkv_ref, 3 * heads)
        writers = [head_writer(out_ref, i * part, part // heads) for i in range(3)]
        attend_heads_back(
            blocks[:heads],
            blocks[heads : 2 * heads],
            blocks[2 * heads :],
            None,
            scale,
            logsum_ref,
            parts_of(grad_ref, heads),
            writers,
        )

    return pl.pallas_call(
        kernel,
        grid=(images,),
        in_specs=[row_block(length, columns), row_block(length, heads), row_block(length, part)],
        out_specs=row_block(length, columns),
        out_shape=jax.ShapeDtypeStruct((rows, columns), jnp.bfloat16),
        compiler_params=pltpu.CompilerParams(vmem_limit_bytes=VMEM_LIMIT),
        cost_estimate=attention_cost(images, length, length, heads, part // heads, 5),
        name="attend_self_back",
    )(qkv, logsum, grad_mixed)


def attend_cross(queries, keyval, limits, images, heads, scale):
    rows, part = queries.shape
    length, slots = rows // images, keyval.shape[0] // images

    def kernel(limits_ref, query_ref, keyval_ref, mixed_ref, logsum_ref):
        blocks = parts_of(keyval_ref, 2 * heads)
        attend_heads(
            parts_of(query_ref, heads),
            blocks[:heads],
            blocks[heads:],
            limits_ref[pl.program_id(0)],
            scale,
            mixed_ref,
            logsum_ref,
        )

    return pl.pallas_call(
        kernel,
        grid_spec=pltpu.PrefetchScalarGridSpec(
            num_scalar_prefetch=1,
            grid=(images,),
            in_specs=[row_block(length, part), row_block(slots, 2 * part)],
            out_specs=[row_block(length, part), row_block(length, heads)],
        ),
        out_shape=[
            jax.ShapeDtypeStruct((rows, part), jnp.bfloat16),
            jax.ShapeDtypeStruct((rows, heads), jnp.float32),
        ],
        compiler_params=pltpu.CompilerParams(vmem_limit_bytes=VMEM_LIMIT),
        cost_estimate=attention_cost(images, length, slots, heads, part // heads, 2),
        name="attend_cross",
    )(limits, queries, keyval)


def attend_cross_back(queries, keyval, limits, logsum, grad_mixed, images, heads, scale):
    rows, part = queries.shape
    length, slots = rows // images, keyval.shape[0] // images

    def kernel(limits_ref, query_ref, keyval_ref, logsum_ref, grad_ref, out_ref, text_ref):
        blocks = parts_of(keyval_ref, 2 * heads)
        width = part // heads
        attend_heads_back(
            parts_of(query_ref, heads),
            blocks[:heads],
            blocks[heads:],
            limits_ref[pl.program_id(0)],
            scale,
            logsum_ref,
            parts_of(grad_ref, heads),
            [
                head_writer(out_ref, 0, width),
                head_writer(text_ref, 0, width),
                head_writer(text_ref, part, width),
            ],
        )

    return pl.pallas_call(
        kernel,
        grid_spec=pltpu.PrefetchScalarGridSpec(
            num_scalar_prefetch=1,
            grid=(images,),
            in_specs=[
                row_block(length, part),
                row_block(slots, 2 * part),
                row_block(length, heads),
                row_block(length, part),
            ],
            out_specs=[row_block(length, part), row_block(slots, 2 * part)],
        ),
        out_shape=[
            jax.ShapeDtypeStruct((rows, part), jnp.bfloat16),
            jax.ShapeDtypeStruct((images * slots, 2 * part), jnp.bfloat16),
        ],
        compiler_params=pltpu.CompilerParams(vmem_limit_bytes=VMEM_LIMIT),
        cost_estimate=attention_cost(images, length, slots, heads, part // heads, 5),
        name="attend_cross_back",
    )(limits, queries, keyval, logsum, grad_mixed)


def pick_blocks(weights, counts, rank):
    rows = weights[0].shape[0]
    width = weights[0].shape[1] // (counts[0] * PEERS)
    firsts = [sum(counts[:i]) for i in range(len(counts))]

    def kernel(rank_ref, *refs):
        step = pl.program_id(0)
        out_ref = refs[-1]
        for ref, first, count in zip(refs, firsts, counts):

            @pl.when((step >= first) & (step < first + count))
            def _():
                out_ref[...] = ref[...]

    def spec(first, count):
        return pl.BlockSpec(
            (rows, width),
            lambda step, rank_ref: (
                0,
                jnp.clip(step - first, 0, count - 1) * PEERS + rank_ref[0],
            ),
        )

    return pl.pallas_call(
        kernel,
        grid_spec=pltpu.PrefetchScalarGridSpec(
            num_scalar_prefetch=1,
            grid=(sum(counts),),
            in_specs=[spec(first, count) for first, count in zip(firsts, counts)],
            out_specs=pl.BlockSpec((rows, width), lambda step, rank_ref: (0, step)),
        ),
        out_shape=jax.ShapeDtypeStruct((rows, width * sum(counts)), weights[0].dtype),
        cost_estimate=cost(0, 4 * rows * width * sum(counts)),
        name="pick_blocks",
    )(rank.reshape(1), *weights)


def spread_blocks(found, first, count, width):
    rows = found.shape[0] // PEERS

    def kernel(found_ref, out_ref):
        for peer in range(PEERS):
            out_ref[:, peer * width : (peer + 1) * width] = found_ref[
                peer * rows : (peer + 1) * rows, :
            ].astype(jnp.float32)

    return pl.pallas_call(
        kernel,
        grid=(count,),
        in_specs=[pl.BlockSpec((PEERS * rows, width), lambda block: (0, first + block))],
        out_specs=pl.BlockSpec((rows, PEERS * width), lambda block: (0, block)),
        out_shape=jax.ShapeDtypeStruct((rows, count * PEERS * width), jnp.float32),
        cost_estimate=cost(0, 6 * rows * count * PEERS * width),
        compiler_params=pltpu.CompilerParams(vmem_limit_bytes=VMEM_LIMIT),
        name="spread_blocks",
    )(found)


def spread_peers(found, rank, first, count, width):
    rows = found[0].shape[0]

    def kernel(rank_ref, *refs):
        for peer in range(PEERS):
            for mask in range(PEERS):

                @pl.when((rank_ref[0] ^ mask) == peer)
                def _():
                    refs[-1][:, peer * width : (peer + 1) * width] = refs[mask][...].astype(
                        jnp.float32
                    )

    return pl.pallas_call(
        kernel,
        grid_spec=pltpu.PrefetchScalarGridSpec(
            num_scalar_prefetch=1,
            grid=(count,),
            in_specs=[pl.BlockSpec((rows, width), lambda block, rank_ref: (0, first + block))]
            * PEERS,
            out_specs=pl.BlockSpec((rows, PEERS * width), lambda block, rank_ref: (0, block)),
        ),
        out_shape=jax.ShapeDtypeStruct((rows, count * PEERS * width), jnp.float32),
        cost_estimate=cost(0, 6 * rows * count * PEERS * width),
        compiler_params=pltpu.CompilerParams(vmem_limit_bytes=VMEM_LIMIT),
        name="spread_peers",
    )(rank.reshape(1), *found)


def spread_rows(found, width):
    rows = found.shape[0] // PEERS

    def kernel(found_ref, out_ref):
        out_ref[...] = found_ref[...].astype(jnp.float32)

    return pl.pallas_call(
        kernel,
        grid=(PEERS,),
        in_specs=[pl.BlockSpec((rows, width), lambda peer: (peer, 0))],
        out_specs=pl.BlockSpec((rows, width), lambda peer: (peer, 0)),
        out_shape=jax.ShapeDtypeStruct((PEERS * rows, width), jnp.float32),
        cost_estimate=cost(0, 6 * PEERS * rows * width),
        compiler_params=pltpu.CompilerParams(vmem_limit_bytes=VMEM_LIMIT),
        name="spread_rows",
    )(found)


PEERS = 4


def swap(value, mask):
    return lax.ppermute(value, "rep", [(peer, peer ^ mask) for peer in range(PEERS)])


def stack_rows(parts):
    rows, columns = parts[0].shape
    count = len(parts)

    def kernel(*refs):
        ins, out, held, arrived, left = refs[:count], refs[count], refs[-3], refs[-2], refs[-1]
        fetches = [
            pltpu.make_async_copy(ins[i], held.at[i], arrived.at[i]) for i in range(count)
        ]
        stores = [
            pltpu.make_async_copy(held.at[i], out.at[i * rows : (i + 1) * rows, :], left.at[i])
            for i in range(count)
        ]
        for fetch in fetches:
            fetch.start()
        for fetch, store in zip(fetches, stores):
            fetch.wait()
            store.start()
        for store in stores:
            store.wait()

    return pl.pallas_call(
        kernel,
        in_specs=[pl.BlockSpec(memory_space=pl.ANY)] * count,
        out_specs=pl.BlockSpec(memory_space=pl.ANY),
        out_shape=jax.ShapeDtypeStruct((count * rows, columns), parts[0].dtype),
        scratch_shapes=[
            pltpu.VMEM((count, rows, columns), parts[0].dtype),
            pltpu.SemaphoreType.DMA((count,)),
            pltpu.SemaphoreType.DMA((count,)),
        ],
        cost_estimate=cost(0, 4 * count * rows * columns),
        compiler_params=pltpu.CompilerParams(vmem_limit_bytes=VMEM_LIMIT),
        name="stack_rows",
    )(*parts)


def stack_columns(parts):
    orders = ((0, 1, 2, 3), (2, 3, 0, 1), (1, 0, 3, 2), (3, 2, 1, 0))
    rows, columns = parts[0].shape
    block = rows // PEERS

    def kernel(*refs):
        for i, order in enumerate(orders):

            @pl.when(pl.program_id(0) == i)
            def _():
                for j, source in enumerate(order):
                    refs[-1][j * block : (j + 1) * block, :] = refs[i][
                        source * block : (source + 1) * block, :
                    ]

    return pl.pallas_call(
        kernel,
        grid=(PEERS,),
        in_specs=[pl.BlockSpec((rows, columns), lambda step: (0, 0))] * PEERS,
        out_specs=pl.BlockSpec((rows, columns), lambda step: (0, step)),
        out_shape=jax.ShapeDtypeStruct((rows, PEERS * columns), parts[0].dtype),
        cost_estimate=cost(0, 4 * PEERS * rows * columns),
        compiler_params=pltpu.CompilerParams(vmem_limit_bytes=VMEM_LIMIT),
        name="stack_columns",
    )(*parts)


def narrow(total):
    return (total.astype(jnp.bfloat16),)


def plus(total, extra):
    return (total + extra.astype(jnp.float32),)


def narrow_plus(total, extra):
    return ((total + extra.astype(jnp.float32)).astype(jnp.bfloat16),)


def halves(total):
    rows = total.shape[0] // 2
    return (total[:rows].astype(jnp.bfloat16), total[rows:].astype(jnp.bfloat16))


def scaled(total, factor):
    return ((total * factor.astype(jnp.float32)).astype(jnp.bfloat16),)


def gate_and_slope(total):
    value, back = jax.vjp(smooth_gate, total)
    return (value.astype(jnp.bfloat16), back(jnp.ones_like(total))[0].astype(jnp.bfloat16))


def multiply(
    left, right, turned, finish=narrow, types=(jnp.bfloat16,), first=0, rows=None, extra=None, half=None
):
    rows = left.shape[0] if rows is None else rows
    depth = left.shape[1]
    breadth = right.shape[1] // (1 if half is None else 2)
    columns = right.shape[0] if turned else breadth
    width = min(512, columns)
    skip = 0 if half is None else half * breadth // (depth if turned else width)
    product = back_product if turned else matmul
    tall = rows // 2 if finish is halves else rows

    def kernel(*refs):
        left_ref, right_ref = refs[:2]
        outs = refs[-len(types) :]
        blocks = [ref[...] for ref in refs[2 : -len(types)]]
        for out, value in zip(outs, finish(product(left_ref[...], right_ref[...]), *blocks)):
            out[...] = value

    specs = [
        pl.BlockSpec((rows, depth), lambda step: (first // rows, 0)),
        pl.BlockSpec((width, depth), lambda step: (step, skip))
        if turned
        else pl.BlockSpec((depth, width), lambda step: (0, skip + step)),
    ]
    values = [left, right]
    if extra is not None:
        extra, start = extra
        specs.append(pl.BlockSpec((rows, width), lambda step: (start // rows, step)))
        values.append(extra)
    found = pl.pallas_call(
        kernel,
        grid=(columns // width,),
        in_specs=specs,
        out_specs=[pl.BlockSpec((tall, width), lambda step: (0, step))] * len(types),
        out_shape=[jax.ShapeDtypeStruct((tall, columns), kind) for kind in types],
        cost_estimate=cost(2 * rows * depth * columns, 2 * (rows * depth + depth * columns + rows * columns)),
        compiler_params=pltpu.CompilerParams(vmem_limit_bytes=VMEM_LIMIT),
        name="multiply",
    )(*values)
    return found[0] if len(types) == 1 else found


def weight_term(left, right, rank=None, into=None, first=0, total=None):
    depth, rows = left.shape
    columns = right.shape[1] if rank is None else right.shape[1] // PEERS
    height = min(1024, rows) if rank is None else rows // PEERS
    width = min(512, columns)
    shift = columns // width
    chosen = jnp.zeros((1,), jnp.int32) if rank is None else rank.reshape(1)
    total = columns if total is None else total

    def kernel(chosen_ref, left_ref, right_ref, *refs):
        refs[-1][...] = outer_sum(left_ref[...], right_ref[...]).astype(jnp.bfloat16)

    return pl.pallas_call(
        kernel,
        grid_spec=pltpu.PrefetchScalarGridSpec(
            num_scalar_prefetch=1,
            grid=(columns // width, rows // height),
            in_specs=[
                pl.BlockSpec(
                    (depth, height),
                    lambda j, i, chosen_ref: (0, i if rank is None else i ^ chosen_ref[0]),
                ),
                pl.BlockSpec(
                    (depth, width), lambda j, i, chosen_ref: (0, chosen_ref[0] * shift + j)
                ),
            ]
            + [pl.BlockSpec(memory_space=pl.ANY)] * (into is not None),
            out_specs=pl.BlockSpec(
                (height, width), lambda j, i, chosen_ref: (i, first // width + j)
            ),
        ),
        out_shape=jax.ShapeDtypeStruct((rows, total), jnp.bfloat16),
        input_output_aliases={} if into is None else {3: 0},
        cost_estimate=cost(
            2 * rows * depth * columns, 2 * (rows * depth + depth * columns + rows * columns)
        ),
        compiler_params=pltpu.CompilerParams(vmem_limit_bytes=VMEM_LIMIT),
        name="weight_term",
    )(chosen, left, right, *([] if into is None else [into]))


def multiply_rest(left, right, turned, got):
    (rows, columns), depth = got[0].shape, left.shape[1]
    width = min(512, columns)
    product = back_product if turned else matmul

    def kernel(left_ref, right_ref, got_ref, got_far_ref, own_ref, far_ref):
        total = product(left_ref[...], right_ref[...])
        own_ref[...] = total[:rows] + got_ref[...].astype(jnp.float32)
        far_ref[...] = (total[rows:] + got_far_ref[...].astype(jnp.float32)).astype(jnp.bfloat16)

    return pl.pallas_call(
        kernel,
        grid=(columns // width,),
        in_specs=[
            pl.BlockSpec((2 * rows, depth), lambda step: (0, 0)),
            pl.BlockSpec((width, depth), lambda step: (step, 0))
            if turned
            else pl.BlockSpec((depth, width), lambda step: (0, step)),
        ]
        + [pl.BlockSpec((rows, width), lambda step: (0, step))] * 2,
        out_specs=[pl.BlockSpec((rows, width), lambda step: (0, step))] * 2,
        out_shape=[
            jax.ShapeDtypeStruct((rows, columns), jnp.float32),
            jax.ShapeDtypeStruct((rows, columns), jnp.bfloat16),
        ],
        cost_estimate=cost(
            4 * rows * depth * columns, 2 * (2 * rows * depth + depth * columns + 5 * rows * columns)
        ),
        compiler_params=pltpu.CompilerParams(vmem_limit_bytes=VMEM_LIMIT),
        name="multiply_rest",
    )(left, right, *got)


class Order:
    def __init__(self):
        self.token = ()

    def run(self, work, first, *others):
        if self.token:
            first = after(first, self.token)
        found = work(first, *others)
        self.token = tuple(jax.tree.leaves(found))
        return found

    def hold(self, value):
        return after(value, self.token)

    def tick(self, *rings):
        heads = [ring.pieces[-1] for ring in rings]
        after_work = after(heads, self.token)
        for ring, head in zip(rings, after_work):
            ring.pieces[-1] = head
            if ring.sevenths < 7:
                ring.send()
        self.wait(*heads)

    def wait(self, *values):
        self.token = self.token + tuple(jax.tree.leaves(values))


class State:
    pass


class GroupSum:
    def __init__(self, order, left, right, turned, half=None):
        self.order, self.left, self.right, self.turned = order, left, right, turned
        self.half = half
        self.rows = left.shape[0] // PEERS

    def near(self):
        rows = self.rows
        sent = self.order.run(
            lambda left: multiply(
                left,
                self.right,
                self.turned,
                halves,
                (jnp.bfloat16, jnp.bfloat16),
                first=2 * rows,
                rows=2 * rows,
            ),
            self.left,
        )
        self.got = [swap(part, 1) for part in sent]

    def rest(self):
        self.mine, self.sent = self.order.run(
            lambda left: multiply_rest(left, self.right, self.turned, self.got), self.left
        )
        self.crossed = swap(self.sent, 2)

    def send(self):
        self.near()
        self.rest()
        return self

def ring_member(place, size):
    place = place % size
    return jnp.where(place < size // 2, 2 * place, 2 * (size - 1 - place) + 1)


def ring_pairs(size, step):
    order = [2 * i for i in range(size // 2)] + [2 * i + 1 for i in reversed(range(size // 2))]
    return [(order[i], order[(i + step) % size]) for i in range(size)]


def after(value, earlier):
    return lax.optimization_barrier((value, earlier))[0]


class Gather:
    def __init__(self, value, size, step):
        self.size, self.step, self.pieces = size, step, [value]
        self.sevenths = 0

    def send(self):
        self.sevenths += 1
        while len(self.pieces) - 1 < self.sevenths * (self.size - 1) // 7:
            self.pieces.append(
                lax.ppermute(self.pieces[-1], "fsdp", ring_pairs(self.size, self.step))
            )

    def starts(self, place, rows):
        return jnp.stack(
            [ring_member(place - self.step * k, self.size) * rows for k in range(self.size)]
        ).astype(jnp.int32)


def lay_out(pieces, starts, widths):
    size = len(pieces)
    rows = pieces[0].shape[0]
    count = len(widths)
    edges = [sum(widths[:i]) for i in range(count)]

    def kernel(starts_ref, *refs):
        shards, outs, done = refs[:size], refs[size:-1], refs[-1]
        copies = []
        for i, shard in enumerate(shards):
            start = pl.multiple_of(starts_ref[i], rows)
            for j, out in enumerate(outs):
                copies.append(
                    pltpu.make_async_copy(
                        shard.at[:, edges[j] : edges[j] + widths[j]],
                        out.at[pl.ds(start, rows), :],
                        done.at[i, j],
                    )
                )
        for copy in copies:
            copy.start()
        for copy in copies:
            copy.wait()

    return pl.pallas_call(
        kernel,
        out_shape=[jax.ShapeDtypeStruct((size * rows, w), pieces[0].dtype) for w in widths],
        in_specs=[pl.BlockSpec(memory_space=pltpu.SMEM)]
        + [pl.BlockSpec(memory_space=pltpu.VMEM)] * size,
        out_specs=[pl.BlockSpec(memory_space=pl.ANY)] * count,
        scratch_shapes=[pltpu.SemaphoreType.DMA((size, count))],
        compiler_params=pltpu.CompilerParams(vmem_limit_bytes=VMEM_LIMIT),
        cost_estimate=cost(0, 4 * size * rows * sum(widths)),
        name="lay_out",
    )(starts, *pieces)


def ring_add(values, spots, rows, got):
    count = len(values)
    columns = values[0].shape[1]
    width = min(1024, columns)

    def kernel(spots_ref, *refs):
        for i in range(count):
            block = refs[i][...]
            refs[-count + i][...] = block if got is None else refs[count + i][...] + block

    def spec(i):
        return pl.BlockSpec((rows, width), lambda step, spots_ref: (spots_ref[i], step))

    plain = [pl.BlockSpec((rows, width), lambda step, spots_ref: (0, step))] * count
    arrived = [] if got is None else list(got)
    return pl.pallas_call(
        kernel,
        grid_spec=pltpu.PrefetchScalarGridSpec(
            num_scalar_prefetch=1,
            grid=(columns // width,),
            in_specs=[spec(i) for i in range(count)] + plain[: len(arrived)],
            out_specs=plain,
        ),
        out_shape=[jax.ShapeDtypeStruct((rows, columns), jnp.bfloat16)] * count,
        cost_estimate=cost(rows * columns * count, 6 * rows * columns * count),
        compiler_params=pltpu.CompilerParams(vmem_limit_bytes=VMEM_LIMIT),
        name="ring_add",
    )(spots, *values, *arrived)


class Scatter:
    def __init__(self, order, entries, size, place, rows, shard_rows):
        self.order, self.entries = order, entries
        self.size, self.place, self.rows, self.step = size, place, rows, 0
        self.sevenths, self.blocks = 0, shard_rows // rows
        self.values = [value for value, _, _ in entries]
        self.sums = order.run(
            lambda first: ring_add([first] + self.values[1:], self.spots(), self.rows, None),
            self.values[0],
        )

    def spots(self):
        return jnp.stack(
            [
                ring_member(self.place - direction * (self.step + 1), self.size) * self.blocks
                + block
                for _, direction, block in self.entries
            ]
        ).astype(jnp.int32)

    def reach(self):
        self.sevenths += 1
        while self.step < self.sevenths * (self.size - 1) // 7:
            self.step += 1
            arrived = [
                lax.ppermute(value, "fsdp", ring_pairs(self.size, direction))
                for value, (_, direction, _) in zip(self.sums, self.entries)
            ]
            spots = self.spots()
            self.sums = self.order.run(
                lambda got: ring_add(self.values, spots, self.rows, got), arrived
            )
        return self.sevenths == 7


class Exchange:
    def __init__(self, order, value, size):
        self.order, self.value, self.size, self.mask = order, value[None], size, 1
        self.send()

    def send(self):
        pairs = [(i, i ^ self.mask) for i in range(self.size)]
        self.got = lax.ppermute(self.value, "fsdp", pairs)

    def hop(self):
        low = (lax.axis_index("fsdp") & self.mask) == 0

        def join(got):
            return jnp.concatenate(
                [jnp.where(low, self.value, got), jnp.where(low, got, self.value)], axis=0
            )

        self.value = self.order.run(join, self.got)
        self.mask *= 2
        if self.mask < self.size:
            self.send()


class Everyone:
    def __init__(self, order, value, size):
        self.order, self.value = order, value
        self.hops = [("fsdp", size // 2 >> i, size) for i in range(size.bit_length() - 1)]
        self.hops += [("rep", 2, PEERS), ("rep", 1, PEERS)]
        self.left = len(self.hops)
        self.send()

    def send(self):
        axis, mask, size = self.hops.pop(0)
        self.got = lax.ppermute(self.value, axis, [(i, i ^ mask) for i in range(size)])

    def hop(self):
        if self.left:
            self.value = self.order.run(
                lambda got: jnp.concatenate([self.value, got], axis=0), self.got
            )
            self.left -= 1
            if self.hops:
                self.send()


PLAN = (
    "p1", "p2", "a0", "r", "p3", "p4", "A", "e", "A", "e", "A", "e", "terms", "A", "start", "xa",
    "A", "ja", "st", "xt", "A", "jt", "sg", "A", "ab", "lay1", "qkv", "lay2", "B", "kv", "self",
    "wo", "near1", "rest1", "B", "wm", "B", "x1", "fin1", "B", "y2", "join2", "sm", "cq", "cross",
    "near2", "B", "rest2", "B", "x2", "fin2", "B", "y3", "join3", "sc", "lay3", "up", "jg",
    "lay4", "pre", "near3", "rest3", "dterm", "uterm", "F0", "x3", "fin3", "jc", "near6", "F",
    "y4", "join4", "mm4", "cback", "near4", "F", "rest4", "qterm", "kterm", "mterm", "C0", "F",
    "x4", "fin4", "near7", "C", "F", "y5", "join5", "mm5", "sback", "near5", "F", "C", "rest5",
    "qkvterm", "jm", "oterm", "S0", "F", "C", "x5", "fin5", "rest6", "S", "C", "F", "S", "C",
    "x6", "fin6", "S", "C", "h", "S", "C", "h", "rest7", "S", "h", "dout", "S", "h", "fin7",
    "uout", "S", "h", "mod", "cout", "sout",
)


def body(
    image_tokens,
    text_tokens,
    text_lengths,
    timesteps,
    cotangent,
    mod_weight,
    qkv_weight,
    out_weight,
    query_weight,
    keyval_weight,
    merge_weight,
    cross_gain,
    up_weight,
    down_weight,
):
    images, length, width = image_tokens.shape
    text_count, text_width = text_tokens.shape[1:]
    group = lax.axis_size("fsdp")
    rank = lax.axis_index("rep")
    member = lax.axis_index("fsdp")
    heads = HEADS // PEERS
    head_width = width // HEADS
    part = width // PEERS
    score_scale = head_width ** (-0.5)
    shard_rows = mod_weight.shape[0]
    hidden = up_weight.shape[1]
    rows = images * length
    all_images = PEERS * images

    def own_part(value, blocks):
        count = value.shape[1] // (blocks * PEERS)
        return lax.dynamic_index_in_dim(
            value.reshape(value.shape[0], blocks, PEERS, count), rank, 2, keepdims=False
        ).reshape(value.shape[0], blocks * count)

    def ordered(found):
        stacked = jnp.stack(found)
        return [
            lax.dynamic_index_in_dim(stacked, rank ^ place, 0, keepdims=False)
            for place in range(PEERS)
        ]

    def columns_to_rows(value):
        blocks = value.reshape(PEERS, part, -1)
        found = [
            lax.dynamic_index_in_dim(blocks, rank ^ mask, 0, keepdims=False)
            for mask in range(PEERS)
        ]
        found = [found[0]] + [swap(found[mask], mask) for mask in range(1, PEERS)]
        return jnp.concatenate(ordered(found), axis=1)

    order = Order()
    aligned = hidden // (group * PEERS) % 128 == 0
    spot = jnp.where(member % 2 == 0, member // 2, group - 1 - member // 2)
    def flatten(value):
        return value.reshape(-1, value.shape[-1])

    def own_rows(value):
        return value.reshape(images, length, width)

    half_width = width // 2
    column = member * shard_rows + jnp.arange(shard_rows, dtype=jnp.int32)
    place = jnp.where(column < half_width, column, column - half_width)
    frequency = jnp.exp(-math.log(10000.0) * place.astype(jnp.float32) / half_width)

    def conditions(steps):
        angles = steps.astype(jnp.float32)[:, None] * frequency[None, :]
        return jnp.where(column < half_width, jnp.sin(angles), jnp.cos(angles)).astype(
            jnp.bfloat16
        )

    residual = image_tokens.astype(jnp.float32)
    grad_block = cotangent.astype(jnp.float32)
    norm_one = normed(residual)

    def send_rows(value):
        return [value, swap(value, 2), swap(value, 1)]

    def join_rows(parts):
        far = order.hold(parts[1])
        return order.run(
            lambda last: stack_rows([parts[0], far, parts[2], last]), swap(far, 1)
        )

    def send_columns(value):
        return [value, swap(value, 1), swap(value, 2)]

    def join_columns(parts):
        far = order.hold(parts[2])
        return order.run(
            lambda last: stack_columns([parts[0], parts[1], far, last]), swap(far, 1)
        )

    v = State()
    mine = jnp.concatenate([timesteps, text_lengths]).astype(jnp.float32)
    mine = [mine, swap(mine, 2), swap(mine, 1)]

    def p1():
        v.pick1 = order.run(lambda w: pick_blocks([w, out_weight], [3, 1], rank), qkv_weight)

    def p2():
        v.pick2 = order.run(
            lambda w: pick_blocks([w, keyval_weight, merge_weight], [1, 2, 1], rank),
            query_weight,
        )

    def p3():
        v.pick3 = order.run(
            lambda w: pick_blocks([w], [group], rank) if aligned else own_part(w, group),
            up_weight,
        )

    def p4():
        v.pick4 = order.run(
            lambda w: lax.dynamic_index_in_dim(
                w.reshape(PEERS, -1, width), rank, 0, keepdims=False
            ),
            down_weight,
        )

    def a0():
        v.first, v.second = Gather(v.pick1, group, 1), Gather(v.pick2, group, -1)
        order.tick(v.first, v.second)

    def ab():
        v.third, v.fourth = Gather(v.pick3, group, 1), Gather(v.pick4, group, -1)
        order.tick(v.first, v.second, v.third, v.fourth)

    def r():
        far = order.hold(mine[1])
        found = order.run(
            lambda last: jnp.stack([mine[0], far, mine[2], last]), swap(far, 1)
        )
        v.length_all = found[:, images:].reshape(-1).astype(jnp.int32)
        v.exchange = Exchange(
            order,
            jnp.concatenate([found[:, :images].reshape(-1), cross_gain.astype(jnp.float32)]),
            group,
        )

    def e():
        v.exchange.hop()

    def terms():
        while v.exchange.mask < group:
            e()
        small = v.exchange.value
        v.gain_full = small[:, all_images:].reshape(-1)
        sequence = [0]
        while len(sequence) < group:
            sequence += [index + group // (2 * len(sequence)) for index in sequence]
        steps = small[:, :all_images][member ^ jnp.array(sequence, dtype=jnp.int32)]
        v.all_steps = steps.reshape(group, PEERS, images).transpose(1, 0, 2).reshape(-1)
        found = order.run(
            lambda steps: matmul(conditions(steps), mod_weight), small[:, :images].reshape(-1)
        )
        v.terms = lax.all_to_all(
            found.reshape(group, images, -1), "fsdp", split_axis=0, concat_axis=0, tiled=True
        )

    def start():
        def work(found):
            pieces = jnp.sum(found, axis=0).reshape(images, 6, 1, width)
            act = flatten(normed(residual) * (1.0 + pieces[:, 1]) + pieces[:, 0])
            grad_three = flatten(pieces[:, 5] * grad_block)
            return pieces, act.astype(jnp.bfloat16), grad_three.astype(jnp.bfloat16)

        pieces, act_one, v.grad_three = order.run(work, v.terms)
        v.shift_self, v.scale_self, v.gate_self = (pieces[:, 0], pieces[:, 1], pieces[:, 2])
        v.shift_mlp, v.scale_mlp, v.gate_mlp = (pieces[:, 3], pieces[:, 4], pieces[:, 5])
        v.act_one = send_rows(act_one)

    def ja():
        v.act_one = join_rows(v.act_one)

    def st():
        v.text_all = send_rows(order.hold(flatten(text_tokens)))

    def jt():
        v.text_all = join_rows(v.text_all)

    def sg():
        v.grad_three = send_rows(order.hold(v.grad_three))

    def jg():
        v.grad_three = join_rows(v.grad_three)

    def lay1():
        v.qkv_part, out_part = order.run(
            lambda last: lay_out(
                v.first.pieces[:-1] + [last], v.first.starts(spot, shard_rows), [3 * part, part]
            ),
            v.first.pieces[-1],
        )
        v.out_part = columns_to_rows(out_part)

    def lay2():
        v.query_part, v.keyval_part, merge_part = order.run(
            lambda last: lay_out(
                v.second.pieces[:-1] + [last],
                v.second.starts(spot, shard_rows),
                [part, 2 * part, part],
            ),
            v.second.pieces[-1],
        )
        v.merge_part = columns_to_rows(merge_part)

    def qkv():
        v.qkv_act = order.run(lambda a: multiply(a, v.qkv_part, False), v.act_one)

    def kv():
        v.keyval = order.run(lambda a: multiply(a, v.keyval_part, False), v.text_all)

    def self_attend():
        v.mixed_flat, v.logsum_self = order.run(
            lambda a: attend_self(a, all_images, heads, score_scale), v.qkv_act
        )

    def near1():
        v.sum1 = GroupSum(order, v.mixed_flat, v.out_part, False)
        v.sum1.near()

    def fin1():
        def finish(crossed):
            branch_one = own_rows(v.sum1.mine + crossed.astype(jnp.float32))
            hidden_one = residual + v.gate_self * branch_one
            return (
                branch_one,
                hidden_one,
                flatten(normed(hidden_one) * v.gain_full).astype(jnp.bfloat16),
            )

        v.branch_one, v.hidden_one, act_two = order.run(finish, v.sum1.crossed)
        v.norm_two = normed(v.hidden_one)
        v.act_two = send_rows(act_two)

    def join2():
        v.act_two = join_rows(v.act_two)

    def cq():
        v.cross_queries = order.run(lambda a: multiply(a, v.query_part, False), v.act_two)

    def cross():
        v.cross_flat, v.logsum_cross = order.run(
            lambda a: attend_cross(a, v.keyval, v.length_all, all_images, heads, score_scale),
            v.cross_queries,
        )

    def near2():
        v.sum2 = GroupSum(order, v.cross_flat, v.merge_part, False)
        v.sum2.near()

    def fin2():
        def finish(crossed):
            hidden_two = v.hidden_one + own_rows(v.sum2.mine + crossed.astype(jnp.float32))
            act = flatten(normed(hidden_two) * (1.0 + v.scale_mlp) + v.shift_mlp)
            return hidden_two, act.astype(jnp.bfloat16)

        v.hidden_two, act_three = order.run(finish, v.sum2.crossed)
        v.norm_three = normed(v.hidden_two)
        v.act_three = send_rows(act_three)

    def join3():
        v.act_three = join_rows(v.act_three)

    def sm():
        v.mixed_parts = send_columns(order.hold(v.mixed_flat))

    def jm():
        v.mixed_all = join_columns(v.mixed_parts)

    def sc():
        v.cross_parts = send_columns(order.hold(v.cross_flat))

    def jc():
        v.cross_all = join_columns(v.cross_parts)

    def lay3():
        (v.up_part,) = order.run(
            lambda last: lay_out(
                v.third.pieces[:-1] + [last], v.third.starts(spot, shard_rows), [hidden // PEERS]
            ),
            v.third.pieces[-1],
        )

    def up():
        v.activated, v.slope = order.run(
            lambda a: multiply(a, v.up_part, False, gate_and_slope, (jnp.bfloat16, jnp.bfloat16)),
            v.act_three,
        )

    def lay4():
        (v.down_part,) = order.run(
            lambda last: lay_out(
                v.fourth.pieces[:-1] + [last], v.fourth.starts(spot, shard_rows), [width]
            ),
            v.fourth.pieces[-1],
        )

    def pre():
        v.grad_pre = order.run(
            lambda a: multiply(a, v.down_part, True, scaled, extra=(v.slope, 0)), v.grad_three
        )

    def ring(value):
        halves = [(value, 1, 0), (value, -1, 1)]
        return Scatter(order, halves, group, spot, shard_rows // 2, shard_rows)

    def near3():
        v.sum3 = GroupSum(order, v.grad_pre, v.up_part, True)
        v.sum3.near()

    def dterm():
        v.down_term = order.run(lambda a: weight_term(a, v.grad_three), v.activated)

    def uterm():
        v.up_term = order.run(lambda a: weight_term(a, v.grad_pre), v.act_three)

    def mlp_start():
        v.mlp_ring = Scatter(
            order,
            [(v.down_term, 1, 0), (v.up_term, -1, 0)],
            group,
            spot,
            shard_rows,
            shard_rows,
        )

    def mlp_step():
        if v.mlp_ring.reach():
            v.down_all, v.up_all = [over_ranks(found) for found in v.mlp_ring.sums]

    def over_ranks(found):
        return lax.all_gather(found, "rep", axis=0, tiled=True)

    def fin3():
        def finish(crossed):
            grad_act = own_rows(v.sum3.mine + crossed.astype(jnp.float32))
            grad_two = grad_block + normed_back(v.hidden_two, grad_act * (1.0 + v.scale_mlp))
            return (
                jnp.sum(grad_act, axis=1),
                jnp.sum(grad_act * v.norm_three, axis=1),
                grad_two,
                flatten(grad_two).astype(jnp.bfloat16),
            )

        v.grad_shift_mlp, v.grad_scale_mlp, v.grad_two, grad_merge = order.run(
            finish, v.sum3.crossed
        )
        v.grad_merge = send_rows(grad_merge)

    def join4():
        v.grad_merge = join_rows(v.grad_merge)

    def mm4():
        v.grad_mixed = order.run(lambda a: multiply(a, v.merge_part, True), v.grad_merge)

    def cback():
        v.grad_query, v.grad_keyval = order.run(
            lambda a: attend_cross_back(
                v.cross_queries,
                v.keyval,
                v.length_all,
                v.logsum_cross,
                a,
                all_images,
                heads,
                score_scale,
            ),
            v.grad_mixed,
        )

    def near4():
        v.sum4 = GroupSum(order, v.grad_query, v.query_part, True)
        v.sum4.near()

    def qterm():
        v.cross_term = order.run(
            lambda a: weight_term(a, v.grad_query, first=0, total=4 * part), v.act_two
        )

    def kterm():
        v.cross_term = order.run(
            lambda a, into: weight_term(a, v.grad_keyval, None, into, part, 4 * part),
            v.text_all,
            v.cross_term,
        )

    def mterm():
        v.cross_term = order.run(
            lambda a, into: weight_term(a, v.grad_merge, rank, into, 3 * part, 4 * part),
            v.cross_all,
            v.cross_term,
        )

    def cross_start():
        v.cross_ring = ring(v.cross_term)

    def cross_step():
        if v.cross_ring.reach():
            v.cross_found = over_ranks(jnp.concatenate(v.cross_ring.sums, axis=0))

    def fin4():
        def finish(crossed):
            grad_act = own_rows(v.sum4.mine + crossed.astype(jnp.float32))
            grad_one = v.grad_two + normed_back(v.hidden_one, grad_act * v.gain_full)
            return (
                jnp.sum(grad_act * v.norm_two, axis=1),
                jnp.sum(grad_one * v.branch_one, axis=1),
                grad_one,
                flatten(v.gate_self * grad_one).astype(jnp.bfloat16),
            )

        v.gain_term, v.grad_gate_self, v.grad_one, grad_out = order.run(finish, v.sum4.crossed)
        v.grad_out = send_rows(grad_out)

    def join5():
        v.grad_out = join_rows(v.grad_out)

    def mm5():
        v.grad_mixed = order.run(lambda a: multiply(a, v.out_part, True), v.grad_out)

    def sback():
        v.grad_qkv = order.run(
            lambda a: attend_self_back(
                v.qkv_act, v.logsum_self, a, all_images, heads, score_scale
            ),
            v.grad_mixed,
        )

    def near5():
        v.sum5 = GroupSum(order, v.grad_qkv, v.qkv_part, True)
        v.sum5.near()

    def qkvterm():
        v.self_term = order.run(
            lambda a: weight_term(a, v.grad_qkv, first=0, total=4 * part), v.act_one
        )

    def oterm():
        v.self_term = order.run(
            lambda a, into: weight_term(a, v.grad_out, rank, into, 3 * part, 4 * part),
            v.mixed_all,
            v.self_term,
        )

    def self_start():
        v.self_ring = ring(v.self_term)

    def self_step():
        if v.self_ring.reach():
            own = jnp.concatenate(v.self_ring.sums, axis=0)
            far = swap(own, 2)
            v.self_found = [own, swap(own, 1), far, swap(far, 1)]

    def fin5():
        def finish(crossed):
            grad_act = own_rows(v.sum5.mine + crossed.astype(jnp.float32))
            image_grad = v.grad_one + normed_back(residual, grad_act * (1.0 + v.scale_self))
            return (
                jnp.sum(grad_act, axis=1),
                jnp.sum(grad_act * norm_one, axis=1),
                image_grad.astype(jnp.bfloat16),
            )

        v.grad_shift_self, v.grad_scale_self, v.image_grad = order.run(finish, v.sum5.crossed)

    def near6():
        v.sum6 = GroupSum(order, v.activated, v.down_part, False)
        v.sum6.near()

    def fin6():
        def finish(crossed):
            branch_three = own_rows(v.sum6.mine + crossed.astype(jnp.float32))
            block_out = (v.hidden_two + v.gate_mlp * branch_three).astype(jnp.bfloat16)
            vectors = jnp.concatenate(
                [
                    v.grad_shift_self,
                    v.grad_scale_self,
                    v.grad_gate_self,
                    v.grad_shift_mlp,
                    v.grad_scale_mlp,
                    jnp.sum(grad_block * branch_three, axis=1),
                    v.gain_term,
                ],
                axis=1,
            )
            return block_out, vectors.astype(jnp.bfloat16)

        v.block_out, vectors = order.run(finish, v.sum6.crossed)
        v.everyone = Everyone(order, vectors, group)

    def hop():
        v.everyone.hop()

    def near7():
        v.sum7 = GroupSum(order, v.grad_keyval, v.keyval_part, True)
        v.sum7.near()

    def fin7():
        v.text_grad = order.run(
            lambda crossed: (v.sum7.mine + crossed.astype(jnp.float32))
            .astype(jnp.bfloat16)
            .reshape(text_tokens.shape),
            v.sum7.crossed,
        )

    def down_out():
        v.down_grad = order.run(lambda a: spread_rows(a, width), v.down_all)

    def up_out():
        if aligned:
            v.up_grad = order.run(
                lambda a: spread_blocks(a, 0, group, hidden // (group * PEERS)), v.up_all
            )
        else:
            v.up_grad = (
                v.up_all.reshape(PEERS, shard_rows, group, -1)
                .transpose(1, 2, 0, 3)
                .reshape(shard_rows, hidden)
                .astype(jnp.float32)
            )

    def mod_out():
        while v.everyone.left:
            hop()

        def finish(found):
            return (
                outer_sum(conditions(v.all_steps), found[:, : 6 * width]),
                jnp.sum(
                    lax.dynamic_slice_in_dim(
                        found, 6 * width + member * shard_rows, shard_rows, 1
                    ).astype(jnp.float32),
                    axis=0,
                ),
            )

        v.mod_grad, v.gain_grad = order.run(finish, v.everyone.value)

    def cross_out():
        v.query_grad, v.keyval_grad, v.merge_grad = [
            order.run(lambda a: spread_blocks(a, start, count, part), v.cross_found)
            for start, count in ((0, 1), (1, 2), (3, 1))
        ]

    def self_out():
        v.qkv_grad, v.out_grad = [
            order.run(
                lambda last: spread_peers(
                    v.self_found[:-1] + [last], rank, start, count, part
                ),
                v.self_found[-1],
            )
            for start, count in ((0, 3), (3, 1))
        ]

    work = {
        "A": lambda: order.tick(v.first, v.second),
        "B": lambda: order.tick(v.third, v.fourth),
        "xa": lambda: order.wait(v.act_one[1]),
        "xt": lambda: order.wait(v.text_all[1]),
        "F0": mlp_start,
        "F": mlp_step,
        "C0": cross_start,
        "C": cross_step,
        "S0": self_start,
        "S": self_step,
        "h": hop,
        "self": self_attend,
        "wo": lambda: order.wait(v.out_part),
        "wm": lambda: order.wait(v.merge_part),
        "dout": down_out,
        "uout": up_out,
        "mod": mod_out,
        "cout": cross_out,
        "sout": self_out,
        "x1": lambda: order.wait(v.sum1.crossed),
        "x2": lambda: order.wait(v.sum2.crossed),
        "x3": lambda: order.wait(v.sum3.crossed),
        "x4": lambda: order.wait(v.sum4.crossed),
        "x5": lambda: order.wait(v.sum5.crossed),
        "x6": lambda: order.wait(v.sum6.crossed),
        "y2": lambda: order.wait(v.act_two[1]),
        "y3": lambda: order.wait(v.act_three[1]),
        "y4": lambda: order.wait(v.grad_merge[1]),
        "y5": lambda: order.wait(v.grad_out[1]),
        "rest1": lambda: v.sum1.rest(),
        "rest2": lambda: v.sum2.rest(),
        "rest3": lambda: v.sum3.rest(),
        "rest4": lambda: v.sum4.rest(),
        "rest5": lambda: v.sum5.rest(),
        "rest6": lambda: v.sum6.rest(),
        "rest7": lambda: v.sum7.rest(),
    }
    for step in (
        (p1, p2, p3, p4, a0, ab, r, e, terms, start, ja, st, jt, sg, jg)
        + (lay1, lay2, qkv, kv, near1, fin1, join2, cq, cross, near2, fin2, join3, sm, jm, sc, jc)
        + (lay3, up, lay4, pre, near3, dterm, uterm, fin3, join4, mm4, cback, near4, qterm, kterm)
        + (mterm, fin4, join5, mm5, sback, near5, qkvterm, oterm, fin5, near6, fin6, near7, fin7)
    ):
        work[step.__name__] = step
    for name in PLAN:
        work[name]()
    return (
        v.block_out,
        v.image_grad,
        v.text_grad,
        v.mod_grad,
        v.qkv_grad,
        v.out_grad,
        v.query_grad,
        v.keyval_grad,
        v.merge_grad,
        v.gain_grad,
        v.up_grad,
        v.down_grad,
    )


def solution(mesh):
    placed = (
        P(("rep", "fsdp"), None, None),
        P(("rep", "fsdp"), None, None),
        P(("rep", "fsdp")),
        P(("rep", "fsdp")),
        P(("rep", "fsdp"), None, None),
        P("fsdp", None),
        P("fsdp", None),
        P("fsdp", None),
        P("fsdp", None),
        P("fsdp", None),
        P("fsdp", None),
        P("fsdp"),
        P("fsdp", None),
        P("fsdp", None),
    )
    return jax.shard_map(
        body,
        mesh=mesh,
        in_specs=placed,
        out_specs=(
            P(("rep", "fsdp"), None, None),
            P(("rep", "fsdp"), None, None),
            P(("rep", "fsdp"), None, None),
            P("fsdp", None),
            P("fsdp", None),
            P("fsdp", None),
            P("fsdp", None),
            P("fsdp", None),
            P("fsdp", None),
            P("fsdp"),
            P("fsdp", None),
            P("fsdp", None),
        ),
        check_vma=False,
    )
```

```python
import math

import jax
import jax.numpy as jnp
from jax import lax
from jax.experimental import pallas as pl
from jax.experimental.pallas import tpu as pltpu
from jax.sharding import PartitionSpec as P

HEADS = 16


EPSILON = 1e-06


def matmul(left, right):
    return jnp.dot(left, right, preferred_element_type=jnp.float32)


def outer_sum(left, right):
    return lax.dot_general(
        left, right, (((0,), (0,)), ((), ())), preferred_element_type=jnp.float32
    )


def back_product(left, right):
    return lax.dot_general(
        left, right, (((1,), (1,)), ((), ())), preferred_element_type=jnp.float32
    )


def normed(value):
    return value * lax.rsqrt(jnp.mean(value * value, axis=-1, keepdims=True) + EPSILON)


def normed_back(value, grad):
    return jax.vjp(normed, value)[1](grad)[0]


def smooth_gate(value):
    return jax.nn.gelu(value, approximate=True)


def row_block(rows, columns, column=0):
    return pl.BlockSpec((rows, columns), lambda image, *_: (image, column))


def parts_of(value, count):
    width = value.shape[1] // count
    return [value[:, i * width : (i + 1) * width] for i in range(count)]


def scores_of(queries, keys, limit, scale):
    scores = back_product(queries, keys) * scale
    if limit is not None:
        slot = lax.broadcasted_iota(jnp.int32, scores.shape, 1)
        scores = jnp.where(slot < limit, scores, -jnp.inf)
    return scores


def attend_heads(queries, keys, values, limit, scale, mixed_ref, logsum_ref):
    head_width = keys[0].shape[1]
    for head, (query, key, value) in enumerate(zip(queries, keys, values)):
        scores = scores_of(query, key, limit, scale)
        row_top = jnp.max(scores, axis=1, keepdims=True)
        raised = jnp.exp(scores - row_top)
        totals = jnp.sum(raised, axis=1, keepdims=True)
        weights = (raised / totals).astype(jnp.bfloat16)
        mixed_ref[:, head * head_width : (head + 1) * head_width] = matmul(weights, value).astype(
            jnp.bfloat16
        )
        logsum_ref[:, head : head + 1] = row_top + jnp.log(totals)


def attend_heads_back(queries, keys, values, limit, scale, logsum_ref, grads, outs):
    grad_query_ref, grad_key_ref, grad_value_ref = outs
    for head, (query, key, value, grad) in enumerate(zip(queries, keys, values, grads)):
        scores = scores_of(query, key, limit, scale)
        weights = jnp.exp(scores - logsum_ref[:, head : head + 1])
        grad_weights = back_product(grad, value)
        grad_value_ref(head, outer_sum(weights.astype(jnp.bfloat16), grad))
        inner_sum = jnp.sum(weights * grad_weights, axis=1, keepdims=True)
        grad_scores = (scale * (weights * (grad_weights - inner_sum))).astype(jnp.bfloat16)
        grad_query_ref(head, matmul(grad_scores, key))
        grad_key_ref(head, outer_sum(grad_scores, query))


def head_writer(ref, first, width):
    def write(head, value):
        start = first + head * width
        ref[:, start : start + width] = value.astype(jnp.bfloat16)

    return write


VMEM_LIMIT = 48 * 1024 * 1024


def cost(flops, moved, transcendentals=0):
    return pl.CostEstimate(
        flops=int(flops), bytes_accessed=int(moved), transcendentals=int(transcendentals)
    )


def attention_cost(images, length, slots, heads, width, products):
    pairs = images * heads * length * slots
    return cost(2 * products * pairs * width, 8 * pairs, pairs)


def attend_self(qkv, images, heads, scale):
    rows, columns = qkv.shape
    length, part = rows // images, columns // 3

    def kernel(qkv_ref, mixed_ref, logsum_ref):
        blocks = parts_of(qkv_ref, 3 * heads)
        attend_heads(
            blocks[:heads],
            blocks[heads : 2 * heads],
            blocks[2 * heads :],
            None,
            scale,
            mixed_ref,
            logsum_ref,
        )

    return pl.pallas_call(
        kernel,
        grid=(images,),
        in_specs=[row_block(length, columns)],
        out_specs=[row_block(length, part), row_block(length, heads)],
        out_shape=[
            jax.ShapeDtypeStruct((rows, part), jnp.bfloat16),
            jax.ShapeDtypeStruct((rows, heads), jnp.float32),
        ],
        compiler_params=pltpu.CompilerParams(vmem_limit_bytes=VMEM_LIMIT),
        cost_estimate=attention_cost(images, length, length, heads, part // heads, 2),
        name="attend_self",
    )(qkv)


def attend_self_back(qkv, logsum, grad_mixed, images, heads, scale):
    rows, columns = qkv.shape
    length, part = rows // images, columns // 3

    def kernel(qkv_ref, logsum_ref, grad_ref, out_ref):
        blocks = parts_of(qkv_ref, 3 * heads)
        writers = [head_writer(out_ref, i * part, part // heads) for i in range(3)]
        attend_heads_back(
            blocks[:heads],
            blocks[heads : 2 * heads],
            blocks[2 * heads :],
            None,
            scale,
            logsum_ref,
            parts_of(grad_ref, heads),
            writers,
        )

    return pl.pallas_call(
        kernel,
        grid=(images,),
        in_specs=[row_block(length, columns), row_block(length, heads), row_block(length, part)],
        out_specs=row_block(length, columns),
        out_shape=jax.ShapeDtypeStruct((rows, columns), jnp.bfloat16),
        compiler_params=pltpu.CompilerParams(vmem_limit_bytes=VMEM_LIMIT),
        cost_estimate=attention_cost(images, length, length, heads, part // heads, 5),
        name="attend_self_back",
    )(qkv, logsum, grad_mixed)


def attend_cross(queries, keyval, limits, images, heads, scale):
    rows, part = queries.shape
    length, slots = rows // images, keyval.shape[0] // images

    def kernel(limits_ref, query_ref, keyval_ref, mixed_ref, logsum_ref):
        blocks = parts_of(keyval_ref, 2 * heads)
        attend_heads(
            parts_of(query_ref, heads),
            blocks[:heads],
            blocks[heads:],
            limits_ref[pl.program_id(0)],
            scale,
            mixed_ref,
            logsum_ref,
        )

    return pl.pallas_call(
        kernel,
        grid_spec=pltpu.PrefetchScalarGridSpec(
            num_scalar_prefetch=1,
            grid=(images,),
            in_specs=[row_block(length, part), row_block(slots, 2 * part)],
            out_specs=[row_block(length, part), row_block(length, heads)],
        ),
        out_shape=[
            jax.ShapeDtypeStruct((rows, part), jnp.bfloat16),
            jax.ShapeDtypeStruct((rows, heads), jnp.float32),
        ],
        compiler_params=pltpu.CompilerParams(vmem_limit_bytes=VMEM_LIMIT),
        cost_estimate=attention_cost(images, length, slots, heads, part // heads, 2),
        name="attend_cross",
    )(limits, queries, keyval)


def attend_cross_back(queries, keyval, limits, logsum, grad_mixed, images, heads, scale):
    rows, part = queries.shape
    length, slots = rows // images, keyval.shape[0] // images

    def kernel(limits_ref, query_ref, keyval_ref, logsum_ref, grad_ref, out_ref, text_ref):
        blocks = parts_of(keyval_ref, 2 * heads)
        width = part // heads
        attend_heads_back(
            parts_of(query_ref, heads),
            blocks[:heads],
            blocks[heads:],
            limits_ref[pl.program_id(0)],
            scale,
            logsum_ref,
            parts_of(grad_ref, heads),
            [
                head_writer(out_ref, 0, width),
                head_writer(text_ref, 0, width),
                head_writer(text_ref, part, width),
            ],
        )

    return pl.pallas_call(
        kernel,
        grid_spec=pltpu.PrefetchScalarGridSpec(
            num_scalar_prefetch=1,
            grid=(images,),
            in_specs=[
                row_block(length, part),
                row_block(slots, 2 * part),
                row_block(length, heads),
                row_block(length, part),
            ],
            out_specs=[row_block(length, part), row_block(slots, 2 * part)],
        ),
        out_shape=[
            jax.ShapeDtypeStruct((rows, part), jnp.bfloat16),
            jax.ShapeDtypeStruct((images * slots, 2 * part), jnp.bfloat16),
        ],
        compiler_params=pltpu.CompilerParams(vmem_limit_bytes=VMEM_LIMIT),
        cost_estimate=attention_cost(images, length, slots, heads, part // heads, 5),
        name="attend_cross_back",
    )(limits, queries, keyval, logsum, grad_mixed)


def pick_blocks(weights, counts, rank):
    rows = weights[0].shape[0]
    width = weights[0].shape[1] // (counts[0] * PEERS)
    firsts = [sum(counts[:i]) for i in range(len(counts))]

    def kernel(rank_ref, *refs):
        step = pl.program_id(0)
        out_ref = refs[-1]
        for ref, first, count in zip(refs, firsts, counts):

            @pl.when((step >= first) & (step < first + count))
            def _():
                out_ref[...] = ref[...]

    def spec(first, count):
        return pl.BlockSpec(
            (rows, width),
            lambda step, rank_ref: (
                0,
                jnp.clip(step - first, 0, count - 1) * PEERS + rank_ref[0],
            ),
        )

    return pl.pallas_call(
        kernel,
        grid_spec=pltpu.PrefetchScalarGridSpec(
            num_scalar_prefetch=1,
            grid=(sum(counts),),
            in_specs=[spec(first, count) for first, count in zip(firsts, counts)],
            out_specs=pl.BlockSpec((rows, width), lambda step, rank_ref: (0, step)),
        ),
        out_shape=jax.ShapeDtypeStruct((rows, width * sum(counts)), weights[0].dtype),
        cost_estimate=cost(0, 4 * rows * width * sum(counts)),
        name="pick_blocks",
    )(rank.reshape(1), *weights)


def spread_blocks(found, first, count, width):
    rows = found.shape[0] // PEERS

    def kernel(found_ref, out_ref):
        for peer in range(PEERS):
            out_ref[:, peer * width : (peer + 1) * width] = found_ref[
                peer * rows : (peer + 1) * rows, :
            ].astype(jnp.float32)

    return pl.pallas_call(
        kernel,
        grid=(count,),
        in_specs=[pl.BlockSpec((PEERS * rows, width), lambda block: (0, first + block))],
        out_specs=pl.BlockSpec((rows, PEERS * width), lambda block: (0, block)),
        out_shape=jax.ShapeDtypeStruct((rows, count * PEERS * width), jnp.float32),
        cost_estimate=cost(0, 6 * rows * count * PEERS * width),
        compiler_params=pltpu.CompilerParams(vmem_limit_bytes=VMEM_LIMIT),
        name="spread_blocks",
    )(found)


def spread_peers(found, rank, first, count, width):
    rows = found[0].shape[0]

    def kernel(rank_ref, *refs):
        for peer in range(PEERS):
            for mask in range(PEERS):

                @pl.when((rank_ref[0] ^ mask) == peer)
                def _():
                    refs[-1][:, peer * width : (peer + 1) * width] = refs[mask][...].astype(
                        jnp.float32
                    )

    return pl.pallas_call(
        kernel,
        grid_spec=pltpu.PrefetchScalarGridSpec(
            num_scalar_prefetch=1,
            grid=(count,),
            in_specs=[pl.BlockSpec((rows, width), lambda block, rank_ref: (0, first + block))]
            * PEERS,
            out_specs=pl.BlockSpec((rows, PEERS * width), lambda block, rank_ref: (0, block)),
        ),
        out_shape=jax.ShapeDtypeStruct((rows, count * PEERS * width), jnp.float32),
        cost_estimate=cost(0, 6 * rows * count * PEERS * width),
        compiler_params=pltpu.CompilerParams(vmem_limit_bytes=VMEM_LIMIT),
        name="spread_peers",
    )(rank.reshape(1), *found)


def spread_rows(found, width):
    rows = found.shape[0] // PEERS

    def kernel(found_ref, out_ref):
        out_ref[...] = found_ref[...].astype(jnp.float32)

    return pl.pallas_call(
        kernel,
        grid=(PEERS,),
        in_specs=[pl.BlockSpec((rows, width), lambda peer: (peer, 0))],
        out_specs=pl.BlockSpec((rows, width), lambda peer: (peer, 0)),
        out_shape=jax.ShapeDtypeStruct((PEERS * rows, width), jnp.float32),
        cost_estimate=cost(0, 6 * PEERS * rows * width),
        compiler_params=pltpu.CompilerParams(vmem_limit_bytes=VMEM_LIMIT),
        name="spread_rows",
    )(found)


PEERS = 4


def swap(value, mask):
    return lax.ppermute(value, "rep", [(peer, peer ^ mask) for peer in range(PEERS)])


def stack_rows(parts):
    rows, columns = parts[0].shape
    count = len(parts)

    def kernel(*refs):
        ins, out, held, arrived, left = refs[:count], refs[count], refs[-3], refs[-2], refs[-1]
        fetches = [
            pltpu.make_async_copy(ins[i], held.at[i], arrived.at[i]) for i in range(count)
        ]
        stores = [
            pltpu.make_async_copy(held.at[i], out.at[i * rows : (i + 1) * rows, :], left.at[i])
            for i in range(count)
        ]
        for fetch in fetches:
            fetch.start()
        for fetch, store in zip(fetches, stores):
            fetch.wait()
            store.start()
        for store in stores:
            store.wait()

    return pl.pallas_call(
        kernel,
        in_specs=[pl.BlockSpec(memory_space=pl.ANY)] * count,
        out_specs=pl.BlockSpec(memory_space=pl.ANY),
        out_shape=jax.ShapeDtypeStruct((count * rows, columns), parts[0].dtype),
        scratch_shapes=[
            pltpu.VMEM((count, rows, columns), parts[0].dtype),
            pltpu.SemaphoreType.DMA((count,)),
            pltpu.SemaphoreType.DMA((count,)),
        ],
        cost_estimate=cost(0, 4 * count * rows * columns),
        compiler_params=pltpu.CompilerParams(vmem_limit_bytes=VMEM_LIMIT),
        name="stack_rows",
    )(*parts)


def stack_columns(parts):
    orders = ((0, 1, 2, 3), (2, 3, 0, 1), (1, 0, 3, 2), (3, 2, 1, 0))
    rows, columns = parts[0].shape
    block = rows // PEERS

    def kernel(*refs):
        for i, order in enumerate(orders):

            @pl.when(pl.program_id(0) == i)
            def _():
                for j, source in enumerate(order):
                    refs[-1][j * block : (j + 1) * block, :] = refs[i][
                        source * block : (source + 1) * block, :
                    ]

    return pl.pallas_call(
        kernel,
        grid=(PEERS,),
        in_specs=[pl.BlockSpec((rows, columns), lambda step: (0, 0))] * PEERS,
        out_specs=pl.BlockSpec((rows, columns), lambda step: (0, step)),
        out_shape=jax.ShapeDtypeStruct((rows, PEERS * columns), parts[0].dtype),
        cost_estimate=cost(0, 4 * PEERS * rows * columns),
        compiler_params=pltpu.CompilerParams(vmem_limit_bytes=VMEM_LIMIT),
        name="stack_columns",
    )(*parts)


def narrow(total):
    return (total.astype(jnp.bfloat16),)


def plus(total, extra):
    return (total + extra.astype(jnp.float32),)


def narrow_plus(total, extra):
    return ((total + extra.astype(jnp.float32)).astype(jnp.bfloat16),)


def halves(total):
    rows = total.shape[0] // 2
    return (total[:rows].astype(jnp.bfloat16), total[rows:].astype(jnp.bfloat16))


def scaled(total, factor):
    return ((total * factor.astype(jnp.float32)).astype(jnp.bfloat16),)


def gate_and_slope(total):
    value, back = jax.vjp(smooth_gate, total)
    return (value.astype(jnp.bfloat16), back(jnp.ones_like(total))[0].astype(jnp.bfloat16))


def multiply(
    left, right, turned, finish=narrow, types=(jnp.bfloat16,), first=0, rows=None, extra=None, half=None
):
    rows = left.shape[0] if rows is None else rows
    depth = left.shape[1]
    breadth = right.shape[1] // (1 if half is None else 2)
    columns = right.shape[0] if turned else breadth
    width = min(512, columns)
    skip = 0 if half is None else half * breadth // (depth if turned else width)
    product = back_product if turned else matmul
    tall = rows // 2 if finish is halves else rows

    def kernel(*refs):
        left_ref, right_ref = refs[:2]
        outs = refs[-len(types) :]
        blocks = [ref[...] for ref in refs[2 : -len(types)]]
        for out, value in zip(outs, finish(product(left_ref[...], right_ref[...]), *blocks)):
            out[...] = value

    specs = [
        pl.BlockSpec((rows, depth), lambda step: (first // rows, 0)),
        pl.BlockSpec((width, depth), lambda step: (step, skip))
        if turned
        else pl.BlockSpec((depth, width), lambda step: (0, skip + step)),
    ]
    values = [left, right]
    if extra is not None:
        extra, start = extra
        specs.append(pl.BlockSpec((rows, width), lambda step: (start // rows, step)))
        values.append(extra)
    found = pl.pallas_call(
        kernel,
        grid=(columns // width,),
        in_specs=specs,
        out_specs=[pl.BlockSpec((tall, width), lambda step: (0, step))] * len(types),
        out_shape=[jax.ShapeDtypeStruct((tall, columns), kind) for kind in types],
        cost_estimate=cost(2 * rows * depth * columns, 2 * (rows * depth + depth * columns + rows * columns)),
        compiler_params=pltpu.CompilerParams(vmem_limit_bytes=VMEM_LIMIT),
        name="multiply",
    )(*values)
    return found[0] if len(types) == 1 else found


def weight_term(left, right, rank=None, into=None, first=0, total=None):
    depth, rows = left.shape
    columns = right.shape[1] if rank is None else right.shape[1] // PEERS
    height = min(1024, rows) if rank is None else rows // PEERS
    width = min(512, columns)
    shift = columns // width
    chosen = jnp.zeros((1,), jnp.int32) if rank is None else rank.reshape(1)
    total = columns if total is None else total

    def kernel(chosen_ref, left_ref, right_ref, *refs):
        refs[-1][...] = outer_sum(left_ref[...], right_ref[...]).astype(jnp.bfloat16)

    return pl.pallas_call(
        kernel,
        grid_spec=pltpu.PrefetchScalarGridSpec(
            num_scalar_prefetch=1,
            grid=(columns // width, rows // height),
            in_specs=[
                pl.BlockSpec(
                    (depth, height),
                    lambda j, i, chosen_ref: (0, i if rank is None else i ^ chosen_ref[0]),
                ),
                pl.BlockSpec(
                    (depth, width), lambda j, i, chosen_ref: (0, chosen_ref[0] * shift + j)
                ),
            ]
            + [pl.BlockSpec(memory_space=pl.ANY)] * (into is not None),
            out_specs=pl.BlockSpec(
                (height, width), lambda j, i, chosen_ref: (i, first // width + j)
            ),
        ),
        out_shape=jax.ShapeDtypeStruct((rows, total), jnp.bfloat16),
        input_output_aliases={} if into is None else {3: 0},
        cost_estimate=cost(
            2 * rows * depth * columns, 2 * (rows * depth + depth * columns + rows * columns)
        ),
        compiler_params=pltpu.CompilerParams(vmem_limit_bytes=VMEM_LIMIT),
        name="weight_term",
    )(chosen, left, right, *([] if into is None else [into]))


def multiply_rest(left, right, turned, got):
    (rows, columns), depth = got[0].shape, left.shape[1]
    width = min(512, columns)
    product = back_product if turned else matmul

    def kernel(left_ref, right_ref, got_ref, got_far_ref, own_ref, far_ref):
        total = product(left_ref[...], right_ref[...])
        own_ref[...] = total[:rows] + got_ref[...].astype(jnp.float32)
        far_ref[...] = (total[rows:] + got_far_ref[...].astype(jnp.float32)).astype(jnp.bfloat16)

    return pl.pallas_call(
        kernel,
        grid=(columns // width,),
        in_specs=[
            pl.BlockSpec((2 * rows, depth), lambda step: (0, 0)),
            pl.BlockSpec((width, depth), lambda step: (step, 0))
            if turned
            else pl.BlockSpec((depth, width), lambda step: (0, step)),
        ]
        + [pl.BlockSpec((rows, width), lambda step: (0, step))] * 2,
        out_specs=[pl.BlockSpec((rows, width), lambda step: (0, step))] * 2,
        out_shape=[
            jax.ShapeDtypeStruct((rows, columns), jnp.float32),
            jax.ShapeDtypeStruct((rows, columns), jnp.bfloat16),
        ],
        cost_estimate=cost(
            4 * rows * depth * columns, 2 * (2 * rows * depth + depth * columns + 5 * rows * columns)
        ),
        compiler_params=pltpu.CompilerParams(vmem_limit_bytes=VMEM_LIMIT),
        name="multiply_rest",
    )(left, right, *got)


class Order:
    def __init__(self):
        self.token = ()

    def run(self, work, first, *others):
        if self.token:
            first = after(first, self.token)
        found = work(first, *others)
        self.token = tuple(jax.tree.leaves(found))
        return found

    def hold(self, value):
        return after(value, self.token)

    def tick(self, *rings):
        heads = [ring.pieces[-1] for ring in rings]
        after_work = after(heads, self.token)
        for ring, head in zip(rings, after_work):
            ring.pieces[-1] = head
            if ring.sevenths < 7:
                ring.send()
        self.wait(*heads)

    def wait(self, *values):
        self.token = self.token + tuple(jax.tree.leaves(values))


class State:
    pass


class GroupSum:
    def __init__(self, order, left, right, turned, half=None):
        self.order, self.left, self.right, self.turned = order, left, right, turned
        self.half = half
        self.rows = left.shape[0] // PEERS

    def near(self):
        rows = self.rows
        sent = self.order.run(
            lambda left: multiply(
                left,
                self.right,
                self.turned,
                halves,
                (jnp.bfloat16, jnp.bfloat16),
                first=2 * rows,
                rows=2 * rows,
            ),
            self.left,
        )
        self.got = [swap(part, 1) for part in sent]

    def rest(self):
        self.mine, self.sent = self.order.run(
            lambda left: multiply_rest(left, self.right, self.turned, self.got), self.left
        )
        self.crossed = swap(self.sent, 2)

    def send(self):
        self.near()
        self.rest()
        return self

def ring_member(place, size):
    place = place % size
    return jnp.where(place < size // 2, 2 * place, 2 * (size - 1 - place) + 1)


def ring_pairs(size, step):
    order = [2 * i for i in range(size // 2)] + [2 * i + 1 for i in reversed(range(size // 2))]
    return [(order[i], order[(i + step) % size]) for i in range(size)]


def after(value, earlier):
    return lax.optimization_barrier((value, earlier))[0]


class Gather:
    def __init__(self, value, size, step):
        self.size, self.step, self.pieces = size, step, [value]
        self.sevenths = 0

    def send(self):
        self.sevenths += 1
        while len(self.pieces) - 1 < self.sevenths * (self.size - 1) // 7:
            self.pieces.append(
                lax.ppermute(self.pieces[-1], "fsdp", ring_pairs(self.size, self.step))
            )

    def starts(self, place, rows):
        return jnp.stack(
            [ring_member(place - self.step * k, self.size) * rows for k in range(self.size)]
        ).astype(jnp.int32)


def lay_out(pieces, starts, widths):
    size = len(pieces)
    rows = pieces[0].shape[0]
    count = len(widths)
    edges = [sum(widths[:i]) for i in range(count)]

    def kernel(starts_ref, *refs):
        shards, outs, done = refs[:size], refs[size:-1], refs[-1]
        copies = []
        for i, shard in enumerate(shards):
            start = pl.multiple_of(starts_ref[i], rows)
            for j, out in enumerate(outs):
                copies.append(
                    pltpu.make_async_copy(
                        shard.at[:, edges[j] : edges[j] + widths[j]],
                        out.at[pl.ds(start, rows), :],
                        done.at[i, j],
                    )
                )
        for copy in copies:
            copy.start()
        for copy in copies:
            copy.wait()

    return pl.pallas_call(
        kernel,
        out_shape=[jax.ShapeDtypeStruct((size * rows, w), pieces[0].dtype) for w in widths],
        in_specs=[pl.BlockSpec(memory_space=pltpu.SMEM)]
        + [pl.BlockSpec(memory_space=pltpu.VMEM)] * size,
        out_specs=[pl.BlockSpec(memory_space=pl.ANY)] * count,
        scratch_shapes=[pltpu.SemaphoreType.DMA((size, count))],
        compiler_params=pltpu.CompilerParams(vmem_limit_bytes=VMEM_LIMIT),
        cost_estimate=cost(0, 4 * size * rows * sum(widths)),
        name="lay_out",
    )(starts, *pieces)


def ring_add(values, spots, rows, got):
    count = len(values)
    columns = values[0].shape[1]
    width = min(1024, columns)

    def kernel(spots_ref, *refs):
        for i in range(count):
            block = refs[i][...]
            refs[-count + i][...] = block if got is None else refs[count + i][...] + block

    def spec(i):
        return pl.BlockSpec((rows, width), lambda step, spots_ref: (spots_ref[i], step))

    plain = [pl.BlockSpec((rows, width), lambda step, spots_ref: (0, step))] * count
    arrived = [] if got is None else list(got)
    return pl.pallas_call(
        kernel,
        grid_spec=pltpu.PrefetchScalarGridSpec(
            num_scalar_prefetch=1,
            grid=(columns // width,),
            in_specs=[spec(i) for i in range(count)] + plain[: len(arrived)],
            out_specs=plain,
        ),
        out_shape=[jax.ShapeDtypeStruct((rows, columns), jnp.bfloat16)] * count,
        cost_estimate=cost(rows * columns * count, 6 * rows * columns * count),
        compiler_params=pltpu.CompilerParams(vmem_limit_bytes=VMEM_LIMIT),
        name="ring_add",
    )(spots, *values, *arrived)


class Scatter:
    def __init__(self, order, entries, size, place, rows, shard_rows):
        self.order, self.entries = order, entries
        self.size, self.place, self.rows, self.step = size, place, rows, 0
        self.sevenths, self.blocks = 0, shard_rows // rows
        self.values = [value for value, _, _ in entries]
        self.sums = order.run(
            lambda first: ring_add([first] + self.values[1:], self.spots(), self.rows, None),
            self.values[0],
        )

    def spots(self):
        return jnp.stack(
            [
                ring_member(self.place - direction * (self.step + 1), self.size) * self.blocks
                + block
                for _, direction, block in self.entries
            ]
        ).astype(jnp.int32)

    def reach(self):
        self.sevenths += 1
        while self.step < self.sevenths * (self.size - 1) // 7:
            self.step += 1
            arrived = [
                lax.ppermute(value, "fsdp", ring_pairs(self.size, direction))
                for value, (_, direction, _) in zip(self.sums, self.entries)
            ]
            spots = self.spots()
            self.sums = self.order.run(
                lambda got: ring_add(self.values, spots, self.rows, got), arrived
            )
        return self.sevenths == 7


class Exchange:
    def __init__(self, order, value, size):
        self.order, self.value, self.size, self.mask = order, value[None], size, 1
        self.send()

    def send(self):
        pairs = [(i, i ^ self.mask) for i in range(self.size)]
        self.got = lax.ppermute(self.value, "fsdp", pairs)

    def hop(self):
        low = (lax.axis_index("fsdp") & self.mask) == 0

        def join(got):
            return jnp.concatenate(
                [jnp.where(low, self.value, got), jnp.where(low, got, self.value)], axis=0
            )

        self.value = self.order.run(join, self.got)
        self.mask *= 2
        if self.mask < self.size:
            self.send()


class Everyone:
    def __init__(self, order, value, size):
        self.order, self.value = order, value
        self.hops = [("fsdp", size // 2 >> i, size) for i in range(size.bit_length() - 1)]
        self.hops += [("rep", 2, PEERS), ("rep", 1, PEERS)]
        self.left = len(self.hops)
        self.send()

    def send(self):
        axis, mask, size = self.hops.pop(0)
        self.got = lax.ppermute(self.value, axis, [(i, i ^ mask) for i in range(size)])

    def hop(self):
        if self.left:
            self.value = self.order.run(
                lambda got: jnp.concatenate([self.value, got], axis=0), self.got
            )
            self.left -= 1
            if self.hops:
                self.send()


PLAN = (
    "p1", "p2", "a0", "r", "p3", "p4", "A", "e", "A", "e", "A", "e", "terms", "A", "start", "xa",
    "A", "ja", "st", "xt", "A", "jt", "sg", "A", "ab", "lay1", "qkv", "lay2", "B", "kv", "self",
    "wo", "near1", "rest1", "B", "wm", "B", "x1", "fin1", "B", "y2", "join2", "sm", "cq", "cross",
    "near2", "B", "rest2", "B", "x2", "fin2", "B", "y3", "join3", "sc", "lay3", "up", "jg",
    "lay4", "pre", "near3", "rest3", "dterm", "uterm", "F0", "x3", "fin3", "jc", "near6", "F",
    "y4", "join4", "mm4", "cback", "near4", "F", "rest4", "qterm", "kterm", "mterm", "C0", "F",
    "x4", "fin4", "near7", "C", "F", "y5", "join5", "mm5", "sback", "near5", "F", "C", "rest5",
    "qkvterm", "jm", "oterm", "S0", "F", "C", "x5", "fin5", "rest6", "S", "C", "F", "S", "C",
    "x6", "fin6", "S", "C", "h", "S", "C", "h", "rest7", "S", "h", "dout", "S", "h", "fin7",
    "uout", "S", "h", "mod", "cout", "sout",
)


def body(
    image_tokens,
    text_tokens,
    text_lengths,
    timesteps,
    cotangent,
    mod_weight,
    qkv_weight,
    out_weight,
    query_weight,
    keyval_weight,
    merge_weight,
    cross_gain,
    up_weight,
    down_weight,
):
    images, length, width = image_tokens.shape
    text_count, text_width = text_tokens.shape[1:]
    group = lax.axis_size("fsdp")
    rank = lax.axis_index("rep")
    member = lax.axis_index("fsdp")
    heads = HEADS // PEERS
    head_width = width // HEADS
    part = width // PEERS
    score_scale = head_width ** (-0.5)
    shard_rows = mod_weight.shape[0]
    hidden = up_weight.shape[1]
    rows = images * length
    all_images = PEERS * images

    def own_part(value, blocks):
        count = value.shape[1] // (blocks * PEERS)
        return lax.dynamic_index_in_dim(
            value.reshape(value.shape[0], blocks, PEERS, count), rank, 2, keepdims=False
        ).reshape(value.shape[0], blocks * count)

    def ordered(found):
        stacked = jnp.stack(found)
        return [
            lax.dynamic_index_in_dim(stacked, rank ^ place, 0, keepdims=False)
            for place in range(PEERS)
        ]

    def columns_to_rows(value):
        blocks = value.reshape(PEERS, part, -1)
        found = [
            lax.dynamic_index_in_dim(blocks, rank ^ mask, 0, keepdims=False)
            for mask in range(PEERS)
        ]
        found = [found[0]] + [swap(found[mask], mask) for mask in range(1, PEERS)]
        return jnp.concatenate(ordered(found), axis=1)

    order = Order()
    aligned = hidden // (group * PEERS) % 128 == 0
    spot = jnp.where(member % 2 == 0, member // 2, group - 1 - member // 2)
    def flatten(value):
        return value.reshape(-1, value.shape[-1])

    def own_rows(value):
        return value.reshape(images, length, width)

    half_width = width // 2
    column = member * shard_rows + jnp.arange(shard_rows, dtype=jnp.int32)
    place = jnp.where(column < half_width, column, column - half_width)
    frequency = jnp.exp(-math.log(10000.0) * place.astype(jnp.float32) / half_width)

    def conditions(steps):
        angles = steps.astype(jnp.float32)[:, None] * frequency[None, :]
        return jnp.where(column < half_width, jnp.sin(angles), jnp.cos(angles)).astype(
            jnp.bfloat16
        )

    residual = image_tokens.astype(jnp.float32)
    grad_block = cotangent.astype(jnp.float32)
    norm_one = normed(residual)

    def send_rows(value):
        return [value, swap(value, 2), swap(value, 1)]

    def join_rows(parts):
        far = order.hold(parts[1])
        return order.run(
            lambda last: stack_rows([parts[0], far, parts[2], last]), swap(far, 1)
        )

    def send_columns(value):
        return [value, swap(value, 1), swap(value, 2)]

    def join_columns(parts):
        far = order.hold(parts[2])
        return order.run(
            lambda last: stack_columns([parts[0], parts[1], far, last]), swap(far, 1)
        )

    v = State()
    mine = jnp.concatenate([timesteps, text_lengths]).astype(jnp.float32)
    mine = [mine, swap(mine, 2), swap(mine, 1)]

    def p1():
        v.pick1 = order.run(lambda w: pick_blocks([w, out_weight], [3, 1], rank), qkv_weight)

    def p2():
        v.pick2 = order.run(
            lambda w: pick_blocks([w, keyval_weight, merge_weight], [1, 2, 1], rank),
            query_weight,
        )

    def p3():
        v.pick3 = order.run(
            lambda w: pick_blocks([w], [group], rank) if aligned else own_part(w, group),
            up_weight,
        )

    def p4():
        v.pick4 = order.run(
            lambda w: lax.dynamic_index_in_dim(
                w.reshape(PEERS, -1, width), rank, 0, keepdims=False
            ),
            down_weight,
        )

    def a0():
        v.first, v.second = Gather(v.pick1, group, 1), Gather(v.pick2, group, -1)
        order.tick(v.first, v.second)

    def ab():
        v.third, v.fourth = Gather(v.pick3, group, 1), Gather(v.pick4, group, -1)
        order.tick(v.first, v.second, v.third, v.fourth)

    def r():
        far = order.hold(mine[1])
        found = order.run(
            lambda last: jnp.stack([mine[0], far, mine[2], last]), swap(far, 1)
        )
        v.length_all = found[:, images:].reshape(-1).astype(jnp.int32)
        v.exchange = Exchange(
            order,
            jnp.concatenate([found[:, :images].reshape(-1), cross_gain.astype(jnp.float32)]),
            group,
        )

    def e():
        v.exchange.hop()

    def terms():
        while v.exchange.mask < group:
            e()
        small = v.exchange.value
        v.gain_full = small[:, all_images:].reshape(-1)
        sequence = [0]
        while len(sequence) < group:
            sequence += [index + group // (2 * len(sequence)) for index in sequence]
        steps = small[:, :all_images][member ^ jnp.array(sequence, dtype=jnp.int32)]
        v.all_steps = steps.reshape(group, PEERS, images).transpose(1, 0, 2).reshape(-1)
        found = order.run(
            lambda steps: matmul(conditions(steps), mod_weight), small[:, :images].reshape(-1)
        )
        v.terms = lax.all_to_all(
            found.reshape(group, images, -1), "fsdp", split_axis=0, concat_axis=0, tiled=True
        )

    def start():
        def work(found):
            pieces = jnp.sum(found, axis=0).reshape(images, 6, 1, width)
            act = flatten(normed(residual) * (1.0 + pieces[:, 1]) + pieces[:, 0])
            grad_three = flatten(pieces[:, 5] * grad_block)
            return pieces, act.astype(jnp.bfloat16), grad_three.astype(jnp.bfloat16)

        pieces, act_one, v.grad_three = order.run(work, v.terms)
        v.shift_self, v.scale_self, v.gate_self = (pieces[:, 0], pieces[:, 1], pieces[:, 2])
        v.shift_mlp, v.scale_mlp, v.gate_mlp = (pieces[:, 3], pieces[:, 4], pieces[:, 5])
        v.act_one = send_rows(act_one)

    def ja():
        v.act_one = join_rows(v.act_one)

    def st():
        v.text_all = send_rows(order.hold(flatten(text_tokens)))

    def jt():
        v.text_all = join_rows(v.text_all)

    def sg():
        v.grad_three = send_rows(order.hold(v.grad_three))

    def jg():
        v.grad_three = join_rows(v.grad_three)

    def lay1():
        v.qkv_part, out_part = order.run(
            lambda last: lay_out(
                v.first.pieces[:-1] + [last], v.first.starts(spot, shard_rows), [3 * part, part]
            ),
            v.first.pieces[-1],
        )
        v.out_part = columns_to_rows(out_part)

    def lay2():
        v.query_part, v.keyval_part, merge_part = order.run(
            lambda last: lay_out(
                v.second.pieces[:-1] + [last],
                v.second.starts(spot, shard_rows),
                [part, 2 * part, part],
            ),
            v.second.pieces[-1],
        )
        v.merge_part = columns_to_rows(merge_part)

    def qkv():
        v.qkv_act = order.run(lambda a: multiply(a, v.qkv_part, False), v.act_one)

    def kv():
        v.keyval = order.run(lambda a: multiply(a, v.keyval_part, False), v.text_all)

    def self_attend():
        v.mixed_flat, v.logsum_self = order.run(
            lambda a: attend_self(a, all_images, heads, score_scale), v.qkv_act
        )

    def near1():
        v.sum1 = GroupSum(order, v.mixed_flat, v.out_part, False)
        v.sum1.near()

    def fin1():
        def finish(crossed):
            branch_one = own_rows(v.sum1.mine + crossed.astype(jnp.float32))
            hidden_one = residual + v.gate_self * branch_one
            return (
                branch_one,
                hidden_one,
                flatten(normed(hidden_one) * v.gain_full).astype(jnp.bfloat16),
            )

        v.branch_one, v.hidden_one, act_two = order.run(finish, v.sum1.crossed)
        v.norm_two = normed(v.hidden_one)
        v.act_two = send_rows(act_two)

    def join2():
        v.act_two = join_rows(v.act_two)

    def cq():
        v.cross_queries = order.run(lambda a: multiply(a, v.query_part, False), v.act_two)

    def cross():
        v.cross_flat, v.logsum_cross = order.run(
            lambda a: attend_cross(a, v.keyval, v.length_all, all_images, heads, score_scale),
            v.cross_queries,
        )

    def near2():
        v.sum2 = GroupSum(order, v.cross_flat, v.merge_part, False)
        v.sum2.near()

    def fin2():
        def finish(crossed):
            hidden_two = v.hidden_one + own_rows(v.sum2.mine + crossed.astype(jnp.float32))
            act = flatten(normed(hidden_two) * (1.0 + v.scale_mlp) + v.shift_mlp)
            return hidden_two, act.astype(jnp.bfloat16)

        v.hidden_two, act_three = order.run(finish, v.sum2.crossed)
        v.norm_three = normed(v.hidden_two)
        v.act_three = send_rows(act_three)

    def join3():
        v.act_three = join_rows(v.act_three)

    def sm():
        v.mixed_parts = send_columns(order.hold(v.mixed_flat))

    def jm():
        v.mixed_all = join_columns(v.mixed_parts)

    def sc():
        v.cross_parts = send_columns(order.hold(v.cross_flat))

    def jc():
        v.cross_all = join_columns(v.cross_parts)

    def lay3():
        (v.up_part,) = order.run(
            lambda last: lay_out(
                v.third.pieces[:-1] + [last], v.third.starts(spot, shard_rows), [hidden // PEERS]
            ),
            v.third.pieces[-1],
        )

    def up():
        v.activated, v.slope = order.run(
            lambda a: multiply(a, v.up_part, False, gate_and_slope, (jnp.bfloat16, jnp.bfloat16)),
            v.act_three,
        )

    def lay4():
        (v.down_part,) = order.run(
            lambda last: lay_out(
                v.fourth.pieces[:-1] + [last], v.fourth.starts(spot, shard_rows), [width]
            ),
            v.fourth.pieces[-1],
        )

    def pre():
        v.grad_pre = order.run(
            lambda a: multiply(a, v.down_part, True, scaled, extra=(v.slope, 0)), v.grad_three
        )

    def ring(value):
        halves = [(value, 1, 0), (value, -1, 1)]
        return Scatter(order, halves, group, spot, shard_rows // 2, shard_rows)

    def near3():
        v.sum3 = GroupSum(order, v.grad_pre, v.up_part, True)
        v.sum3.near()

    def dterm():
        v.down_term = order.run(lambda a: weight_term(a, v.grad_three), v.activated)

    def uterm():
        v.up_term = order.run(lambda a: weight_term(a, v.grad_pre), v.act_three)

    def mlp_start():
        v.mlp_ring = Scatter(
            order,
            [(v.down_term, 1, 0), (v.up_term, -1, 0)],
            group,
            spot,
            shard_rows,
            shard_rows,
        )

    def mlp_step():
        if v.mlp_ring.reach():
            v.down_all, v.up_all = [over_ranks(found) for found in v.mlp_ring.sums]

    def over_ranks(found):
        return lax.all_gather(found, "rep", axis=0, tiled=True)

    def fin3():
        def finish(crossed):
            grad_act = own_rows(v.sum3.mine + crossed.astype(jnp.float32))
            grad_two = grad_block + normed_back(v.hidden_two, grad_act * (1.0 + v.scale_mlp))
            return (
                jnp.sum(grad_act, axis=1),
                jnp.sum(grad_act * v.norm_three, axis=1),
                grad_two,
                flatten(grad_two).astype(jnp.bfloat16),
            )

        v.grad_shift_mlp, v.grad_scale_mlp, v.grad_two, grad_merge = order.run(
            finish, v.sum3.crossed
        )
        v.grad_merge = send_rows(grad_merge)

    def join4():
        v.grad_merge = join_rows(v.grad_merge)

    def mm4():
        v.grad_mixed = order.run(lambda a: multiply(a, v.merge_part, True), v.grad_merge)

    def cback():
        v.grad_query, v.grad_keyval = order.run(
            lambda a: attend_cross_back(
                v.cross_queries,
                v.keyval,
                v.length_all,
                v.logsum_cross,
                a,
                all_images,
                heads,
                score_scale,
            ),
            v.grad_mixed,
        )

    def near4():
        v.sum4 = GroupSum(order, v.grad_query, v.query_part, True)
        v.sum4.near()

    def qterm():
        v.cross_term = order.run(
            lambda a: weight_term(a, v.grad_query, first=0, total=4 * part), v.act_two
        )

    def kterm():
        v.cross_term = order.run(
            lambda a, into: weight_term(a, v.grad_keyval, None, into, part, 4 * part),
            v.text_all,
            v.cross_term,
        )

    def mterm():
        v.cross_term = order.run(
            lambda a, into: weight_term(a, v.grad_merge, rank, into, 3 * part, 4 * part),
            v.cross_all,
            v.cross_term,
        )

    def cross_start():
        v.cross_ring = ring(v.cross_term)

    def cross_step():
        if v.cross_ring.reach():
            v.cross_found = over_ranks(jnp.concatenate(v.cross_ring.sums, axis=0))

    def fin4():
        def finish(crossed):
            grad_act = own_rows(v.sum4.mine + crossed.astype(jnp.float32))
            grad_one = v.grad_two + normed_back(v.hidden_one, grad_act * v.gain_full)
            return (
                jnp.sum(grad_act * v.norm_two, axis=1),
                jnp.sum(grad_one * v.branch_one, axis=1),
                grad_one,
                flatten(v.gate_self * grad_one).astype(jnp.bfloat16),
            )

        v.gain_term, v.grad_gate_self, v.grad_one, grad_out = order.run(finish, v.sum4.crossed)
        v.grad_out = send_rows(grad_out)

    def join5():
        v.grad_out = join_rows(v.grad_out)

    def mm5():
        v.grad_mixed = order.run(lambda a: multiply(a, v.out_part, True), v.grad_out)

    def sback():
        v.grad_qkv = order.run(
            lambda a: attend_self_back(
                v.qkv_act, v.logsum_self, a, all_images, heads, score_scale
            ),
            v.grad_mixed,
        )

    def near5():
        v.sum5 = GroupSum(order, v.grad_qkv, v.qkv_part, True)
        v.sum5.near()

    def qkvterm():
        v.self_term = order.run(
            lambda a: weight_term(a, v.grad_qkv, first=0, total=4 * part), v.act_one
        )

    def oterm():
        v.self_term = order.run(
            lambda a, into: weight_term(a, v.grad_out, rank, into, 3 * part, 4 * part),
            v.mixed_all,
            v.self_term,
        )

    def self_start():
        v.self_ring = ring(v.self_term)

    def self_step():
        if v.self_ring.reach():
            own = jnp.concatenate(v.self_ring.sums, axis=0)
            v.self_found = [own, swap(own, 1), swap(own, 2)]

    def fin5():
        def finish(crossed):
            grad_act = own_rows(v.sum5.mine + crossed.astype(jnp.float32))
            image_grad = v.grad_one + normed_back(residual, grad_act * (1.0 + v.scale_self))
            return (
                jnp.sum(grad_act, axis=1),
                jnp.sum(grad_act * norm_one, axis=1),
                image_grad.astype(jnp.bfloat16),
            )

        v.grad_shift_self, v.grad_scale_self, v.image_grad = order.run(finish, v.sum5.crossed)

    def near6():
        v.sum6 = GroupSum(order, v.activated, v.down_part, False)
        v.sum6.near()

    def fin6():
        def finish(crossed):
            branch_three = own_rows(v.sum6.mine + crossed.astype(jnp.float32))
            block_out = (v.hidden_two + v.gate_mlp * branch_three).astype(jnp.bfloat16)
            vectors = jnp.concatenate(
                [
                    v.grad_shift_self,
                    v.grad_scale_self,
                    v.grad_gate_self,
                    v.grad_shift_mlp,
                    v.grad_scale_mlp,
                    jnp.sum(grad_block * branch_three, axis=1),
                    v.gain_term,
                ],
                axis=1,
            )
            return block_out, vectors.astype(jnp.bfloat16)

        v.block_out, vectors = order.run(finish, v.sum6.crossed)
        v.everyone = Everyone(order, vectors, group)

    def hop():
        v.everyone.hop()

    def near7():
        v.sum7 = GroupSum(order, v.grad_keyval, v.keyval_part, True)
        v.sum7.near()

    def fin7():
        v.text_grad = order.run(
            lambda crossed: (v.sum7.mine + crossed.astype(jnp.float32))
            .astype(jnp.bfloat16)
            .reshape(text_tokens.shape),
            v.sum7.crossed,
        )

    def down_out():
        v.down_grad = order.run(lambda a: spread_rows(a, width), v.down_all)

    def up_out():
        if aligned:
            v.up_grad = order.run(
                lambda a: spread_blocks(a, 0, group, hidden // (group * PEERS)), v.up_all
            )
        else:
            v.up_grad = (
                v.up_all.reshape(PEERS, shard_rows, group, -1)
                .transpose(1, 2, 0, 3)
                .reshape(shard_rows, hidden)
                .astype(jnp.float32)
            )

    def mod_out():
        while v.everyone.left:
            hop()

        def finish(found):
            return (
                outer_sum(conditions(v.all_steps), found[:, : 6 * width]),
                jnp.sum(
                    lax.dynamic_slice_in_dim(
                        found, 6 * width + member * shard_rows, shard_rows, 1
                    ).astype(jnp.float32),
                    axis=0,
                ),
            )

        v.mod_grad, v.gain_grad = order.run(finish, v.everyone.value)

    def cross_out():
        v.query_grad, v.keyval_grad, v.merge_grad = [
            order.run(lambda a: spread_blocks(a, start, count, part), v.cross_found)
            for start, count in ((0, 1), (1, 2), (3, 1))
        ]

    def self_out():
        own, near, far = v.self_found
        far = order.hold(far)
        diagonal = swap(far, 1)
        v.qkv_grad, v.out_grad = [
            order.run(
                lambda last: spread_peers([own, near, far, last], rank, start, count, part),
                diagonal,
            )
            for start, count in ((0, 3), (3, 1))
        ]

    work = {
        "A": lambda: order.tick(v.first, v.second),
        "B": lambda: order.tick(v.third, v.fourth),
        "xa": lambda: order.wait(v.act_one[1]),
        "xt": lambda: order.wait(v.text_all[1]),
        "F0": mlp_start,
        "F": mlp_step,
        "C0": cross_start,
        "C": cross_step,
        "S0": self_start,
        "S": self_step,
        "h": hop,
        "self": self_attend,
        "wo": lambda: order.wait(v.out_part),
        "wm": lambda: order.wait(v.merge_part),
        "dout": down_out,
        "uout": up_out,
        "mod": mod_out,
        "cout": cross_out,
        "sout": self_out,
        "x1": lambda: order.wait(v.sum1.crossed),
        "x2": lambda: order.wait(v.sum2.crossed),
        "x3": lambda: order.wait(v.sum3.crossed),
        "x4": lambda: order.wait(v.sum4.crossed),
        "x5": lambda: order.wait(v.sum5.crossed),
        "x6": lambda: order.wait(v.sum6.crossed),
        "y2": lambda: order.wait(v.act_two[1]),
        "y3": lambda: order.wait(v.act_three[1]),
        "y4": lambda: order.wait(v.grad_merge[1]),
        "y5": lambda: order.wait(v.grad_out[1]),
        "rest1": lambda: v.sum1.rest(),
        "rest2": lambda: v.sum2.rest(),
        "rest3": lambda: v.sum3.rest(),
        "rest4": lambda: v.sum4.rest(),
        "rest5": lambda: v.sum5.rest(),
        "rest6": lambda: v.sum6.rest(),
        "rest7": lambda: v.sum7.rest(),
    }
    for step in (
        (p1, p2, p3, p4, a0, ab, r, e, terms, start, ja, st, jt, sg, jg)
        + (lay1, lay2, qkv, kv, near1, fin1, join2, cq, cross, near2, fin2, join3, sm, jm, sc, jc)
        + (lay3, up, lay4, pre, near3, dterm, uterm, fin3, join4, mm4, cback, near4, qterm, kterm)
        + (mterm, fin4, join5, mm5, sback, near5, qkvterm, oterm, fin5, near6, fin6, near7, fin7)
    ):
        work[step.__name__] = step
    for name in PLAN:
        work[name]()
    return (
        v.block_out,
        v.image_grad,
        v.text_grad,
        v.mod_grad,
        v.qkv_grad,
        v.out_grad,
        v.query_grad,
        v.keyval_grad,
        v.merge_grad,
        v.gain_grad,
        v.up_grad,
        v.down_grad,
    )


def solution(mesh):
    placed = (
        P(("rep", "fsdp"), None, None),
        P(("rep", "fsdp"), None, None),
        P(("rep", "fsdp")),
        P(("rep", "fsdp")),
        P(("rep", "fsdp"), None, None),
        P("fsdp", None),
        P("fsdp", None),
        P("fsdp", None),
        P("fsdp", None),
        P("fsdp", None),
        P("fsdp", None),
        P("fsdp"),
        P("fsdp", None),
        P("fsdp", None),
    )
    return jax.shard_map(
        body,
        mesh=mesh,
        in_specs=placed,
        out_specs=(
            P(("rep", "fsdp"), None, None),
            P(("rep", "fsdp"), None, None),
            P(("rep", "fsdp"), None, None),
            P("fsdp", None),
            P("fsdp", None),
            P("fsdp", None),
            P("fsdp", None),
            P("fsdp", None),
            P("fsdp", None),
            P("fsdp"),
            P("fsdp", None),
            P("fsdp", None),
        ),
        check_vma=False,
    )
```
